32 devices in a mesh: tm: 4 (over x, core), space: 8 (over z, y).
Axes of the slice: x: 2, y: 2, z: 4, core: 2. Of those that a mesh axis runs over, the one named last changes fastest.
Arguments:
- enthalpy: float32 [4, 64, 512, 128], P('tm', 'space'), may hold values from -4 to 4
- solute: float32 [4, 64, 512, 128], P('tm', 'space'), may hold values from 0.5 to 1.5
- material: int32 [64, 512, 128], P('space'), may hold values from 0 to 3
- phase_flag: int32 [64, 512, 128], P('space'), may hold values from 0 to 2
- heat_capacity: float32 [4], replicated, may hold values from 0.8 to 2
- latent: float32 [4], replicated, may hold values from 0.5 to 2
- solidus: float32 [4], replicated, may hold values from -0.5 to 0.5
- partition: float32 [4], replicated, may hold values from 0.3 to 0.6
- back_diffusion: float32 [4], replicated, may hold values from 0.1 to 1
- heat_rate: float32 [4], replicated, may hold values from 0.06 to 0.16
- solute_rate: float32 [3], replicated, may hold values from 0.005 to 0.045
Outputs:
- end_enthalpy: float32 [4, 64, 512, 128], P('tm', 'space')
- end_solute: float32 [4, 64, 512, 128], P('tm', 'space')
The draws below stay inside these ranges and needn't reach their ends.
All inputs are finite; a program needn't handle non-finite values.
Results may differ from the reference program's by a relative error of at most 0.00002.
Values sent between devices are 32-bit elements; how exact they have to be, the bound alone decides.
No kernel may reach another device: no remote copies, remote signals or barrier semaphores. Data moves between devices by JAX's collectives and lax.ppermute only.
A program may use at most 128 MiB of HBM per device.

```python
import math
import jax
import jax.numpy as jnp

NY = 512
NZ = 128
STEPS = 4
NMAT = 4
PHASES = 3
SLICES = 4
NX = 64


def set_ends(entries, stream_key, least, high):
    longest = entries.shape.index(max(entries.shape))
    spots = []
    for shift in (0, 1):
        where = [jax.random.randint(jax.random.fold_in(stream_key, axis), (), 0, length) for axis, length in enumerate(entries.shape)]
        where[longest] = (where[longest] + shift) % entries.shape[longest]
        spots.append(tuple(where))
    return entries.at[spots[0]].set(least).at[spots[1]].set(high)


def level_of(own_key, dims, shards, low, top_value):
    loudness = 1.0
    for axis_at, parts in shards:
        steps = jax.random.uniform(jax.random.fold_in(jax.random.fold_in(own_key, 6), axis_at), (parts,), jnp.float32, low / len(shards), top_value / len(shards))
        loudness = loudness * jnp.repeat(jnp.exp(steps), dims[axis_at] // parts).reshape((-1,) + (1,) * (len(dims) - 1 - axis_at))
    return loudness


def bell_draw(own_key, dims, scale, bound, shards=(), kind=jnp.bfloat16):
    entries = jax.random.normal(own_key, dims, jnp.float32) * scale
    if len(shards) > 0:
        entries = level_of(own_key, dims, shards, -0.22, 0.18) * entries
    return jnp.clip(entries, min=-bound, max=bound).astype(kind)


def setup_inputs(seed: int = 0) -> dict:
    arg_keys = jax.random.split(jax.random.key(seed), 12)
    enthalpy = bell_draw(arg_keys[0], (SLICES, NX, NY, NZ), 1.0, 4.0, ((0, 4), (1, 8)), jnp.float32)
    solute = jnp.clip(0.5 + 1.0 * jax.random.uniform(arg_keys[1], (SLICES, NX, NY, NZ), jnp.float32) ** level_of(arg_keys[1], (SLICES, NX, NY, NZ), ((0, 4), (1, 8)), -0.2, 0.2), 0.5, 1.5)
    material = set_ends(jax.random.randint(arg_keys[2], (NX, NY, NZ), 0, NMAT), jax.random.fold_in(arg_keys[2], 1), 0, NMAT - 1).astype(jnp.int32)
    phase_flag = set_ends(jax.random.randint(arg_keys[3], (NX, NY, NZ), 0, PHASES), jax.random.fold_in(arg_keys[3], 1), 0, PHASES - 1).astype(jnp.int32)
    heat_capacity = jnp.clip(jnp.exp(jax.random.uniform(arg_keys[4], (NMAT,), jnp.float32, math.log(0.8), math.log(2.0))), 0.8, 2.0)
    latent = jnp.clip(jax.random.uniform(arg_keys[5], (NMAT,), jnp.float32, 0.5, 2.0), 0.5, 2.0)
    solidus = jnp.clip(jax.random.uniform(arg_keys[6], (NMAT,), jnp.float32, -0.5, 0.5), -0.5, 0.5)
    partition = jnp.clip(jax.random.uniform(arg_keys[7], (NMAT,), jnp.float32, 0.3, 0.6), 0.3, 0.6)
    back_diffusion = jnp.clip(jnp.exp(jax.random.uniform(arg_keys[8], (NMAT,), jnp.float32, math.log(0.1), math.log(1.0))), 0.1, 1.0)
    heat_rate = jnp.clip(jax.random.uniform(arg_keys[9], (NMAT,), jnp.float32, 0.06, 0.16), 0.06, 0.16)
    solute_rate = jnp.clip(jax.random.uniform(arg_keys[10], (PHASES,), jnp.float32, 0.005, 0.045), 0.005, 0.045)
    return {"enthalpy": enthalpy, "solute": solute, "material": material, "phase_flag": phase_flag, "heat_capacity": heat_capacity, "latent": latent, "solidus": solidus, "partition": partition, "back_diffusion": back_diffusion, "heat_rate": heat_rate, "solute_rate": solute_rate}


def lookup(region_ids, table_values):
    summed = jnp.zeros(region_ids.shape, jnp.float32)
    for member in range(table_values.shape[0]):
        summed = summed + jnp.where(region_ids == member, table_values[member], jnp.zeros((), jnp.float32))
    return summed


def coefficients(material, phase_flag, heat_capacity, latent, solidus, partition, back_diffusion, heat_rate, solute_rate):
    enthalpy_buffer_capacity = lookup(material, heat_capacity)
    melting_energy_map = lookup(material, latent)
    solidus_field = lookup(material, solidus)
    partition_field = lookup(material, partition)
    backflow = lookup(material, back_diffusion)
    thermal_ratio = lookup(material, heat_rate)
    heat_gain = thermal_ratio * enthalpy_buffer_capacity
    solute_gain = lookup(phase_flag, solute_rate)
    rate_pair = jnp.stack([heat_gain, solute_gain])
    coarse_rates = jnp.stack([4.0 * heat_gain / (1.0 + 18.0 * thermal_ratio),
                              4.0 * solute_gain / (1.0 + 18.0 * solute_gain / partition_field)])
    return (enthalpy_buffer_capacity, melting_energy_map, solidus_field, partition_field, backflow), rate_pair, coarse_rates


def fractions(gridded_quantities, coefs):
    enthalpy_buffer_capacity, melting_energy_map, solidus_field, partition_field, backflow = coefs
    molten_share = jnp.clip((gridded_quantities[0] - solidus_field) / melting_energy_map, 0.0, 1.0)
    local_warmth_value = (gridded_quantities[0] - melting_energy_map * molten_share) / enthalpy_buffer_capacity
    denominator_quantity = 1.0 - (1.0 - partition_field) * (1.0 - molten_share) / (1.0 + backflow)
    return jnp.stack([local_warmth_value, gridded_quantities[1] / denominator_quantity])


def laplace(padded):
    middle = padded[:, 1:-1]
    sides = jnp.pad(middle, ((0, 0), (0, 0), (1, 1), (1, 1)))
    return (padded[:, 2:] + padded[:, :-2] + sides[:, :, 2:, 1:-1] + sides[:, :, :-2, 1:-1]
            + sides[:, :, 1:-1, 2:] + sides[:, :, 1:-1, :-2] - 6.0 * middle)


def pad_rows(values):
    return jnp.pad(values, ((0, 0), (1, 1), (0, 0), (0, 0)))


def reference(enthalpy, solute, material, phase_flag, heat_capacity, latent, solidus, partition, back_diffusion, heat_rate, solute_rate):
    coefs, rate_pair, coarse_rates = coefficients(material, phase_flag, heat_capacity, latent, solidus,
                                                  partition, back_diffusion, heat_rate, solute_rate)
    outcome_list = []
    prior_iterate = None
    for member in range(SLICES):
        gridded_quantities = jnp.stack([enthalpy[member], solute[member]])
        initial = gridded_quantities
        first_laplacian = None
        for domain_portion in range(STEPS):
            laplacian = laplace(pad_rows(fractions(gridded_quantities, coefs)))
            if domain_portion == 0:
                first_laplacian = laplacian
            gridded_quantities = gridded_quantities + rate_pair * laplacian
        coarse = initial + coarse_rates * first_laplacian
        if member == 0:
            result = gridded_quantities
        else:
            predicted = prior_iterate + coarse_rates * laplace(pad_rows(fractions(prior_iterate, coefs)))
            result = predicted + (gridded_quantities - coarse)
        outcome_list.append(result)
        prior_iterate = result
    stacked = jnp.stack(outcome_list)
    return stacked[:, 0], stacked[:, 1]
```

```python
import functools

import jax
import jax.numpy as jnp
from jax import lax
from jax.experimental import pallas as pl
from jax.experimental.pallas import tpu as pltpu
from jax.sharding import PartitionSpec as P

STEPS = 4
CHUNK = 64
MIB = 1024 * 1024
SMEM = pl.BlockSpec(memory_space=pltpu.SMEM)
VMEM = pl.BlockSpec(memory_space=pltpu.VMEM)


class Tables:
    def __init__(self, prm):
        def raw(first, count):
            return [jnp.full((8, 128), prm[first + m], jnp.float32) for m in range(count)]

        cap, self.lat, self.hs = raw(0, 4), raw(4, 4), raw(8, 4)
        kp, bd, xr = raw(12, 4), raw(16, 4), raw(20, 4)
        self.sg = raw(24, 3)
        q = [(1.0 - k) / (1.0 + b) for k, b in zip(kp, bd)]
        self.icap = [1.0 / c for c in cap]
        self.den0 = [1.0 - v for v in q]
        self.den1 = [v / t for v, t in zip(q, self.lat)]
        self.hg = [x * c for x, c in zip(xr, cap)]
        self.gh = [4.0 / (1.0 + 18.0 * x) for x in xr]
        self.crh = [h * g for h, g in zip(self.hg, self.gh)]
        self.kp18 = [18.0 / k for k in kp]


class Cells:
    def __init__(self, tab, ids):
        self.tab, self.shape = tab, ids.shape
        self.b0 = (ids & 1) != 0
        self.b1 = (ids & 2) != 0
        self.p1 = (ids & 4) != 0
        self.p2 = (ids & 8) != 0

    def wide(self, tile):
        reps = self.shape[0] // 8
        return jnp.broadcast_to(tile[None], (reps, 8, 128)).reshape(self.shape)

    def alloy(self, name):
        t = [self.wide(v) for v in getattr(self.tab, name)]
        return jnp.where(self.b1, jnp.where(self.b0, t[3], t[2]), jnp.where(self.b0, t[1], t[0]))

    def solute_gain(self):
        t = [self.wide(v) for v in self.tab.sg]
        return jnp.where(self.p2, t[2], jnp.where(self.p1, t[1], t[0]))

    def fine(self):
        return self.alloy("hg"), self.solute_gain()

    def ratio(self):
        sg = self.solute_gain()
        return self.alloy("gh"), 4.0 / (1.0 + sg * self.alloy("kp18"))

    def coarse(self):
        sg = self.solute_gain()
        return self.alloy("crh"), 4.0 * sg / (1.0 + sg * self.alloy("kp18"))

    def melt(self, h, c):
        sensible = h - self.alloy("hs")
        held = jnp.minimum(jnp.maximum(sensible, 0.0), self.alloy("lat"))
        t = (h - held) * self.alloy("icap")
        return t, c / (self.alloy("den0") + self.alloy("den1") * held)


def chunks(ny, body):
    step = min(CHUNK, ny)

    def run(i, carry):
        body(pl.multiple_of(i * step, step), step)
        return carry

    lax.fori_loop(0, ny // step, run, 0)


def clear_rims(pad, ny):
    rows = pad.shape[1]
    for f in range(2):
        for r in range(rows):
            pad[f, r, 0:8, :] = jnp.zeros((8, 128), jnp.float32)
            pad[f, r, 8 + ny : 16 + ny, :] = jnp.zeros((8, 128), jnp.float32)


def put_melt(pad, r, y, n, cells, h, c):
    t, l = cells.melt(h, c)
    pad[0, r, pl.ds(y + 8, n), :] = t
    pad[1, r, pl.ds(y + 8, n), :] = l


def lap(pad, f, r, y, n, below, above):
    ext = pad[f, r, pl.ds(y, n + 16), :]
    mid = ext[8 : 8 + n]
    lane = lax.broadcasted_iota(jnp.int32, (n, 128), 1)
    total = pltpu.roll(ext, 1, 0)[8 : 8 + n] + pltpu.roll(ext, n + 15, 0)[8 : 8 + n]
    total = total + jnp.where(lane == 0, 0.0, pltpu.roll(mid, 1, 1))
    total = total + jnp.where(lane == 127, 0.0, pltpu.roll(mid, 127, 1))
    total = total - 6.0 * mid
    if below:
        total = total + pad[f, r - 1, pl.ds(y + 8, n), :]
    if above:
        total = total + pad[f, r + 1, pl.ds(y + 8, n), :]
    return total


def first_edges_kernel(prm, h, c, mat, ph, tl0, tl7):
    tab = Tables(prm)
    ny = h.shape[1]
    side = pl.program_id(0)

    def body(y, n):
        s = pl.ds(y, n)
        cells = Cells(tab, mat[0, s, :])
        t, l = cells.melt(h[0, s, :], c[0, s, :])

        @pl.when(side == 0)
        def _():
            tl0[0, s, :] = t
            tl0[1, s, :] = l

        @pl.when(side == 1)
        def _():
            tl7[0, s, :] = t
            tl7[1, s, :] = l

    chunks(ny, body)


def first_step_kernel(prm, h, c, mat, ph, hm, cm, part, idm, ide, pad):
    tab = Tables(prm)
    rows, ny = h.shape[0], h.shape[1]
    clear_rims(pad, ny)

    def melt_row(r):
        def body(y, n):
            s = pl.ds(y, n)
            ids = mat[r, s, :] + 4 * ph[r, s, :]
            put_melt(pad, r, y, n, Cells(tab, ids), h[r, s, :], c[r, s, :])
            if r == 0:
                ide[0, s, :] = ids
            elif r == rows - 1:
                ide[1, s, :] = ids
            else:
                idm[r - 1, s, :] = ids

        chunks(ny, body)

    def step_row(r):
        def body(y, n):
            s = pl.ds(y, n)
            ids = mat[r, s, :] + 4 * ph[r, s, :]
            rh, rc = Cells(tab, ids).fine()
            nh = h[r, s, :] + rh * lap(pad, 0, r, y, n, r > 0, r < rows - 1)
            nc = c[r, s, :] + rc * lap(pad, 1, r, y, n, r > 0, r < rows - 1)
            if 0 < r < rows - 1:
                hm[r - 1, s, :] = nh
                cm[r - 1, s, :] = nc
            else:
                part[min(r, 1), 0, s, :] = nh
                part[min(r, 1), 1, s, :] = nc

        chunks(ny, body)

    for r in range(rows):
        melt_row(r)
    for r in range(rows):
        step_row(r)


def step_kernel(prm, hm, cm, edge, idm, ide, nhm, ncm, part, pad):
    tab = Tables(prm)
    rows, ny = hm.shape[0] + 2, hm.shape[1]
    clear_rims(pad, ny)

    def load(r, s):
        if 0 < r < rows - 1:
            return hm[r - 1, s, :], cm[r - 1, s, :], idm[r - 1, s, :]
        e = min(r, 1)
        return edge[e, 0, s, :], edge[e, 1, s, :], ide[e, s, :]

    def melt_row(r):
        def body(y, n):
            h, c, ids = load(r, pl.ds(y, n))
            put_melt(pad, r, y, n, Cells(tab, ids), h, c)

        chunks(ny, body)

    def step_row(r):
        def body(y, n):
            s = pl.ds(y, n)
            h, c, ids = load(r, s)
            rh, rc = Cells(tab, ids).fine()
            nh = h + rh * lap(pad, 0, r, y, n, r > 0, r < rows - 1)
            nc = c + rc * lap(pad, 1, r, y, n, r > 0, r < rows - 1)
            if 0 < r < rows - 1:
                nhm[r - 1, s, :] = nh
                ncm[r - 1, s, :] = nc
            else:
                part[min(r, 1), 0, s, :] = nh
                part[min(r, 1), 1, s, :] = nc

        chunks(ny, body)

    for r in range(rows):
        melt_row(r)
    for r in range(rows):
        step_row(r)


def edges_kernel(prm, part, low, high, ide, edge, tl0, tl7):
    tab = Tables(prm)
    for e, (halo, tl) in enumerate(((low, tl0), (high, tl7))):

        def body(y, n):
            s = pl.ds(y, n)
            cells = Cells(tab, ide[e, s, :])
            rh, rc = cells.fine()
            h = part[e, 0, s, :] + rh * halo[0, s, :]
            c = part[e, 1, s, :] + rc * halo[1, s, :]
            edge[e, 0, s, :] = h
            edge[e, 1, s, :] = c
            t, l = cells.melt(h, c)
            tl[0, s, :] = t
            tl[1, s, :] = l

        chunks(part.shape[2], body)


def coarse_edges_kernel(own, prm, part, low, high, ide, old, edge, tl0, tl7):
    tab = Tables(prm)
    mine = own[0] != 0

    @pl.when(mine)
    def _():
        for e, (halo, tl) in enumerate(((low, tl0), (high, tl7))):

            def body(y, n):
                s = pl.ds(y, n)
                cells = Cells(tab, ide[e, s, :])
                rh, rc = cells.coarse()
                h = part[e, 0, s, :] + rh * halo[0, s, :]
                c = part[e, 1, s, :] + rc * halo[1, s, :]
                edge[e, 0, s, :] = h
                edge[e, 1, s, :] = c
                t, l = cells.melt(h, c)
                tl[0, s, :] = t
                tl[1, s, :] = l

            chunks(part.shape[2], body)

    @pl.when(jnp.logical_not(mine))
    def _():
        edge[...] = old[...]


def last_edges_kernel(own, prm, part, low, high, ide, old, oh, oc, nh, nc):
    tab = Tables(prm)
    mine = own[0] != 0
    side = pl.program_id(0)

    @pl.when(mine)
    def _():
        def body(y, n):
            s = pl.ds(y, n)
            cells = Cells(tab, ide[0, s, :])
            rh, rc = cells.coarse()
            ht = jnp.where(side == 0, low[0, s, :], high[0, s, :])
            hl = jnp.where(side == 0, low[1, s, :], high[1, s, :])
            nh[0, 0, s, :] = part[0, 0, s, :] + rh * ht
            nc[0, 0, s, :] = part[0, 1, s, :] + rc * hl

        chunks(part.shape[2], body)

    @pl.when(jnp.logical_not(mine))
    def _():
        nh[0, 0] = old[0, 0]
        nc[0, 0] = old[0, 1]


def drift_kernel(prm, h4, c4, h0, c0, h1, c1, ids, dh, dc):
    tab = Tables(prm)

    def body(y, n):
        s = pl.ds(y, n)
        gh, gc = Cells(tab, ids[0, s, :]).ratio()
        u, v = h0[0, s, :], c0[0, s, :]
        dh[0, s, :] = h4[0, s, :] - u - gh * (h1[0, s, :] - u)
        dc[0, s, :] = c4[0, s, :] - v - gc * (c1[0, s, :] - v)

    chunks(h4.shape[1], body)


def drift_edges_kernel(prm, e4, h0, c0, e1, ids, de):
    tab = Tables(prm)

    def body(y, n):
        s = pl.ds(y, n)
        gh, gc = Cells(tab, ids[0, s, :]).ratio()
        u, v = h0[0, s, :], c0[0, s, :]
        de[0, 0, s, :] = e4[0, 0, s, :] - u - gh * (e1[0, 0, s, :] - u)
        de[0, 1, s, :] = e4[0, 1, s, :] - v - gc * (e1[0, 1, s, :] - v)

    chunks(e4.shape[2], body)


def coarse_mid_kernel(own, prm, vm, vn, dhm, dcm, idm, old, new, pad):
    tab = Tables(prm)
    mine = own[0] != 0
    mid, ny = vm.shape[1], vm.shape[2]

    @pl.when(mine)
    def _():
        clear_rims(pad, ny)

        def load(r, s):
            if 0 < r < mid + 1:
                return vm[0, r - 1, s, :], vm[1, r - 1, s, :]
            return vn[0, min(r, 1), s, :], vn[1, min(r, 1), s, :]

        for r in range(mid + 2):

            def body(y, n):
                s = pl.ds(y, n)
                h, c = load(r, s)
                put_melt(pad, r, y, n, Cells(tab, idm[r, s, :]), h, c)

            chunks(ny, body)
        for r in range(1, mid + 1):

            def body2(y, n):
                s = pl.ds(y, n)
                h, c = load(r, s)
                rh, rc = Cells(tab, idm[r, s, :]).coarse()
                new[0, r - 1, s, :] = h + dhm[r, s, :] + rh * lap(pad, 0, r, y, n, True, True)
                new[1, r - 1, s, :] = c + dcm[r, s, :] + rc * lap(pad, 1, r, y, n, True, True)

            chunks(ny, body2)

    @pl.when(jnp.logical_not(mine))
    def _():
        new[...] = old[...]


def coarse_rim_kernel(own, prm, vo, vn, vm, dhm, dcm, de, idm, ide, old, new, part, pad):
    tab = Tables(prm)
    mine = own[0] != 0
    mid, ny = vm.shape[1], vm.shape[2]

    @pl.when(mine)
    def _():
        clear_rims(pad, ny)
        for e in range(2):
            near, far = (0, mid - 1)[e], (1, mid)[e]

            def load(k, s):
                if k == 0:
                    return vo[e, 0, s, :], vo[e, 1, s, :], ide[e, s, :]
                if k == 1:
                    return vn[0, e, s, :], vn[1, e, s, :], idm[e * (mid + 1), s, :]
                row = e * (mid - 1)
                return vm[0, row, s, :], vm[1, row, s, :], idm[row + 1, s, :]

            for k in range(3):

                def body(y, n):
                    h, c, ids = load(k, pl.ds(y, n))
                    put_melt(pad, 3 * e + k, y, n, Cells(tab, ids), h, c)

                chunks(ny, body)
            for k in range(2):

                def body2(y, n):
                    s = pl.ds(y, n)
                    h, c, ids = load(k, s)
                    rh, rc = Cells(tab, ids).coarse()
                    h = h + rh * lap(pad, 0, 3 * e + k, y, n, k > 0, True)
                    c = c + rc * lap(pad, 1, 3 * e + k, y, n, k > 0, True)
                    if k == 0:
                        part[e, 0, s, :] = h + de[e, 0, s, :]
                        part[e, 1, s, :] = c + de[e, 1, s, :]
                    else:
                        new[0, e, s, :] = h + dhm[e * (mid + 1), s, :]
                        new[1, e, s, :] = c + dcm[e * (mid + 1), s, :]

                chunks(ny, body2)

    @pl.when(jnp.logical_not(mine))
    def _():
        new[...] = old[...]


def spread_kernel(vm, vn, oh, oc):
    mid = vm.shape[1]
    for f, out in enumerate((oh, oc)):
        out[0, 1] = vn[f, 0]
        out[0, mid + 2] = vn[f, 1]
        for r in range(mid):
            out[0, 2 + r] = vm[f, r]


def f32(*shape):
    return jax.ShapeDtypeStruct(shape, jnp.float32)


def i32(*shape):
    return jax.ShapeDtypeStruct(shape, jnp.int32)


def call(kernel, outs, args, smem, cells, scratch=(), limit=32, name=None):
    nbytes = 4 * sum(a.size for a in args) + 4 * sum(o.size for o in outs)
    return pl.pallas_call(
        kernel,
        out_shape=outs,
        in_specs=[SMEM] * smem + [VMEM] * (len(args) - smem),
        out_specs=[VMEM] * len(outs),
        scratch_shapes=scratch,
        compiler_params=pltpu.CompilerParams(vmem_limit_bytes=limit * MIB),
        cost_estimate=pl.CostEstimate(flops=100 * cells, bytes_accessed=nbytes, transcendentals=0),
        name=name,
    )(*args)


def per_device(slices, parts, enthalpy, solute, material, phase_flag, *params):
    rows, ny, nz = material.shape
    mid = rows - 4
    row = ny * nz
    h0 = enthalpy.reshape(rows, ny, nz)
    c0 = solute.reshape(rows, ny, nz)
    prm = jnp.concatenate(params)
    slot = lax.axis_index("tm")

    def pad(n):
        return [pltpu.VMEM((2, n, ny + 16, nz), jnp.float32)]

    def move(x, tms, up, by):
        pairs = [
            (t * parts + s, (t + up) * parts + s + by)
            for t in tms
            for s in range(parts)
            if 0 <= s + by < parts
        ]
        return lax.ppermute(x, ("tm", "space"), pairs)

    def halos(tl0, tl7, tms, up):
        return move(tl7, tms, up, 1), move(tl0, tms, up, -1)

    edge_rows = pl.BlockSpec((1, ny, nz), lambda i: ((rows - 1) * i, 0, 0))
    whole = pl.BlockSpec((2, ny, nz), lambda i: (0, 0, 0))
    tl0, tl7 = pl.pallas_call(
        first_edges_kernel,
        grid=(2,),
        out_shape=[f32(2, ny, nz)] * 2,
        in_specs=[SMEM] + [edge_rows] * 4,
        out_specs=[whole] * 2,
        compiler_params=pltpu.CompilerParams(vmem_limit_bytes=16 * MIB),
        name="first_edges",
    )(prm, h0, c0, material, phase_flag)

    every = range(slices)
    low, high = halos(tl0, tl7, every, 0)
    hm, cm, part, idm, ide = call(
        first_step_kernel,
        [f32(rows - 2, ny, nz)] * 2 + [f32(2, 2, ny, nz), i32(rows - 2, ny, nz), i32(2, ny, nz)],
        (prm, h0, c0, material, phase_flag),
        1,
        rows * row,
        pad(rows),
        40,
        "first_step",
    )
    h1, c1 = hm, cm
    e1 = None
    for k in range(STEPS):
        edge, tl0, tl7 = call(
            edges_kernel,
            [f32(2, 2, ny, nz)] + [f32(2, ny, nz)] * 2,
            (prm, part, low, high, ide),
            1,
            2 * row,
            limit=16,
            name="edges",
        )
        if k == 0:
            e1 = edge
        if k < STEPS - 1:
            low, high = halos(tl0, tl7, every, 0)
            hm, cm, part = call(
                step_kernel,
                [f32(rows - 2, ny, nz)] * 2 + [f32(2, 2, ny, nz)],
                (prm, hm, cm, edge, idm, ide),
                1,
                rows * row,
                pad(rows),
                40,
                "step",
            )

    one = pl.BlockSpec((1, ny, nz), lambda i: (i, 0, 0))
    inner = pl.BlockSpec((1, ny, nz), lambda i: (i + 1, 0, 0))
    dhm, dcm = pl.pallas_call(
        drift_kernel,
        grid=(rows - 2,),
        out_shape=[f32(rows - 2, ny, nz)] * 2,
        in_specs=[SMEM, one, one, inner, inner, one, one, one],
        out_specs=[one] * 2,
        compiler_params=pltpu.CompilerParams(vmem_limit_bytes=16 * MIB),
        name="drift",
    )(prm, hm, cm, h0, c0, h1, c1, idm)
    pair = pl.BlockSpec((1, 2, ny, nz), lambda i: (i, 0, 0, 0))
    de = pl.pallas_call(
        drift_edges_kernel,
        grid=(2,),
        out_shape=f32(2, 2, ny, nz),
        in_specs=[SMEM, pair, edge_rows, edge_rows, pair, one],
        out_specs=pair,
        compiler_params=pltpu.CompilerParams(vmem_limit_bytes=16 * MIB),
        name="drift_edges",
    )(prm, edge, h0, c0, e1, ide)

    vm = jnp.stack([hm[1:-1], cm[1:-1]])
    vn = jnp.stack([jnp.stack([x[0], x[-1]]) for x in (hm, cm)])
    vo = edge
    for n in range(1, slices):
        own = (slot == n).astype(jnp.int32).reshape(1)
        am = move(vm, (n - 1,), 1, 0)
        an = move(vn, (n - 1,), 1, 0)
        ao = move(vo, (n - 1,), 1, 0)
        low, high = halos(tl0, tl7, (n - 1,), 1)
        vm = call(
            coarse_mid_kernel,
            [f32(2, mid, ny, nz)],
            (own, prm, am, an, dhm, dcm, idm, vm),
            2,
            (rows - 2) * row,
            pad(mid + 2),
            40,
            "coarse_mid",
        )[0]
        vn, part = call(
            coarse_rim_kernel,
            [f32(2, 2, ny, nz)] * 2,
            (own, prm, ao, an, am, dhm, dcm, de, idm, ide, vn),
            2,
            6 * row,
            pad(6),
            40,
            "coarse_rim",
        )
        if n < slices - 1:
            vo, tl0, tl7 = call(
                coarse_edges_kernel,
                [f32(2, 2, ny, nz)] + [f32(2, ny, nz)] * 2,
                (own, prm, part, low, high, ide, vo),
                2,
                2 * row,
                limit=16,
                name="coarse_edges",
            )

    oh, oc = call(spread_kernel, [f32(1, rows, ny, nz)] * 2, (vm, vn), 0, rows * row, limit=20, name="spread")
    out_edge = pl.BlockSpec((1, 1, ny, nz), lambda i: (0, (rows - 1) * i, 0, 0))
    anyspec = pl.BlockSpec(memory_space=pl.ANY)
    return tuple(
        pl.pallas_call(
            last_edges_kernel,
            grid=(2,),
            out_shape=[f32(1, rows, ny, nz)] * 2,
            in_specs=[SMEM, SMEM, pair, whole, whole, one, pair, anyspec, anyspec],
            out_specs=[out_edge] * 2,
            input_output_aliases={7: 0, 8: 1},
            compiler_params=pltpu.CompilerParams(vmem_limit_bytes=16 * MIB),
            name="last_edges",
        )(own, prm, part, low, high, ide, vo, oh, oc)
    )


def solution(mesh):
    body = functools.partial(per_device, mesh.shape["tm"], mesh.shape["space"])
    return jax.shard_map(
        body,
        mesh=mesh,
        in_specs=(
            P("tm", "space", None, None),
            P("tm", "space", None, None),
            P("space", None, None),
            P("space", None, None),
        )
        + (P(),) * 7,
        out_specs=(P("tm", "space", None, None), P("tm", "space", None, None)),
        check_vma=False,
    )
```

```python
import functools

import jax
import jax.numpy as jnp
from jax import lax
from jax.experimental import pallas as pl
from jax.experimental.pallas import tpu as pltpu
from jax.sharding import PartitionSpec as P

STEPS = 4
MIB = 1024 * 1024
SMEM = pl.BlockSpec(memory_space=pltpu.SMEM)
VMEM = pl.BlockSpec(memory_space=pltpu.VMEM)
ANY = pl.BlockSpec(memory_space=pl.ANY)


class Tables:
    def __init__(self, prm):
        def raw(first, count):
            return [jnp.full((8, 128), prm[first + m], jnp.float32) for m in range(count)]

        cap, self.lat, self.hs = raw(0, 4), raw(4, 4), raw(8, 4)
        kp, bd, xr = raw(12, 4), raw(16, 4), raw(20, 4)
        self.sg = raw(24, 3)
        q = [(1.0 - k) / (1.0 + b) for k, b in zip(kp, bd)]
        self.icap = [1.0 / c for c in cap]
        self.den0 = [1.0 - v for v in q]
        self.den1 = [v / t for v, t in zip(q, self.lat)]
        self.hg = [x * c for x, c in zip(xr, cap)]
        self.gh = [4.0 / (1.0 + 18.0 * x) for x in xr]
        self.crh = [h * g for h, g in zip(self.hg, self.gh)]
        self.kp18 = [18.0 / k for k in kp]


class Cells:
    def __init__(self, tab, ids):
        self.tab, self.shape = tab, ids.shape
        self.b0 = (ids & 1) != 0
        self.b1 = (ids & 2) != 0
        self.p1 = (ids & 4) != 0
        self.p2 = (ids & 8) != 0

    def wide(self, tile):
        reps = self.shape[0] // 8
        return jnp.broadcast_to(tile[None], (reps, 8, 128)).reshape(self.shape)

    def alloy(self, name):
        t = [self.wide(v) for v in getattr(self.tab, name)]
        return jnp.where(self.b1, jnp.where(self.b0, t[3], t[2]), jnp.where(self.b0, t[1], t[0]))

    def solute_gain(self):
        t = [self.wide(v) for v in self.tab.sg]
        return jnp.where(self.p2, t[2], jnp.where(self.p1, t[1], t[0]))

    def fine(self):
        return self.alloy("hg"), self.solute_gain()

    def ratio(self):
        sg = self.solute_gain()
        return self.alloy("gh"), 4.0 / (1.0 + sg * self.alloy("kp18"))

    def coarse(self):
        sg = self.solute_gain()
        return self.alloy("crh"), 4.0 * sg / (1.0 + sg * self.alloy("kp18"))

    def melt(self, h, c):
        sensible = h - self.alloy("hs")
        held = jnp.minimum(jnp.maximum(sensible, 0.0), self.alloy("lat"))
        t = (h - held) * self.alloy("icap")
        return t, c / (self.alloy("den0") + self.alloy("den1") * held)


F2 = range(2)


def clear_rims(pad, ny):
    for f in F2:
        for r in range(pad.shape[1]):
            pad[f, r, 0:8, :] = jnp.zeros((8, 128), jnp.float32)
            pad[f, r, 8 + ny : 16 + ny, :] = jnp.zeros((8, 128), jnp.float32)


def put_melt(tab, pad, r, ids, h, c):
    ny = ids.shape[0]
    t, l = Cells(tab, ids).melt(h, c)
    pad[0, r, 8 : 8 + ny, :] = t
    pad[1, r, 8 : 8 + ny, :] = l


def lap(pad, f, r, below, above):
    ny = pad.shape[2] - 16
    mid = pad[f, r, 8 : 8 + ny, :]
    lane = lax.broadcasted_iota(jnp.int32, mid.shape, 1)
    total = pad[f, r, 7 : 7 + ny, :] + pad[f, r, 9 : 9 + ny, :]
    total = total + jnp.where(lane == 0, 0.0, pltpu.roll(mid, 1, 1))
    total = total + jnp.where(lane == 127, 0.0, pltpu.roll(mid, 127, 1))
    total = total - 6.0 * mid
    if below:
        total = total + pad[f, r - 1, 8 : 8 + ny, :]
    if above:
        total = total + pad[f, r + 1, 8 : 8 + ny, :]
    return total


def each(first, count, body):
    def run(i, carry):
        body(first + i)
        return carry

    lax.fori_loop(0, count, run, 0)


def first_edges_kernel(prm, h, c, mat, tl0, tl7):
    tab = Tables(prm)
    t, l = Cells(tab, mat[0]).melt(h[0], c[0])
    side = pl.program_id(0)

    @pl.when(side == 0)
    def _():
        tl0[0] = t
        tl0[1] = l

    @pl.when(side == 1)
    def _():
        tl7[0] = t
        tl7[1] = l


def fine_update(tab, pad, r, ids, h, c, below, above):
    rh, rc = Cells(tab, ids).fine()
    return h + rh * lap(pad, 0, r, below, above), c + rc * lap(pad, 1, r, below, above)


def first_step_kernel(prm, h, c, mat, ph, sm, sn, part, idi, ide, pad):
    tab = Tables(prm)
    rows, ny = h.shape[0], h.shape[1]
    clear_rims(pad, ny)

    def melt(r):
        ids = mat[r] + 4 * ph[r]
        put_melt(tab, pad, r, ids, h[r], c[r])
        return ids

    def melt_inner(r):
        idi[r - 1] = melt(r)

    ide[0] = melt(0)
    ide[1] = melt(rows - 1)
    each(1, rows - 2, melt_inner)

    def update(r, below=True, above=True):
        return fine_update(tab, pad, r, mat[r] + 4 * ph[r], h[r], c[r], below, above)

    def update_mid(r):
        sm[0, r - 2], sm[1, r - 2] = update(r)

    for e, r in enumerate((0, rows - 1)):
        part[0, e], part[1, e] = update(r, r > 0, r == 0)
    for e, r in enumerate((1, rows - 2)):
        sn[0, e], sn[1, e] = update(r)
    each(2, rows - 4, update_mid)


def step_kernel(prm, sm, sn, sx, idi, ide, nm, nn, part, pad):
    tab = Tables(prm)
    rows, ny = sm.shape[1] + 4, sm.shape[2]
    ends, nexts = (0, rows - 1), (1, rows - 2)
    clear_rims(pad, ny)
    for e in range(2):
        put_melt(tab, pad, ends[e], ide[e], sx[0, e], sx[1, e])
        put_melt(tab, pad, nexts[e], idi[nexts[e] - 1], sn[0, e], sn[1, e])

    def melt_mid(r):
        put_melt(tab, pad, r, idi[r - 1], sm[0, r - 2], sm[1, r - 2])

    each(2, rows - 4, melt_mid)
    for e in range(2):
        part[0, e], part[1, e] = fine_update(
            tab, pad, ends[e], ide[e], sx[0, e], sx[1, e], e == 1, e == 0
        )
        nn[0, e], nn[1, e] = fine_update(
            tab, pad, nexts[e], idi[nexts[e] - 1], sn[0, e], sn[1, e], True, True
        )

    def update_mid(r):
        nm[0, r - 2], nm[1, r - 2] = fine_update(
            tab, pad, r, idi[r - 1], sm[0, r - 2], sm[1, r - 2], True, True
        )

    each(2, rows - 4, update_mid)


def edges_kernel(prm, part, low, high, ide, edge, tl0, tl7):
    tab = Tables(prm)
    for e, (halo, tl) in enumerate(((low, tl0), (high, tl7))):
        cells = Cells(tab, ide[e])
        rh, rc = cells.fine()
        h = part[0, e] + rh * halo[0]
        c = part[1, e] + rc * halo[1]
        edge[0, e], edge[1, e] = h, c
        tl[0], tl[1] = cells.melt(h, c)


def drift_kernel(prm, s4, h0, c0, s1, ids, d):
    gh, gc = Cells(Tables(prm), ids[0]).ratio()
    u, v = h0[0], c0[0]
    d[0, 0] = s4[0, 0] - u - gh * (s1[0, 0] - u)
    d[1, 0] = s4[1, 0] - v - gc * (s1[1, 0] - v)


def coarse_update(tab, pad, r, ids, h, c, below, above):
    rh, rc = Cells(tab, ids).coarse()
    return h + rh * lap(pad, 0, r, below, above), c + rc * lap(pad, 1, r, below, above)


def coarse_mid_kernel(own, prm, vm, vn, dm, idi, old, new, pad):
    tab = Tables(prm)
    mid, ny = vm.shape[1], vm.shape[2]

    @pl.when(own[0] != 0)
    def _():
        clear_rims(pad, ny)
        for e in range(2):
            r = (mid + 1) * e
            put_melt(tab, pad, r, idi[r], vn[0, e], vn[1, e])

        def melt_mid(r):
            put_melt(tab, pad, r, idi[r], vm[0, r - 1], vm[1, r - 1])

        def update_mid(r):
            h, c = coarse_update(tab, pad, r, idi[r], vm[0, r - 1], vm[1, r - 1], True, True)
            new[0, r - 1] = h + dm[0, r - 1]
            new[1, r - 1] = c + dm[1, r - 1]

        each(1, mid, melt_mid)
        each(1, mid, update_mid)

    @pl.when(own[0] == 0)
    def _():
        new[...] = old[...]


def rim_rows(tab, pad, e, vx, vn, near, dn, dx, idx, idn, idm):
    at = 3 * e
    put_melt(tab, pad, at, idx, *vx)
    put_melt(tab, pad, at + 1, idn, *vn)
    put_melt(tab, pad, at + 2, idm, *near)
    h, c = coarse_update(tab, pad, at, idx, *vx, False, True)
    g, b = coarse_update(tab, pad, at + 1, idn, *vn, True, True)
    return (h + dx[0], c + dx[1]), (g + dn[0], b + dn[1])


def coarse_rim_kernel(own, prm, vx, vn, vm, dn, dx, idi, ide, old, new, part, pad):
    tab = Tables(prm)
    mid, ny = vm.shape[1], vm.shape[2]

    @pl.when(own[0] != 0)
    def _():
        clear_rims(pad, ny)
        for e in range(2):
            near = (mid - 1) * e
            (part[0, e], part[1, e]), (new[0, e], new[1, e]) = rim_rows(
                tab,
                pad,
                e,
                [vx[f, e] for f in F2],
                [vn[f, e] for f in F2],
                [vm[f, near] for f in F2],
                [dn[f, e] for f in F2],
                [dx[f, e] for f in F2],
                ide[e],
                idi[(mid + 1) * e],
                idi[near + 1],
            )

    @pl.when(own[0] == 0)
    def _():
        new[...] = old[...]


def coarse_edges_kernel(own, prm, part, low, high, ide, old, edge, tl0, tl7):
    tab = Tables(prm)

    @pl.when(own[0] != 0)
    def _():
        for e, (halo, tl) in enumerate(((low, tl0), (high, tl7))):
            cells = Cells(tab, ide[e])
            rh, rc = cells.coarse()
            h = part[0, e] + rh * halo[0]
            c = part[1, e] + rc * halo[1]
            edge[0, e], edge[1, e] = h, c
            tl[0], tl[1] = cells.melt(h, c)

    @pl.when(own[0] == 0)
    def _():
        edge[...] = old[...]


def last_rows_kernel(own, prm, vm, vn, vx, dm, dn, dx, idi, ide, om, on, ox, oh, oc, pad):
    tab = Tables(prm)
    mid, ny = vm.shape[1], vm.shape[2]
    rows = mid + 4
    out = (oh, oc)
    ends, nexts = (0, rows - 1), (1, rows - 2)

    @pl.when(own[0] != 0)
    def _():
        clear_rims(pad, ny)
        for e in range(2):
            put_melt(tab, pad, ends[e], ide[e], vx[0, e], vx[1, e])
            put_melt(tab, pad, nexts[e], idi[nexts[e] - 1], vn[0, e], vn[1, e])

        def melt_mid(r):
            put_melt(tab, pad, r, idi[r - 1], vm[0, r - 2], vm[1, r - 2])

        each(2, mid, melt_mid)
        for e in range(2):
            new = coarse_update(tab, pad, ends[e], ide[e], vx[0, e], vx[1, e], e == 1, e == 0)
            for f in F2:
                out[f][0, ends[e]] = new[f] + dx[f, e]
            new = coarse_update(
                tab, pad, nexts[e], idi[nexts[e] - 1], vn[0, e], vn[1, e], True, True
            )
            for f in F2:
                out[f][0, nexts[e]] = new[f] + dn[f, e]

        def update_mid(r):
            new = coarse_update(tab, pad, r, idi[r - 1], vm[0, r - 2], vm[1, r - 2], True, True)
            for f in F2:
                out[f][0, r] = new[f] + dm[f, r - 2]

        each(2, mid, update_mid)

    @pl.when(own[0] == 0)
    def _():
        for f in F2:
            for e in range(2):
                out[f][0, ends[e]] = ox[f, e]
                out[f][0, nexts[e]] = on[f, e]
            for r in range(mid):
                out[f][0, r + 2] = om[f, r]


def last_edges_kernel(own, prm, low, high, ide, oh, oc, nh, nc):
    side = pl.program_id(0)

    @pl.when(own[0] != 0)
    def _():
        rh, rc = Cells(Tables(prm), ide[0]).coarse()
        first = side == 0
        nh[0, 0] = oh[0, 0] + rh * jnp.where(first, low[0], high[0])
        nc[0, 0] = oc[0, 0] + rc * jnp.where(first, low[1], high[1])

    @pl.when(own[0] == 0)
    def _():
        nh[...] = oh[...]
        nc[...] = oc[...]


def f32(*shape):
    return jax.ShapeDtypeStruct(shape, jnp.float32)


def i32(*shape):
    return jax.ShapeDtypeStruct(shape, jnp.int32)


TINY = pl.CostEstimate(flops=1000, bytes_accessed=1000, transcendentals=0)


def call(kernel, outs, args, smem, name, scratch=(), limit=16, after=()):
    if after:
        inner, count = kernel, len(args)

        def kernel(*refs):
            inner(*refs[:count], *refs[count + len(after) :])

    return pl.pallas_call(
        kernel,
        out_shape=outs,
        in_specs=[SMEM] * smem + [VMEM] * (len(args) - smem) + [ANY] * len(after),
        out_specs=[VMEM] * len(outs),
        scratch_shapes=scratch,
        compiler_params=pltpu.CompilerParams(vmem_limit_bytes=limit * MIB),
        cost_estimate=TINY,
        name=name,
    )(*args, *after)


def per_device(slices, parts, enthalpy, solute, material, phase_flag, *params):
    rows, ny, nz = material.shape
    mid = rows - 4
    h0 = enthalpy.reshape(rows, ny, nz)
    c0 = solute.reshape(rows, ny, nz)
    prm = jnp.concatenate(params)
    slot = lax.axis_index("tm")
    pair, tall = f32(2, 2, ny, nz), f32(2, mid, ny, nz)
    halo = f32(2, ny, nz)

    def pad(n):
        return [pltpu.VMEM((2, n, ny + 16, nz), jnp.float32)]

    def move(x, tms, up, by):
        pairs = [
            (t * parts + s, (t + up) * parts + s + by)
            for t in tms
            for s in range(parts)
            if 0 <= s + by < parts
        ]
        return lax.ppermute(x, ("tm", "space"), pairs)

    def halos(tl0, tl7, tms, up):
        return move(tl7, tms, up, 1), move(tl0, tms, up, -1)

    def gridded(kernel, steps, outs, out_specs, in_specs, args, name, aliases={}):
        return pl.pallas_call(
            kernel,
            grid=(steps,),
            out_shape=outs,
            in_specs=in_specs,
            out_specs=out_specs,
            input_output_aliases=aliases,
            compiler_params=pltpu.CompilerParams(vmem_limit_bytes=16 * MIB),
            cost_estimate=TINY,
            name=name,
        )(*args)

    edge_row = pl.BlockSpec((1, ny, nz), lambda i: ((rows - 1) * i, 0, 0))
    whole = pl.BlockSpec((2, ny, nz), lambda i: (0, 0, 0))
    far = [pltpu.with_memory_space_constraint(x, pltpu.HBM) for x in (h0, c0, material)]
    tl0, tl7 = gridded(
        first_edges_kernel, 2, [halo] * 2, [whole] * 2, [SMEM] + [edge_row] * 3, (prm, *far), "first_edges"
    )
    every = range(slices)
    low, high = halos(tl0, tl7, every, 0)
    sm, sn, part, idi, ide = call(
        first_step_kernel,
        [tall, pair, pair, i32(rows - 2, ny, nz), i32(2, ny, nz)],
        (prm, h0, c0, material, phase_flag),
        1,
        "first_step",
        pad(rows),
        40,
    )
    m1, n1 = sm, sn

    def fine_edges(part, low, high, after=()):
        return call(
            edges_kernel, [pair, halo, halo], (prm, part, low, high, ide), 1, "edges", after=after
        )

    def drift(count, first, stride, s4, s1, ids, id_at, id_by, name):
        row = pl.BlockSpec((2, 1, ny, nz), lambda i: (0, i, 0, 0))
        cell = pl.BlockSpec((1, ny, nz), lambda i: (first + stride * i, 0, 0))
        ident = pl.BlockSpec((1, ny, nz), lambda i: (id_at + id_by * i, 0, 0))
        return gridded(
            drift_kernel,
            count,
            f32(2, count, ny, nz),
            row,
            [SMEM, row, cell, cell, row, ident],
            (prm, s4, h0, c0, s1, ids),
            name,
        )

    def own(n):
        return (slot == n).astype(jnp.int32).reshape(1)

    def send(x, n):
        return move(x, (n - 1,), 1, 0)

    def coarse_mid(n, am, an, old):
        return call(
            coarse_mid_kernel,
            [tall],
            (own(n), prm, am, an, dm, idi, old),
            2,
            "coarse_mid",
            pad(mid + 2),
            40,
        )[0]

    x1 = None
    for k in range(STEPS - 1):
        sx, tl0, tl7 = fine_edges(part, low, high)
        if k == 0:
            x1 = sx
        low, high = halos(tl0, tl7, every, 0)
        sm, sn, part = call(
            step_kernel,
            [tall, pair, pair],
            (prm, sm, sn, sx, idi, ide),
            1,
            "step",
            pad(rows),
            40,
        )

    vm, vn = sm, sn
    dm = drift(mid, 2, 1, sm, m1, idi, 1, 1, "drift_m")
    dn = drift(2, 1, rows - 3, sn, n1, idi, 0, rows - 3, "drift_n")
    am, an = send(vm, 1), send(vn, 1)
    vm = coarse_mid(1, am, an, vm)
    vx, tl0, tl7 = fine_edges(part, low, high, (vm, dn))
    dx = drift(2, 0, rows - 1, vx, x1, ide, 0, 1, "drift_x")
    for n in range(1, slices):
        if n > 1:
            am, an = send(vm, n), send(vn, n)
        ax = send(vx, n)
        low, high = halos(tl0, tl7, (n - 1,), 1)
        if n < slices - 1:
            if n > 1:
                vm = coarse_mid(n, am, an, vm)
            vn, part = call(
                coarse_rim_kernel,
                [pair, pair],
                (own(n), prm, ax, an, am, dn, dx, idi, ide, vn),
                2,
                "coarse_rim",
                pad(6),
                40,
            )
            vx, tl0, tl7 = call(
                coarse_edges_kernel,
                [pair, halo, halo],
                (own(n), prm, part, low, high, ide, vx),
                2,
                "coarse_edges",
            )
    own = own(slices - 1)

    out = f32(1, rows, ny, nz)
    oh, oc = call(
        last_rows_kernel,
        [out, out],
        (own, prm, am, an, ax, dm, dn, dx, idi, ide, vm, vn, vx),
        2,
        "last_rows",
        pad(rows),
        48,
    )
    out_row = pl.BlockSpec((1, 1, ny, nz), lambda i: (0, (rows - 1) * i, 0, 0))
    one = pl.BlockSpec((1, ny, nz), lambda i: (i, 0, 0))
    return tuple(
        gridded(
            last_edges_kernel,
            2,
            [out, out],
            [out_row] * 2,
            [SMEM, SMEM, whole, whole, one, out_row, out_row],
            (own, prm, low, high, ide, oh, oc),
            "last_edges",
            {5: 0, 6: 1},
        )
    )


def solution(mesh):
    body = functools.partial(per_device, mesh.shape["tm"], mesh.shape["space"])
    return jax.shard_map(
        body,
        mesh=mesh,
        in_specs=(
            P("tm", "space", None, None),
            P("tm", "space", None, None),
            P("space", None, None),
            P("space", None, None),
        )
        + (P(),) * 7,
        out_specs=(P("tm", "space", None, None), P("tm", "space", None, None)),
        check_vma=False,
    )
```

```python
import functools

import jax
import jax.numpy as jnp
from jax import lax
from jax.experimental import pallas as pl
from jax.experimental.pallas import tpu as pltpu
from jax.sharding import PartitionSpec as P

STEPS = 4
CHUNK = 256
MIB = 1024 * 1024
SMEM = pl.BlockSpec(memory_space=pltpu.SMEM)
VMEM = pl.BlockSpec(memory_space=pltpu.VMEM)
ANY = pl.BlockSpec(memory_space=pl.ANY)


class Tables:
    def __init__(self, prm):
        def raw(first, count):
            return [jnp.full((8, 128), prm[first + m], jnp.float32) for m in range(count)]

        cap, self.lat, self.hs = raw(0, 4), raw(4, 4), raw(8, 4)
        kp, bd, xr = raw(12, 4), raw(16, 4), raw(20, 4)
        self.sg = raw(24, 3)
        q = [(1.0 - k) / (1.0 + b) for k, b in zip(kp, bd)]
        self.icap = [1.0 / c for c in cap]
        self.den0 = [1.0 - v for v in q]
        self.den1 = [v / t for v, t in zip(q, self.lat)]
        self.hg = [x * c for x, c in zip(xr, cap)]
        self.gh = [4.0 / (1.0 + 18.0 * x) for x in xr]
        self.crh = [h * g for h, g in zip(self.hg, self.gh)]
        self.kp18 = [18.0 / k for k in kp]


class Cells:
    def __init__(self, tab, ids):
        self.tab, self.shape = tab, ids.shape
        self.b0 = (ids & 1) != 0
        self.b1 = (ids & 2) != 0
        self.p1 = (ids & 4) != 0
        self.p2 = (ids & 8) != 0

    def wide(self, tile):
        reps = self.shape[0] // 8
        return jnp.broadcast_to(tile[None], (reps, 8, 128)).reshape(self.shape)

    def alloy(self, name):
        t = [self.wide(v) for v in getattr(self.tab, name)]
        return jnp.where(self.b1, jnp.where(self.b0, t[3], t[2]), jnp.where(self.b0, t[1], t[0]))

    def solute_gain(self):
        t = [self.wide(v) for v in self.tab.sg]
        return jnp.where(self.p2, t[2], jnp.where(self.p1, t[1], t[0]))

    def fine(self):
        return self.alloy("hg"), self.solute_gain()

    def ratio(self):
        sg = self.solute_gain()
        return self.alloy("gh"), 4.0 / (1.0 + sg * self.alloy("kp18"))

    def coarse(self):
        sg = self.solute_gain()
        return self.alloy("crh"), 4.0 * sg / (1.0 + sg * self.alloy("kp18"))

    def melt(self, h, c):
        sensible = h - self.alloy("hs")
        held = jnp.minimum(jnp.maximum(sensible, 0.0), self.alloy("lat"))
        t = (h - held) * self.alloy("icap")
        return t, c / (self.alloy("den0") + self.alloy("den1") * held)


F2 = range(2)


class Fields:
    def __init__(self, *refs):
        self.refs = refs
        self.shape = (2,) + tuple(refs[0].shape)

    def __getitem__(self, key):
        return self.refs[key[0]][key[1:]]

    def __setitem__(self, key, value):
        self.refs[key[0]][key[1:]] = value


class Tile:
    def __init__(self, y, n):
        self.y, self.n = y, n
        self.at = pl.ds(y, n)

    def pad(self, by=0):
        return pl.ds(self.y + (8 + by), self.n)


def tiles(count, ny, body):
    n = CHUNK if ny % CHUNK == 0 else ny
    per = ny // n

    def run(k, carry):
        body(k // per, Tile(pl.multiple_of((k % per) * n, n), n))
        return carry

    lax.fori_loop(0, count * per, run, 0)


def clear_rims(pad):
    rows, long = pad.shape[1], pad.shape[2]
    for f in F2:
        for r in range(rows):
            pad[f, r, 0:8, :] = jnp.zeros((8, 128), jnp.float32)
            pad[f, r, long - 8 : long, :] = jnp.zeros((8, 128), jnp.float32)


def clear_ends(pad):
    def body(i, t):
        for f in F2:
            pad[f, i * (pad.shape[1] - 1), t.pad(), :] = jnp.zeros((t.n, 128), jnp.float32)

    tiles(2, pad.shape[2] - 16, body)


def put_melt(tab, pad, r, t, ids, h, c):
    values = Cells(tab, ids).melt(h, c)
    for f in F2:
        pad[f, r, t.pad(), :] = values[f]


def lap(pad, f, r, t):
    mid = pad[f, r, t.pad(), :]
    lane = lax.broadcasted_iota(jnp.int32, mid.shape, 1)
    total = pad[f, r, t.pad(-1), :] + pad[f, r, t.pad(1), :]
    total = total + jnp.where(lane == 0, 0.0, pltpu.roll(mid, 1, 1))
    total = total + jnp.where(lane == 127, 0.0, pltpu.roll(mid, 127, 1))
    return total - 6.0 * mid + pad[f, r - 1, t.pad(), :] + pad[f, r + 1, t.pad(), :]


def fine(tab, pad, r, t, ids, now):
    rate = Cells(tab, ids).fine()
    return [now[f] + rate[f] * lap(pad, f, r, t) for f in F2]


def coarse(tab, pad, r, t, ids, now):
    rate = Cells(tab, ids).coarse()
    return [now[f] + rate[f] * lap(pad, f, r, t) for f in F2]


class Parts:
    def __init__(self, mid):
        self.mid, self.rows = mid, mid + 4

    def each(self, ny, body, which="mnx"):
        if "x" in which:
            tiles(2, ny, lambda i, t: body("x", i, i * (self.rows - 1), t))
        if "n" in which:
            tiles(2, ny, lambda i, t: body("n", i, 1 + i * (self.rows - 3), t))
        if "m" in which:
            tiles(self.mid, ny, lambda i, t: body("m", i, i + 2, t))


def first_edges_kernel(prm, h, c, mat, tl0, tl7):
    tab = Tables(prm)
    side = pl.program_id(0)

    def body(i, t):
        values = Cells(tab, mat[0, t.at, :]).melt(h[0, t.at, :], c[0, t.at, :])

        @pl.when(side == 0)
        def _():
            for f in F2:
                tl0[f, t.at, :] = values[f]

        @pl.when(side == 1)
        def _():
            for f in F2:
                tl7[f, t.at, :] = values[f]

    tiles(1, h.shape[1], body)


def first_step_kernel(prm, h, c, mat, ph, sm, sn, part, ids, ide, pad):
    tab = Tables(prm)
    rows, ny = h.shape[0], h.shape[1]
    outs = {"m": sm, "n": sn, "x": part}
    clear_rims(pad)
    clear_ends(pad)

    def melt(r, t):
        cell = mat[r, t.at, :] + 4 * ph[r, t.at, :]
        ids[r, t.at, :] = cell
        put_melt(tab, pad, r + 1, t, cell, h[r, t.at, :], c[r, t.at, :])

    def update(part_name, i, r, t):
        new = fine(tab, pad, r + 1, t, ids[r, t.at, :], (h[r, t.at, :], c[r, t.at, :]))
        for f in F2:
            outs[part_name][f, i, t.at, :] = new[f]

    tiles(rows, ny, melt)
    ide[0] = ids[0]
    ide[1] = ids[rows - 1]
    Parts(rows - 4).each(ny, update)


def step_body(prm, sm, sn, sx, ids, outs, pad):
    tab = Tables(prm)
    ny = sm.shape[2]
    now = {"m": sm, "n": sn, "x": sx}
    block = Parts(sm.shape[1])
    clear_rims(pad)
    clear_ends(pad)

    def at(name, i, t):
        return [now[name][f, i, t.at, :] for f in F2]

    def melt(name, i, r, t):
        put_melt(tab, pad, r + 1, t, ids[r, t.at, :], *at(name, i, t))

    def update(name, i, r, t):
        new = fine(tab, pad, r + 1, t, ids[r, t.at, :], at(name, i, t))
        for f in F2:
            outs[name][f, i, t.at, :] = new[f]

    block.each(ny, melt)
    block.each(ny, update, outs)


def step_kernel(prm, sm, sn, sx, ids, nm, nn, part, pad):
    step_body(prm, sm, sn, sx, ids, {"x": part, "n": nn, "m": nm}, pad)


def step_apart_kernel(prm, sm, sn, sx, ids, mh, mc, nn, part, pad):
    step_body(prm, sm, sn, sx, ids, {"x": part, "n": nn, "m": Fields(mh, mc)}, pad)


def step_joined_kernel(prm, mh, mc, sn, sx, ids, nm, nn, part, pad):
    step_body(prm, Fields(mh, mc), sn, sx, ids, {"x": part, "n": nn, "m": nm}, pad)


def replay_kernel(own, prm, mh, mc, sn, sx, ids, nm, nn, pad):
    @pl.when(own[0] != 0)
    def _():
        step_body(prm, Fields(mh, mc), sn, sx, ids, {"n": nn, "m": nm}, pad)


def edges_body(prm, gains, part, low, high, ide, edge, tl0, tl7):
    tab = Tables(prm)
    for e, (halo, tl) in enumerate(((low, tl0), (high, tl7))):

        def body(i, t, e=e, halo=halo, tl=tl):
            cells = Cells(tab, ide[e, t.at, :])
            rate = getattr(cells, gains)()
            new = [part[f, e, t.at, :] + rate[f] * halo[f, t.at, :] for f in F2]
            values = cells.melt(*new)
            for f in F2:
                edge[f, e, t.at, :] = new[f]
                tl[f, t.at, :] = values[f]

        tiles(1, part.shape[2], body)


def edges_kernel(prm, part, low, high, ide, edge, tl0, tl7):
    edges_body(prm, "fine", part, low, high, ide, edge, tl0, tl7)


def coarse_edges_kernel(own, prm, part, low, high, ide, old, *refs):
    edge, tl0, tl7 = refs[-3:]

    @pl.when(own[0] != 0)
    def _():
        edges_body(prm, "coarse", part, low, high, ide, edge, tl0, tl7)

    @pl.when(own[0] == 0)
    def _():
        edge[...] = old[...]


def base_kernel(prm, h, c, sm, sn, sx, ids, km, kn, kx):
    tab = Tables(prm)
    first = {"m": sm, "n": sn, "x": sx}
    outs = {"m": km, "n": kn, "x": kx}

    def body(name, i, r, t):
        ratio = Cells(tab, ids[r, t.at, :]).ratio()
        for f, u in enumerate((h[r, t.at, :], c[r, t.at, :])):
            outs[name][f, i, t.at, :] = u + ratio[f] * (first[name][f, i, t.at, :] - u)

    Parts(sm.shape[1]).each(h.shape[1], body)


def coarse_body(prm, arrived, base, old, ids, put, which, pad, edge_less):
    tab = Tables(prm)
    mid, ny = arrived["m"].shape[1], arrived["m"].shape[2]
    block = Parts(mid)
    clear_rims(pad)
    if edge_less:
        clear_ends(pad)

    def at(ref, i, t):
        return [ref[f, i, t.at, :] for f in F2]

    def melt(name, i, r, t):
        put_melt(tab, pad, r + 1, t, ids[r, t.at, :], *at(arrived[name], i, t))

    def update(name, i, r, t):
        new = coarse(tab, pad, r + 1, t, ids[r, t.at, :], at(arrived[name], i, t))
        end, start = at(old[name], i, t), at(base[name], i, t)
        for f in F2:
            put(name, f, i, r, t, new[f] + (end[f] - start[f]))

    block.each(ny, melt, arrived)
    block.each(ny, update, which)


def into(outs):
    def put(name, f, i, r, t, value):
        outs[name][f, i, t.at, :] = value

    return put


def coarse_mid_kernel(own, prm, am, an, km, ids, om, nm, pad):
    @pl.when(own[0] != 0)
    def _():
        coarse_body(
            prm, {"n": an, "m": am}, {"m": km}, {"m": om}, ids, into({"m": nm}), "m", pad, False
        )

    @pl.when(own[0] == 0)
    def _():
        nm[...] = om[...]


def coarse_rim_kernel(own, prm, am, an, ax, kn, kx, ids, on, ox, nn, part, pad):
    @pl.when(own[0] != 0)
    def _():
        coarse_body(
            prm,
            {"x": ax, "n": an, "m": am},
            {"n": kn, "x": kx},
            {"n": on, "x": ox},
            ids,
            into({"n": nn, "x": part}),
            "xn",
            pad,
            True,
        )

    @pl.when(own[0] == 0)
    def _():
        nn[...] = on[...]


def coarse_inner_kernel(own, prm, am, an, ax, km, kn, kx, ids, om, on, ox, nm, nn, part, pad):
    @pl.when(own[0] != 0)
    def _():
        coarse_body(
            prm,
            {"x": ax, "n": an, "m": am},
            {"m": km, "n": kn, "x": kx},
            {"m": om, "n": on, "x": ox},
            ids,
            into({"m": nm, "n": nn, "x": part}),
            "mnx",
            pad,
            True,
        )

    @pl.when(own[0] == 0)
    def _():
        nm[...] = om[...]
        nn[...] = on[...]


def last_rows_kernel(own, prm, am, an, ax, km, kn, kx, ids, om, on, ox, oh, oc, pad):
    out = (oh, oc)

    @pl.when(own[0] != 0)
    def _():
        def put(name, f, i, r, t, value):
            out[f][0, r, t.at, :] = value

        coarse_body(
            prm,
            {"x": ax, "n": an, "m": am},
            {"m": km, "n": kn, "x": kx},
            {"m": om, "n": on, "x": ox},
            ids,
            put,
            "mnx",
            pad,
            True,
        )

    @pl.when(own[0] == 0)
    def _():
        old = {"m": om, "n": on, "x": ox}

        def body(name, i, r, t):
            for f in F2:
                out[f][0, r, t.at, :] = old[name][f, i, t.at, :]

        Parts(om.shape[1]).each(om.shape[2], body)


def last_edges_kernel(own, prm, low, high, ide, oh, oc, nh, nc):
    first = pl.program_id(0) == 0

    @pl.when(own[0] != 0)
    def _():
        tab = Tables(prm)

        def body(i, t):
            rate = Cells(tab, ide[0, t.at, :]).coarse()
            for f, (old, new) in enumerate(((oh, nh), (oc, nc))):
                halo = jnp.where(first, low[f, t.at, :], high[f, t.at, :])
                new[0, 0, t.at, :] = old[0, 0, t.at, :] + rate[f] * halo

        tiles(1, ide.shape[1], body)

    @pl.when(own[0] == 0)
    def _():
        nh[...] = oh[...]
        nc[...] = oc[...]


def f32(*shape):
    return jax.ShapeDtypeStruct(shape, jnp.float32)


def i32(*shape):
    return jax.ShapeDtypeStruct(shape, jnp.int32)


TINY = pl.CostEstimate(flops=1000, bytes_accessed=1000, transcendentals=0)


def call(kernel, outs, args, smem, name, scratch=(), limit=8, after=(), through=()):
    after = (*after, *through)
    first = len(args) + len(after) - len(through)
    run = kernel
    if after:
        count = len(args)

        def run(*refs):
            kernel(*refs[:count], *refs[count + len(after) + len(through) :])

    return pl.pallas_call(
        run,
        out_shape=[f32(*x.shape) for x in through] + list(outs),
        in_specs=[SMEM] * smem + [VMEM] * (len(args) - smem) + [ANY] * len(after),
        out_specs=[ANY] * len(through) + [VMEM] * len(outs),
        input_output_aliases={first + i: i for i in range(len(through))},
        scratch_shapes=scratch,
        compiler_params=pltpu.CompilerParams(vmem_limit_bytes=limit * MIB),
        cost_estimate=TINY,
        name=name,
    )(*args, *after)


def per_device(slices, parts, enthalpy, solute, material, phase_flag, *params):
    rows, ny, nz = material.shape
    mid = rows - 4
    h0 = enthalpy.reshape(rows, ny, nz)
    c0 = solute.reshape(rows, ny, nz)
    prm = jnp.concatenate(params)
    slot = lax.axis_index("tm")
    pair, tall = f32(2, 2, ny, nz), f32(2, mid, ny, nz)
    halo = f32(2, ny, nz)
    pad = [pltpu.VMEM((2, rows + 2, ny + 16, nz), jnp.float32)]

    def move(x, tms, up, by):
        pairs = [
            (t * parts + s, (t + up) * parts + s + by)
            for t in tms
            for s in range(parts)
            if 0 <= s + by < parts
        ]
        return lax.ppermute(x, ("tm", "space"), pairs)

    def halos(tl0, tl7, tms, up):
        return move(tl7, tms, up, 1), move(tl0, tms, up, -1)

    def send(x, n):
        return move(x, (n - 1,), 1, 0)

    def own(n):
        return (slot == n).astype(jnp.int32).reshape(1)

    def gridded(kernel, steps, outs, out_specs, in_specs, args, name, aliases={}):
        return pl.pallas_call(
            kernel,
            grid=(steps,),
            out_shape=outs,
            in_specs=in_specs,
            out_specs=out_specs,
            input_output_aliases=aliases,
            compiler_params=pltpu.CompilerParams(vmem_limit_bytes=8 * MIB),
            cost_estimate=TINY,
            name=name,
        )(*args)

    edge_row = pl.BlockSpec((1, ny, nz), lambda i: ((rows - 1) * i, 0, 0))
    whole = pl.BlockSpec((2, ny, nz), lambda i: (0, 0, 0))
    far = [pltpu.with_memory_space_constraint(x, pltpu.HBM) for x in (h0, c0, material)]
    tl0, tl7 = gridded(
        first_edges_kernel,
        2,
        [halo] * 2,
        [whole] * 2,
        [SMEM] + [edge_row] * 3,
        (prm, *far),
        "first_edges",
    )
    every = range(slices)
    low, high = halos(tl0, tl7, every, 0)
    sm, sn, part, ids, ide = call(
        first_step_kernel,
        [tall, pair, pair, i32(rows, ny, nz), i32(2, ny, nz)],
        (prm, h0, c0, material, phase_flag),
        1,
        "first_step",
        pad,
        26,
    )

    def fine_edges(part, low, high, after=()):
        return call(
            edges_kernel, [pair, halo, halo], (prm, part, low, high, ide), 1, "edges", after=after
        )

    base = ()
    for k in range(STEPS - 1):
        sx, tl0, tl7 = fine_edges(part, low, high, base)
        low, high = halos(tl0, tl7, every, 0)
        if k == 0:
            base = call(
                base_kernel,
                [tall, pair, pair],
                (prm, h0, c0, sm, sn, sx, ids),
                1,
                "base",
                limit=16,
            )
        if k == STEPS - 3:
            *sm, sn, part = call(
                step_apart_kernel,
                [f32(mid, ny, nz)] * 2 + [pair, pair],
                (prm, sm, sn, sx, ids),
                1,
                "step_apart",
                pad,
                18,
            )
        elif k == STEPS - 2:
            last = (*sm, sn, sx)
            sm, sn, part = call(
                step_joined_kernel,
                [tall, pair, pair],
                (prm, *sm, sn, sx, ids),
                1,
                "step_joined",
                pad,
                18,
            )
        else:
            sm, sn, part = call(
                step_kernel, [tall, pair, pair], (prm, sm, sn, sx, ids), 1, "step", pad, 18
            )
    km, kn, kx = base

    am, an = call(
        replay_kernel,
        [tall, pair],
        (own(1), prm, *(send(x, 1) for x in last), ids),
        2,
        "replay",
        pad,
        18,
    )
    vm, vn = (
        call(
            coarse_mid_kernel,
            [tall],
            (own(1), prm, am, an, km, ids, sm),
            2,
            "coarse_mid",
            pad,
            18,
        )[0],
        sn,
    )
    vx, tl0, tl7 = fine_edges(part, low, high, (vm,))
    for n in range(1, slices):
        low, high = halos(tl0, tl7, (n - 1,), 1)
        ax = send(vx, n)
        if n > 1:
            am, an = send(vm, n), send(vn, n)
        if n == slices - 1:
            break
        if n == 1:
            vn, part = call(
                coarse_rim_kernel,
                [pair, pair],
                (own(n), prm, am, an, ax, kn, kx, ids, vn, vx),
                2,
                "coarse_rim",
                pad,
                20,
            )
        else:
            vm, vn, part = call(
                coarse_inner_kernel,
                [tall, pair, pair],
                (own(n), prm, am, an, ax, km, kn, kx, ids, vm, vn, vx),
                2,
                "coarse_inner",
                pad,
                26,
            )
        *passed, vx, tl0, tl7 = call(
            coarse_edges_kernel,
            [pair, halo, halo],
            (own(n), prm, part, low, high, ide, vx),
            2,
            "coarse_edges",
            through=(vm, vn) if n > 1 else (),
        )
        if n > 1:
            vm, vn = passed

    out = f32(1, rows, ny, nz)
    last_own = own(slices - 1)
    oh, oc = call(
        last_rows_kernel,
        [out, out],
        (last_own, prm, am, an, ax, km, kn, kx, ids, vm, vn, vx),
        2,
        "last_rows",
        pad,
        28,
    )
    out_row = pl.BlockSpec((1, 1, ny, nz), lambda i: (0, (rows - 1) * i, 0, 0))
    one = pl.BlockSpec((1, ny, nz), lambda i: (i, 0, 0))
    return tuple(
        gridded(
            last_edges_kernel,
            2,
            [out, out],
            [out_row] * 2,
            [SMEM, SMEM, whole, whole, one, out_row, out_row],
            (last_own, prm, low, high, ide, oh, oc),
            "last_edges",
            {5: 0, 6: 1},
        )
    )


def solution(mesh):
    body = functools.partial(per_device, mesh.shape["tm"], mesh.shape["space"])
    return jax.shard_map(
        body,
        mesh=mesh,
        in_specs=(
            P("tm", "space", None, None),
            P("tm", "space", None, None),
            P("space", None, None),
            P("space", None, None),
        )
        + (P(),) * 7,
        out_specs=(P("tm", "space", None, None), P("tm", "space", None, None)),
        check_vma=False,
    )
```

```python
import functools

import jax
import jax.numpy as jnp
from jax import lax
from jax.experimental import pallas as pl
from jax.experimental.pallas import tpu as pltpu
from jax.sharding import PartitionSpec as P

STEPS = 4
CHUNK = 256
MIB = 1024 * 1024
SMEM = pl.BlockSpec(memory_space=pltpu.SMEM)
VMEM = pl.BlockSpec(memory_space=pltpu.VMEM)
ANY = pl.BlockSpec(memory_space=pl.ANY)


class Tables:
    def __init__(self, prm):
        def raw(first, count):
            return [jnp.full((8, 128), prm[first + m], jnp.float32) for m in range(count)]

        cap, self.lat, self.hs = raw(0, 4), raw(4, 4), raw(8, 4)
        kp, bd, xr = raw(12, 4), raw(16, 4), raw(20, 4)
        self.sg = raw(24, 3)
        q = [(1.0 - k) / (1.0 + b) for k, b in zip(kp, bd)]
        self.icap = [1.0 / c for c in cap]
        self.den0 = [1.0 - v for v in q]
        self.den1 = [v / t for v, t in zip(q, self.lat)]
        self.hg = [x * c for x, c in zip(xr, cap)]
        self.gh = [4.0 / (1.0 + 18.0 * x) for x in xr]
        self.crh = [h * g for h, g in zip(self.hg, self.gh)]
        self.kp18 = [18.0 / k for k in kp]


class Cells:
    def __init__(self, tab, ids):
        self.tab, self.shape = tab, ids.shape
        self.b0 = (ids & 1) != 0
        self.b1 = (ids & 2) != 0
        self.p1 = (ids & 4) != 0
        self.p2 = (ids & 8) != 0

    def wide(self, tile):
        reps = self.shape[0] // 8
        return jnp.broadcast_to(tile[None], (reps, 8, 128)).reshape(self.shape)

    def alloy(self, name):
        t = [self.wide(v) for v in getattr(self.tab, name)]
        return jnp.where(self.b1, jnp.where(self.b0, t[3], t[2]), jnp.where(self.b0, t[1], t[0]))

    def solute_gain(self):
        t = [self.wide(v) for v in self.tab.sg]
        return jnp.where(self.p2, t[2], jnp.where(self.p1, t[1], t[0]))

    def fine(self):
        return self.alloy("hg"), self.solute_gain()

    def ratio(self):
        sg = self.solute_gain()
        return self.alloy("gh"), 4.0 / (1.0 + sg * self.alloy("kp18"))

    def coarse(self):
        sg = self.solute_gain()
        return self.alloy("crh"), 4.0 * sg / (1.0 + sg * self.alloy("kp18"))

    def melt(self, h, c):
        sensible = h - self.alloy("hs")
        held = jnp.minimum(jnp.maximum(sensible, 0.0), self.alloy("lat"))
        t = (h - held) * self.alloy("icap")
        return t, c / (self.alloy("den0") + self.alloy("den1") * held)


F2 = range(2)


class Fields:
    def __init__(self, *refs):
        self.refs = refs
        self.shape = (2,) + tuple(refs[0].shape)

    def __getitem__(self, key):
        return self.refs[key[0]][key[1:]]

    def __setitem__(self, key, value):
        self.refs[key[0]][key[1:]] = value


class Rows:
    def __init__(self, ref, first):
        self.ref, self.first = ref, first

    def key(self, key):
        return (key[0], key[1] + self.first, *key[2:])

    def __getitem__(self, key):
        return self.ref[self.key(key)]

    def __setitem__(self, key, value):
        self.ref[self.key(key)] = value


class Tile:
    def __init__(self, y, n):
        self.y, self.n = y, n
        self.at = pl.ds(y, n)

    def pad(self, by=0):
        return pl.ds(self.y + (8 + by), self.n)


def tiles(count, ny, body):
    n = CHUNK if ny % CHUNK == 0 else ny
    per = ny // n

    def run(k, carry):
        body(k // per, Tile(pl.multiple_of((k % per) * n, n), n))
        return carry

    lax.fori_loop(0, count * per, run, 0)


def clear_rims(pad):
    rows, long = pad.shape[1], pad.shape[2]
    for f in F2:
        for r in range(rows):
            pad[f, r, 0:8, :] = jnp.zeros((8, 128), jnp.float32)
            pad[f, r, long - 8 : long, :] = jnp.zeros((8, 128), jnp.float32)


def clear_ends(pad):
    def body(i, t):
        for f in F2:
            pad[f, i * (pad.shape[1] - 1), t.pad(), :] = jnp.zeros((t.n, 128), jnp.float32)

    tiles(2, pad.shape[2] - 16, body)


def put_melt(tab, pad, r, t, ids, h, c):
    values = Cells(tab, ids).melt(h, c)
    for f in F2:
        pad[f, r, t.pad(), :] = values[f]


def lap(pad, f, r, t):
    mid = pad[f, r, t.pad(), :]
    lane = lax.broadcasted_iota(jnp.int32, mid.shape, 1)
    total = pad[f, r, t.pad(-1), :] + pad[f, r, t.pad(1), :]
    total = total + jnp.where(lane == 0, 0.0, pltpu.roll(mid, 1, 1))
    total = total + jnp.where(lane == 127, 0.0, pltpu.roll(mid, 127, 1))
    return total - 6.0 * mid + pad[f, r - 1, t.pad(), :] + pad[f, r + 1, t.pad(), :]


def fine(tab, pad, r, t, ids, now):
    rate = Cells(tab, ids).fine()
    return [now[f] + rate[f] * lap(pad, f, r, t) for f in F2]


def coarse(tab, pad, r, t, ids, now):
    rate = Cells(tab, ids).coarse()
    return [now[f] + rate[f] * lap(pad, f, r, t) for f in F2]


class Parts:
    def __init__(self, mid):
        self.mid, self.rows = mid, mid + 4

    def each(self, ny, body, which="mnx"):
        if "x" in which:
            tiles(2, ny, lambda i, t: body("x", i, i * (self.rows - 1), t))
        if "n" in which:
            tiles(2, ny, lambda i, t: body("n", i, 1 + i * (self.rows - 3), t))
        if "m" in which:
            tiles(self.mid, ny, lambda i, t: body("m", i, i + 2, t))


def first_edges_kernel(prm, h, c, mat, tl0, tl7):
    tab = Tables(prm)
    side = pl.program_id(0)

    def body(i, t):
        values = Cells(tab, mat[0, t.at, :]).melt(h[0, t.at, :], c[0, t.at, :])

        @pl.when(side == 0)
        def _():
            for f in F2:
                tl0[f, t.at, :] = values[f]

        @pl.when(side == 1)
        def _():
            for f in F2:
                tl7[f, t.at, :] = values[f]

    tiles(1, h.shape[1], body)


def first_step_kernel(prm, h, c, mat, ph, sm, sn, part, ids, ide, pad):
    tab = Tables(prm)
    rows, ny = h.shape[0], h.shape[1]
    outs = {"m": sm, "n": sn, "x": part}
    clear_rims(pad)
    clear_ends(pad)

    def melt(r, t):
        cell = mat[r, t.at, :] + 4 * ph[r, t.at, :]
        ids[r, t.at, :] = cell
        put_melt(tab, pad, r + 1, t, cell, h[r, t.at, :], c[r, t.at, :])

    def update(part_name, i, r, t):
        new = fine(tab, pad, r + 1, t, ids[r, t.at, :], (h[r, t.at, :], c[r, t.at, :]))
        for f in F2:
            outs[part_name][f, i, t.at, :] = new[f]

    tiles(rows, ny, melt)
    ide[0] = ids[0]
    ide[1] = ids[rows - 1]
    Parts(rows - 4).each(ny, update)


def step_body(prm, sm, sn, sx, ids, outs, pad):
    tab = Tables(prm)
    ny = sm.shape[2]
    now = {"m": sm, "n": sn, "x": sx}
    block = Parts(sm.shape[1])
    clear_rims(pad)
    clear_ends(pad)

    def at(name, i, t):
        return [now[name][f, i, t.at, :] for f in F2]

    def melt(name, i, r, t):
        put_melt(tab, pad, r + 1, t, ids[r, t.at, :], *at(name, i, t))

    def update(name, i, r, t):
        new = fine(tab, pad, r + 1, t, ids[r, t.at, :], at(name, i, t))
        for f in F2:
            outs[name][f, i, t.at, :] = new[f]

    block.each(ny, melt)
    block.each(ny, update, outs)


def step_kernel(prm, sm, sn, sx, ids, nm, nn, part, pad):
    step_body(prm, sm, sn, sx, ids, {"x": part, "n": nn, "m": nm}, pad)


def step_apart_kernel(prm, sm, sn, sx, ids, mh, mc, nn, part, pad):
    step_body(prm, sm, sn, sx, ids, {"x": part, "n": nn, "m": Fields(mh, mc)}, pad)


def step_joined_kernel(prm, mh, mc, sn, sx, ids, nm, nn, part, pad):
    step_body(prm, Fields(mh, mc), sn, sx, ids, {"x": part, "n": nn, "m": nm}, pad)


def replay_kernel(own, prm, mh, mc, sn, sx, ids, km, om, am, an, nm, pad):
    @pl.when(own[0] != 0)
    def _():
        step_body(prm, Fields(mh, mc), sn, sx, ids, {"n": an, "m": am}, pad)
        coarse_body(
            prm, {"n": an, "m": am}, {"m": km}, {"m": om}, ids, into({"m": nm}), "m", pad, False
        )

    @pl.when(own[0] == 0)
    def _():
        nm[...] = om[...]


def edges_body(prm, gains, part, low, high, ide, edge, tl0, tl7):
    tab = Tables(prm)
    for e, (halo, tl) in enumerate(((low, tl0), (high, tl7))):

        def body(i, t, e=e, halo=halo, tl=tl):
            cells = Cells(tab, ide[e, t.at, :])
            rate = getattr(cells, gains)()
            new = [part[f, e, t.at, :] + rate[f] * halo[f, t.at, :] for f in F2]
            values = cells.melt(*new)
            for f in F2:
                edge[f, e, t.at, :] = new[f]
                tl[f, t.at, :] = values[f]

        tiles(1, part.shape[2], body)


def edges_kernel(prm, part, low, high, ide, edge, tl0, tl7):
    edges_body(prm, "fine", part, low, high, ide, edge, tl0, tl7)


def coarse_edges_kernel(own, prm, part, low, high, ide, old, *refs):
    edge, tl0, tl7 = refs

    @pl.when(own[0] != 0)
    def _():
        edges_body(prm, "coarse", part, low, high, ide, edge, tl0, tl7)

    @pl.when(own[0] == 0)
    def _():
        edge[...] = old[...]


def base_kernel(prm, h, c, sm, sn, sx, ids, km, kn, kx):
    tab = Tables(prm)
    first = {"m": sm, "n": sn, "x": sx}
    outs = {"m": km, "n": kn, "x": kx}

    def body(name, i, r, t):
        ratio = Cells(tab, ids[r, t.at, :]).ratio()
        for f, u in enumerate((h[r, t.at, :], c[r, t.at, :])):
            outs[name][f, i, t.at, :] = u + ratio[f] * (first[name][f, i, t.at, :] - u)

    Parts(sm.shape[1]).each(h.shape[1], body)


def coarse_body(prm, arrived, base, old, ids, put, which, pad, edge_less):
    tab = Tables(prm)
    mid, ny = arrived["m"].shape[1], arrived["m"].shape[2]
    block = Parts(mid)
    clear_rims(pad)
    if edge_less:
        clear_ends(pad)

    def at(ref, i, t):
        return [ref[f, i, t.at, :] for f in F2]

    def melt(name, i, r, t):
        put_melt(tab, pad, r + 1, t, ids[r, t.at, :], *at(arrived[name], i, t))

    def update(name, i, r, t):
        new = coarse(tab, pad, r + 1, t, ids[r, t.at, :], at(arrived[name], i, t))
        end, start = at(old[name], i, t), at(base[name], i, t)
        for f in F2:
            put(name, f, i, r, t, new[f] + (end[f] - start[f]))

    if "m" in which:
        block.each(ny, melt, arrived)
    else:
        block.each(ny, melt, "nx")
        tiles(2, ny, lambda i, t: melt("m", i * (mid - 1), 2 + i * (mid - 1), t))
    block.each(ny, update, which)


def into(outs):
    def put(name, f, i, r, t, value):
        outs[name][f, i, t.at, :] = value

    return put


def coarse_mid_kernel(own, prm, am, an, km, ids, om, nm, pad):
    @pl.when(own[0] != 0)
    def _():
        coarse_body(
            prm, {"n": an, "m": am}, {"m": km}, {"m": om}, ids, into({"m": nm}), "m", pad, False
        )

    @pl.when(own[0] == 0)
    def _():
        nm[...] = om[...]


def coarse_rim_kernel(own, prm, am, an, ax, kn, kx, ids, on, ox, nn, part, pad):
    @pl.when(own[0] != 0)
    def _():
        coarse_body(
            prm,
            {"x": ax, "n": an, "m": am},
            {"n": kn, "x": kx},
            {"n": on, "x": ox},
            ids,
            into({"n": nn, "x": part}),
            "xn",
            pad,
            True,
        )

    @pl.when(own[0] == 0)
    def _():
        nn[...] = on[...]


def coarse_outer_kernel(
    own, prm, am, an, ax, low, high, kn, kx, ids, ide, on, ox, *refs
):
    rim, tl0, tl7, part, pad = refs[-5:]
    edge, beside = Rows(rim, 0), Rows(rim, 2)

    @pl.when(own[0] != 0)
    def _():
        coarse_body(
            prm,
            {"x": ax, "n": an, "m": am},
            {"n": kn, "x": kx},
            {"n": on, "x": ox},
            ids,
            into({"n": beside, "x": part}),
            "xn",
            pad,
            True,
        )
        edges_body(prm, "coarse", part, low, high, ide, edge, tl0, tl7)

    @pl.when(own[0] == 0)
    def _():
        for f in F2:
            for e in range(2):
                edge[f, e] = ox[f, e]
                beside[f, e] = on[f, e]


def last_rows_kernel(own, prm, am, ar, km, kn, kx, ids, om, rim, oh, oc, pad):
    out = (oh, oc)
    ax, an, ox, on = Rows(ar, 0), Rows(ar, 2), Rows(rim, 0), Rows(rim, 2)

    @pl.when(own[0] != 0)
    def _():
        def put(name, f, i, r, t, value):
            out[f][0, r, t.at, :] = value

        coarse_body(
            prm,
            {"x": ax, "n": an, "m": am},
            {"m": km, "n": kn, "x": kx},
            {"m": om, "n": on, "x": ox},
            ids,
            put,
            "mnx",
            pad,
            True,
        )

    @pl.when(own[0] == 0)
    def _():
        old = {"m": om, "n": on, "x": ox}

        def body(name, i, r, t):
            for f in F2:
                out[f][0, r, t.at, :] = old[name][f, i, t.at, :]

        Parts(om.shape[1]).each(om.shape[2], body)


def last_edges_kernel(own, prm, low, high, ide, oh, oc, nh, nc):
    first = pl.program_id(0) == 0

    @pl.when(own[0] != 0)
    def _():
        tab = Tables(prm)

        def body(i, t):
            rate = Cells(tab, ide[0, t.at, :]).coarse()
            for f, (old, new) in enumerate(((oh, nh), (oc, nc))):
                halo = jnp.where(first, low[f, t.at, :], high[f, t.at, :])
                new[0, 0, t.at, :] = old[0, 0, t.at, :] + rate[f] * halo

        tiles(1, ide.shape[1], body)

    @pl.when(own[0] == 0)
    def _():
        nh[...] = oh[...]
        nc[...] = oc[...]


def f32(*shape):
    return jax.ShapeDtypeStruct(shape, jnp.float32)


def i32(*shape):
    return jax.ShapeDtypeStruct(shape, jnp.int32)


TINY = pl.CostEstimate(flops=1000, bytes_accessed=1000, transcendentals=0)


def call(kernel, outs, args, smem, name, scratch=(), limit=8, after=(), through=()):
    after = (*after, *through)
    first = len(args) + len(after) - len(through)
    run = kernel
    if after:
        count = len(args)

        def run(*refs):
            kernel(*refs[:count], *refs[count + len(after) + len(through) :])

    return pl.pallas_call(
        run,
        out_shape=[f32(*x.shape) for x in through] + list(outs),
        in_specs=[SMEM] * smem + [VMEM] * (len(args) - smem) + [ANY] * len(after),
        out_specs=[ANY] * len(through) + [VMEM] * len(outs),
        input_output_aliases={first + i: i for i in range(len(through))},
        scratch_shapes=scratch,
        compiler_params=pltpu.CompilerParams(vmem_limit_bytes=limit * MIB),
        cost_estimate=TINY,
        name=name,
    )(*args, *after)


def per_device(slices, parts, enthalpy, solute, material, phase_flag, *params):
    rows, ny, nz = material.shape
    mid = rows - 4
    h0 = enthalpy.reshape(rows, ny, nz)
    c0 = solute.reshape(rows, ny, nz)
    prm = jnp.concatenate(params)
    slot = lax.axis_index("tm")
    pair, tall = f32(2, 2, ny, nz), f32(2, mid, ny, nz)
    halo = f32(2, ny, nz)
    pad = [pltpu.VMEM((2, rows + 2, ny + 16, nz), jnp.float32)]

    def move(x, tms, up, by):
        pairs = [
            (t * parts + s, (t + up) * parts + s + by)
            for t in tms
            for s in range(parts)
            if 0 <= s + by < parts
        ]
        return lax.ppermute(x, ("tm", "space"), pairs)

    def halos(tl0, tl7, tms, up):
        return move(tl7, tms, up, 1), move(tl0, tms, up, -1)

    def send(x, n):
        return move(x, (n - 1,), 1, 0)

    def own(n):
        return (slot == n).astype(jnp.int32).reshape(1)

    def gridded(kernel, steps, outs, out_specs, in_specs, args, name, aliases={}):
        return pl.pallas_call(
            kernel,
            grid=(steps,),
            out_shape=outs,
            in_specs=in_specs,
            out_specs=out_specs,
            input_output_aliases=aliases,
            compiler_params=pltpu.CompilerParams(vmem_limit_bytes=8 * MIB),
            cost_estimate=TINY,
            name=name,
        )(*args)

    edge_row = pl.BlockSpec((1, ny, nz), lambda i: ((rows - 1) * i, 0, 0))
    whole = pl.BlockSpec((2, ny, nz), lambda i: (0, 0, 0))
    far = [pltpu.with_memory_space_constraint(x, pltpu.HBM) for x in (h0, c0, material)]
    tl0, tl7 = gridded(
        first_edges_kernel,
        2,
        [halo] * 2,
        [whole] * 2,
        [SMEM] + [edge_row] * 3,
        (prm, *far),
        "first_edges",
    )
    every = range(slices)
    low, high = halos(tl0, tl7, every, 0)
    sm, sn, part, ids, ide = call(
        first_step_kernel,
        [tall, pair, pair, i32(rows, ny, nz), i32(2, ny, nz)],
        (prm, h0, c0, material, phase_flag),
        1,
        "first_step",
        pad,
        26,
    )

    def fine_edges(part, low, high, after=()):
        return call(
            edges_kernel, [pair, halo, halo], (prm, part, low, high, ide), 1, "edges", after=after
        )

    base = ()
    for k in range(STEPS - 1):
        sx, tl0, tl7 = fine_edges(part, low, high, base)
        low, high = halos(tl0, tl7, every, 0)
        if k == 0:
            base = call(
                base_kernel,
                [tall, pair, pair],
                (prm, h0, c0, sm, sn, sx, ids),
                1,
                "base",
                limit=16,
            )
        if k == STEPS - 3:
            *sm, sn, part = call(
                step_apart_kernel,
                [f32(mid, ny, nz)] * 2 + [pair, pair],
                (prm, sm, sn, sx, ids),
                1,
                "step_apart",
                pad,
                18,
            )
        elif k == STEPS - 2:
            last = (*sm, sn, sx)
            sm, sn, part = call(
                step_joined_kernel,
                [tall, pair, pair],
                (prm, *sm, sn, sx, ids),
                1,
                "step_joined",
                pad,
                18,
            )
        else:
            sm, sn, part = call(
                step_kernel, [tall, pair, pair], (prm, sm, sn, sx, ids), 1, "step", pad, 18
            )
    km, kn, kx = base

    am, an, vm = call(
        replay_kernel,
        [tall, pair, tall],
        (own(1), prm, *(send(x, 1) for x in last), ids, km, sm),
        2,
        "replay",
        pad,
        24,
    )
    vn = sn
    vx, tl0, tl7 = fine_edges(part, low, high, (vm,))
    low, high = halos(tl0, tl7, (0,), 1)
    ax = send(vx, 1)
    vn, part = call(
        coarse_rim_kernel,
        [pair, pair],
        (own(1), prm, am, an, ax, kn, kx, ids, vn, vx),
        2,
        "coarse_rim",
        pad,
        20,
    )
    vx, tl0, tl7 = call(
        coarse_edges_kernel,
        [pair, halo, halo],
        (own(1), prm, part, low, high, ide, vx),
        2,
        "coarse_edges",
    )
    rim = None
    for n in range(2, slices):
        low, high = halos(tl0, tl7, (n - 1,), 1)
        am = send(vm, n)
        if n == 2:
            an, ax = send(vn, n), send(vx, n)
        else:
            ar = send(rim, n)
        if n == slices - 1:
            break
        vm = call(
            coarse_mid_kernel,
            [tall],
            (own(n), prm, am, an, km, ids, vm),
            2,
            "coarse_mid",
            pad,
            18,
        )[0]
        vm, rim, tl0, tl7 = call(
            coarse_outer_kernel,
            [f32(2, 4, ny, nz), halo, halo],
            (own(n), prm, am, an, ax, low, high, kn, kx, ids, ide, vn, vx),
            2,
            "coarse_outer",
            [pltpu.VMEM((2, 2, ny, nz), jnp.float32), *pad],
            26,
            through=(vm,),
        )

    out = f32(1, rows, ny, nz)
    last_own = own(slices - 1)
    oh, oc = call(
        last_rows_kernel,
        [out, out],
        (last_own, prm, am, ar, km, kn, kx, ids, vm, rim),
        2,
        "last_rows",
        pad,
        28,
    )
    out_row = pl.BlockSpec((1, 1, ny, nz), lambda i: (0, (rows - 1) * i, 0, 0))
    one = pl.BlockSpec((1, ny, nz), lambda i: (i, 0, 0))
    return tuple(
        gridded(
            last_edges_kernel,
            2,
            [out, out],
            [out_row] * 2,
            [SMEM, SMEM, whole, whole, one, out_row, out_row],
            (last_own, prm, low, high, ide, oh, oc),
            "last_edges",
            {5: 0, 6: 1},
        )
    )


def solution(mesh):
    body = functools.partial(per_device, mesh.shape["tm"], mesh.shape["space"])
    return jax.shard_map(
        body,
        mesh=mesh,
        in_specs=(
            P("tm", "space", None, None),
            P("tm", "space", None, None),
            P("space", None, None),
            P("space", None, None),
        )
        + (P(),) * 7,
        out_specs=(P("tm", "space", None, None), P("tm", "space", None, None)),
        check_vma=False,
    )
```

```python
import functools

import jax
import jax.numpy as jnp
from jax import lax
from jax.experimental import pallas as pl
from jax.experimental.pallas import tpu as pltpu
from jax.sharding import PartitionSpec as P

STEPS = 4
CHUNK = 256
MIB = 1024 * 1024
SMEM = pl.BlockSpec(memory_space=pltpu.SMEM)
VMEM = pl.BlockSpec(memory_space=pltpu.VMEM)
ANY = pl.BlockSpec(memory_space=pl.ANY)


class Tables:
    def __init__(self, prm):
        def raw(first, count):
            return [jnp.full((8, 128), prm[first + m], jnp.float32) for m in range(count)]

        cap, self.lat, self.hs = raw(0, 4), raw(4, 4), raw(8, 4)
        kp, bd, xr = raw(12, 4), raw(16, 4), raw(20, 4)
        self.sg = raw(24, 3)
        q = [(1.0 - k) / (1.0 + b) for k, b in zip(kp, bd)]
        self.icap = [1.0 / c for c in cap]
        self.den0 = [1.0 - v for v in q]
        self.den1 = [v / t for v, t in zip(q, self.lat)]
        self.hg = [x * c for x, c in zip(xr, cap)]
        self.gh = [4.0 / (1.0 + 18.0 * x) for x in xr]
        self.crh = [h * g for h, g in zip(self.hg, self.gh)]
        self.kp18 = [18.0 / k for k in kp]


class Cells:
    def __init__(self, tab, ids):
        self.tab, self.shape = tab, ids.shape
        self.b0 = (ids & 1) != 0
        self.b1 = (ids & 2) != 0
        self.p1 = (ids & 4) != 0
        self.p2 = (ids & 8) != 0

    def wide(self, tile):
        reps = self.shape[0] // 8
        return jnp.broadcast_to(tile[None], (reps, 8, 128)).reshape(self.shape)

    def alloy(self, name):
        t = [self.wide(v) for v in getattr(self.tab, name)]
        return jnp.where(self.b1, jnp.where(self.b0, t[3], t[2]), jnp.where(self.b0, t[1], t[0]))

    def solute_gain(self):
        t = [self.wide(v) for v in self.tab.sg]
        return jnp.where(self.p2, t[2], jnp.where(self.p1, t[1], t[0]))

    def fine(self):
        return self.alloy("hg"), self.solute_gain()

    def ratio(self):
        sg = self.solute_gain()
        return self.alloy("gh"), 4.0 / (1.0 + sg * self.alloy("kp18"))

    def coarse(self):
        sg = self.solute_gain()
        return self.alloy("crh"), 4.0 * sg / (1.0 + sg * self.alloy("kp18"))

    def melt(self, h, c):
        sensible = h - self.alloy("hs")
        held = jnp.minimum(jnp.maximum(sensible, 0.0), self.alloy("lat"))
        t = (h - held) * self.alloy("icap")
        return t, c / (self.alloy("den0") + self.alloy("den1") * held)


F2 = range(2)


class Fields:
    def __init__(self, *refs):
        self.refs = refs
        self.shape = (2,) + tuple(refs[0].shape)

    def __getitem__(self, key):
        return self.refs[key[0]][key[1:]]

    def __setitem__(self, key, value):
        self.refs[key[0]][key[1:]] = value


class Rows:
    def __init__(self, ref, first):
        self.ref, self.first = ref, first

    def key(self, key):
        return (key[0], key[1] + self.first, *key[2:])

    def __getitem__(self, key):
        return self.ref[self.key(key)]

    def __setitem__(self, key, value):
        self.ref[self.key(key)] = value


class Tile:
    def __init__(self, y, n):
        self.y, self.n = y, n
        self.at = pl.ds(y, n)

    def pad(self, by=0):
        return pl.ds(self.y + (8 + by), self.n)


def tiles(count, ny, body):
    n = CHUNK if ny % CHUNK == 0 else ny
    per = ny // n

    def run(k, carry):
        body(k // per, Tile(pl.multiple_of((k % per) * n, n), n))
        return carry

    lax.fori_loop(0, count * per, run, 0)


def clear_rims(pad):
    rows, long = pad.shape[1], pad.shape[2]
    for f in F2:
        for r in range(rows):
            pad[f, r, 0:8, :] = jnp.zeros((8, 128), jnp.float32)
            pad[f, r, long - 8 : long, :] = jnp.zeros((8, 128), jnp.float32)


def clear_ends(pad):
    def body(i, t):
        for f in F2:
            pad[f, i * (pad.shape[1] - 1), t.pad(), :] = jnp.zeros((t.n, 128), jnp.float32)

    tiles(2, pad.shape[2] - 16, body)


def put_melt(tab, pad, r, t, ids, h, c):
    values = Cells(tab, ids).melt(h, c)
    for f in F2:
        pad[f, r, t.pad(), :] = values[f]


def lap(pad, f, r, t):
    mid = pad[f, r, t.pad(), :]
    lane = lax.broadcasted_iota(jnp.int32, mid.shape, 1)
    total = pad[f, r, t.pad(-1), :] + pad[f, r, t.pad(1), :]
    total = total + jnp.where(lane == 0, 0.0, pltpu.roll(mid, 1, 1))
    total = total + jnp.where(lane == 127, 0.0, pltpu.roll(mid, 127, 1))
    return total - 6.0 * mid + pad[f, r - 1, t.pad(), :] + pad[f, r + 1, t.pad(), :]


def fine(tab, pad, r, t, ids, now):
    rate = Cells(tab, ids).fine()
    return [now[f] + rate[f] * lap(pad, f, r, t) for f in F2]


def coarse(tab, pad, r, t, ids, now):
    rate = Cells(tab, ids).coarse()
    return [now[f] + rate[f] * lap(pad, f, r, t) for f in F2]


class Parts:
    def __init__(self, mid):
        self.mid, self.rows = mid, mid + 4

    def each(self, ny, body, which="mnx"):
        if "x" in which:
            tiles(2, ny, lambda i, t: body("x", i, i * (self.rows - 1), t))
        if "n" in which:
            tiles(2, ny, lambda i, t: body("n", i, 1 + i * (self.rows - 3), t))
        if "m" in which:
            tiles(self.mid, ny, lambda i, t: body("m", i, i + 2, t))


def first_edges_kernel(prm, h, c, mat, tl0, tl7, later0, later7):
    tab = Tables(prm)
    side = pl.program_id(0)

    def body(i, t):
        values = Cells(tab, mat[0, t.at, :]).melt(h[0, t.at, :], c[0, t.at, :])

        @pl.when(side == 0)
        def _():
            for f in F2:
                tl0[f, t.at, :] = values[f]
                later0[f, t.at, :] = values[f]

        @pl.when(side == 1)
        def _():
            for f in F2:
                tl7[f, t.at, :] = values[f]
                later7[f, t.at, :] = values[f]

    tiles(1, h.shape[1], body)


def first_step_kernel(prm, h, c, mat, ph, sm, sn, part, ids, ide, pad):
    tab = Tables(prm)
    rows, ny = h.shape[0], h.shape[1]
    outs = {"m": sm, "n": sn, "x": part}
    clear_rims(pad)
    clear_ends(pad)

    def melt(r, t):
        cell = mat[r, t.at, :] + 4 * ph[r, t.at, :]
        ids[r, t.at, :] = cell
        put_melt(tab, pad, r + 1, t, cell, h[r, t.at, :], c[r, t.at, :])

    def update(part_name, i, r, t):
        new = fine(tab, pad, r + 1, t, ids[r, t.at, :], (h[r, t.at, :], c[r, t.at, :]))
        for f in F2:
            outs[part_name][f, i, t.at, :] = new[f]

    tiles(rows, ny, melt)
    ide[0] = ids[0]
    ide[1] = ids[rows - 1]
    Parts(rows - 4).each(ny, update)


def step_body(prm, sm, sn, sx, ids, outs, pad):
    tab = Tables(prm)
    ny = sm.shape[2]
    now = {"m": sm, "n": sn, "x": sx}
    block = Parts(sm.shape[1])
    clear_rims(pad)
    clear_ends(pad)

    def at(name, i, t):
        return [now[name][f, i, t.at, :] for f in F2]

    def melt(name, i, r, t):
        put_melt(tab, pad, r + 1, t, ids[r, t.at, :], *at(name, i, t))

    def update(name, i, r, t):
        new = fine(tab, pad, r + 1, t, ids[r, t.at, :], at(name, i, t))
        for f in F2:
            outs[name][f, i, t.at, :] = new[f]

    block.each(ny, melt)
    block.each(ny, update, outs)


def step_kernel(prm, sm, sn, sx, ids, nm, nn, part, pad):
    step_body(prm, sm, sn, sx, ids, {"x": part, "n": nn, "m": nm}, pad)


def step_apart_kernel(prm, sm, sn, sx, ids, mh, mc, nn, part, pad):
    step_body(prm, sm, sn, sx, ids, {"x": part, "n": nn, "m": Fields(mh, mc)}, pad)


def step_joined_kernel(prm, mh, mc, sn, sx, ids, nm, nn, part, pad):
    step_body(prm, Fields(mh, mc), sn, sx, ids, {"x": part, "n": nn, "m": nm}, pad)


def replay_kernel(own, prm, mh, mc, sn, sx, ids, km, om, am, an, nm, pad):
    @pl.when(own[0] != 0)
    def _():
        step_body(prm, Fields(mh, mc), sn, sx, ids, {"n": an, "m": am}, pad)
        coarse_body(
            prm, {"n": an, "m": am}, {"m": km}, {"m": om}, ids, into({"m": nm}), "m", pad, False
        )

    @pl.when(own[0] == 0)
    def _():
        nm[...] = om[...]


def edges_body(prm, gains, part, low, high, ide, edge, tl0, tl7):
    tab = Tables(prm)
    for e, (halo, tl) in enumerate(((low, tl0), (high, tl7))):

        def body(i, t, e=e, halo=halo, tl=tl):
            cells = Cells(tab, ide[e, t.at, :])
            rate = getattr(cells, gains)()
            new = [part[f, e, t.at, :] + rate[f] * halo[f, t.at, :] for f in F2]
            values = cells.melt(*new)
            for f in F2:
                edge[f, e, t.at, :] = new[f]
                tl[f, t.at, :] = values[f]

        tiles(1, part.shape[2], body)


class Sum:
    def __init__(self, one, other):
        self.one, self.other = one, other

    def __getitem__(self, key):
        return self.one[key] + self.other[key]


def nothing_kernel():
    pass


def edges_kernel(prm, part, low, high, ide, edge, tl0, tl7):
    edges_body(prm, "fine", part, low, high, ide, edge, tl0, tl7)


def edges_kernel_of_two(prm, part, low, high, low2, high2, ide, edge, tl0, tl7):
    edges_body(prm, "fine", part, Sum(low, low2), Sum(high, high2), ide, edge, tl0, tl7)


def coarse_edges_kernel(own, prm, part, low, high, ide, old, *refs):
    edge, tl0, tl7 = refs

    @pl.when(own[0] != 0)
    def _():
        edges_body(prm, "coarse", part, low, high, ide, edge, tl0, tl7)

    @pl.when(own[0] == 0)
    def _():
        edge[...] = old[...]


def base_kernel(prm, h, c, sm, sn, sx, ids, km, kn, kx):
    tab = Tables(prm)
    first = {"m": sm, "n": sn, "x": sx}
    outs = {"m": km, "n": kn, "x": kx}

    def body(name, i, r, t):
        ratio = Cells(tab, ids[r, t.at, :]).ratio()
        for f, u in enumerate((h[r, t.at, :], c[r, t.at, :])):
            outs[name][f, i, t.at, :] = u + ratio[f] * (first[name][f, i, t.at, :] - u)

    Parts(sm.shape[1]).each(h.shape[1], body)


def coarse_body(prm, arrived, base, old, ids, put, which, pad, edge_less):
    tab = Tables(prm)
    mid, ny = arrived["m"].shape[1], arrived["m"].shape[2]
    block = Parts(mid)
    clear_rims(pad)
    if edge_less:
        clear_ends(pad)

    def at(ref, i, t):
        return [ref[f, i, t.at, :] for f in F2]

    def melt(name, i, r, t):
        put_melt(tab, pad, r + 1, t, ids[r, t.at, :], *at(arrived[name], i, t))

    def update(name, i, r, t):
        new = coarse(tab, pad, r + 1, t, ids[r, t.at, :], at(arrived[name], i, t))
        end, start = at(old[name], i, t), at(base[name], i, t)
        for f in F2:
            put(name, f, i, r, t, new[f] + (end[f] - start[f]))

    if "m" in which:
        block.each(ny, melt, arrived)
    else:
        block.each(ny, melt, "nx")
        tiles(2, ny, lambda i, t: melt("m", i * (mid - 1), 2 + i * (mid - 1), t))
    block.each(ny, update, which)


def into(outs):
    def put(name, f, i, r, t, value):
        outs[name][f, i, t.at, :] = value

    return put


def coarse_mid_kernel(own, prm, am, an, km, ids, om, nm, pad):
    @pl.when(own[0] != 0)
    def _():
        coarse_body(
            prm, {"n": an, "m": am}, {"m": km}, {"m": om}, ids, into({"m": nm}), "m", pad, False
        )

    @pl.when(own[0] == 0)
    def _():
        nm[...] = om[...]


def coarse_rim_kernel(own, prm, am, an, ax, kn, kx, ids, on, ox, nn, part, pad):
    @pl.when(own[0] != 0)
    def _():
        coarse_body(
            prm,
            {"x": ax, "n": an, "m": am},
            {"n": kn, "x": kx},
            {"n": on, "x": ox},
            ids,
            into({"n": nn, "x": part}),
            "xn",
            pad,
            True,
        )

    @pl.when(own[0] == 0)
    def _():
        nn[...] = on[...]


def coarse_outer_kernel(
    own, prm, am, an, ax, low, high, kn, kx, ids, ide, on, ox, *refs
):
    rim, tl0, tl7, part, pad = refs[-5:]
    edge, beside = Rows(rim, 0), Rows(rim, 2)

    @pl.when(own[0] != 0)
    def _():
        coarse_body(
            prm,
            {"x": ax, "n": an, "m": am},
            {"n": kn, "x": kx},
            {"n": on, "x": ox},
            ids,
            into({"n": beside, "x": part}),
            "xn",
            pad,
            True,
        )
        edges_body(prm, "coarse", part, low, high, ide, edge, tl0, tl7)

    @pl.when(own[0] == 0)
    def _():
        for f in F2:
            for e in range(2):
                edge[f, e] = ox[f, e]
                beside[f, e] = on[f, e]


def last_rows_kernel(own, prm, am, ar, km, kn, kx, ids, om, rim, oh, oc, pad):
    out = (oh, oc)
    ax, an, ox, on = Rows(ar, 0), Rows(ar, 2), Rows(rim, 0), Rows(rim, 2)

    @pl.when(own[0] != 0)
    def _():
        def put(name, f, i, r, t, value):
            out[f][0, r, t.at, :] = value

        coarse_body(
            prm,
            {"x": ax, "n": an, "m": am},
            {"m": km, "n": kn, "x": kx},
            {"m": om, "n": on, "x": ox},
            ids,
            put,
            "mnx",
            pad,
            True,
        )

    @pl.when(own[0] == 0)
    def _():
        old = {"m": om, "n": on, "x": ox}

        def body(name, i, r, t):
            for f in F2:
                out[f][0, r, t.at, :] = old[name][f, i, t.at, :]

        Parts(om.shape[1]).each(om.shape[2], body)


def last_edges_kernel(own, prm, low, high, ide, oh, oc, nh, nc):
    first = pl.program_id(0) == 0

    @pl.when(own[0] != 0)
    def _():
        tab = Tables(prm)

        def body(i, t):
            rate = Cells(tab, ide[0, t.at, :]).coarse()
            for f, (old, new) in enumerate(((oh, nh), (oc, nc))):
                halo = jnp.where(first, low[f, t.at, :], high[f, t.at, :])
                new[0, 0, t.at, :] = old[0, 0, t.at, :] + rate[f] * halo

        tiles(1, ide.shape[1], body)

    @pl.when(own[0] == 0)
    def _():
        nh[...] = oh[...]
        nc[...] = oc[...]


def f32(*shape):
    return jax.ShapeDtypeStruct(shape, jnp.float32)


def i32(*shape):
    return jax.ShapeDtypeStruct(shape, jnp.int32)


TINY = pl.CostEstimate(flops=1000, bytes_accessed=1000, transcendentals=0)


def call(kernel, outs, args, smem, name, scratch=(), limit=8, after=(), through=(), flops=1000):
    after = (*after, *through)
    first = len(args) + len(after) - len(through)
    run = kernel
    if after:
        count = len(args)

        def run(*refs):
            kernel(*refs[:count], *refs[count + len(after) + len(through) :])

    return pl.pallas_call(
        run,
        out_shape=[f32(*x.shape) for x in through] + list(outs),
        in_specs=[SMEM] * smem + [VMEM] * (len(args) - smem) + [ANY] * len(after),
        out_specs=[ANY] * len(through) + [VMEM] * len(outs),
        input_output_aliases={first + i: i for i in range(len(through))},
        scratch_shapes=scratch,
        compiler_params=pltpu.CompilerParams(vmem_limit_bytes=limit * MIB),
        cost_estimate=pl.CostEstimate(flops=flops, bytes_accessed=1000, transcendentals=0),
        name=name,
    )(*args, *after)


def per_device(slices, parts, enthalpy, solute, material, phase_flag, *params):
    rows, ny, nz = material.shape
    mid = rows - 4
    h0 = enthalpy.reshape(rows, ny, nz)
    c0 = solute.reshape(rows, ny, nz)
    prm = jnp.concatenate(params)
    slot = lax.axis_index("tm")
    pair, tall = f32(2, 2, ny, nz), f32(2, mid, ny, nz)
    halo = f32(2, ny, nz)
    pad = [pltpu.VMEM((2, rows + 2, ny + 16, nz), jnp.float32)]

    def move(x, tms, up, by):
        pairs = [
            (t * parts + s, (t + up) * parts + s + by)
            for t in tms
            for s in range(parts)
            if 0 <= s + by < parts
        ]
        return lax.ppermute(x, ("tm", "space"), pairs)

    def halos(tl0, tl7, tms, up):
        return move(tl7, tms, up, 1), move(tl0, tms, up, -1)

    def send(x, n):
        return move(x, (n - 1,), 1, 0)

    def own(n):
        return (slot == n).astype(jnp.int32).reshape(1)

    def gridded(kernel, steps, outs, out_specs, in_specs, args, name, aliases={}):
        return pl.pallas_call(
            kernel,
            grid=(steps,),
            out_shape=outs,
            in_specs=in_specs,
            out_specs=out_specs,
            input_output_aliases=aliases,
            compiler_params=pltpu.CompilerParams(vmem_limit_bytes=8 * MIB),
            cost_estimate=TINY,
            name=name,
        )(*args)

    edge_row = pl.BlockSpec((1, ny, nz), lambda i: ((rows - 1) * i, 0, 0))
    whole = pl.BlockSpec((2, ny, nz), lambda i: (0, 0, 0))
    far = [pltpu.with_memory_space_constraint(x, pltpu.HBM) for x in (h0, c0, material)]
    tl0, tl7, later0, later7 = gridded(
        first_edges_kernel,
        2,
        [halo] * 4,
        [whole] * 4,
        [SMEM] + [edge_row] * 3,
        (prm, *far),
        "first_edges",
    )
    every = range(slices)
    even = halos(tl0, tl7, every[::2], 0)
    later0, later7, sm, sn, part, ids, ide = call(
        first_step_kernel,
        [tall, pair, pair, i32(rows, ny, nz), i32(2, ny, nz)],
        (prm, h0, c0, material, phase_flag),
        1,
        "first_step",
        pad,
        26,
        through=(later0, later7),
    )
    odd = halos(later0, later7, every[1::2], 0)
    even = call(nothing_kernel, [], (), 0, "even_arrived", through=even, flops=10**11)

    def fine_edges(part, sides, after=()):
        return call(
            edges_kernel if len(sides) == 2 else edges_kernel_of_two,
            [pair, halo, halo],
            (prm, part, *sides, ide),
            1,
            "edges",
            after=after,
        )

    base = ()
    sides = (*even, *odd)
    for k in range(STEPS - 1):
        sx, tl0, tl7 = fine_edges(part, sides, base)
        sides = halos(tl0, tl7, every, 0)
        if k == 0:
            base = call(
                base_kernel,
                [tall, pair, pair],
                (prm, h0, c0, sm, sn, sx, ids),
                1,
                "base",
                limit=16,
            )
        if k == STEPS - 3:
            *sm, sn, part = call(
                step_apart_kernel,
                [f32(mid, ny, nz)] * 2 + [pair, pair],
                (prm, sm, sn, sx, ids),
                1,
                "step_apart",
                pad,
                18,
            )
        elif k == STEPS - 2:
            last = (*sm, sn, sx)
            sm, sn, part = call(
                step_joined_kernel,
                [tall, pair, pair],
                (prm, *sm, sn, sx, ids),
                1,
                "step_joined",
                pad,
                18,
            )
        else:
            sm, sn, part = call(
                step_kernel, [tall, pair, pair], (prm, sm, sn, sx, ids), 1, "step", pad, 18
            )
    km, kn, kx = base

    am, an, vm = call(
        replay_kernel,
        [tall, pair, tall],
        (own(1), prm, *(send(x, 1) for x in last), ids, km, sm),
        2,
        "replay",
        pad,
        24,
    )
    vn = sn
    vx, tl0, tl7 = fine_edges(part, sides, (vm,))
    low, high = halos(tl0, tl7, (0,), 1)
    ax = send(vx, 1)
    vn, part = call(
        coarse_rim_kernel,
        [pair, pair],
        (own(1), prm, am, an, ax, kn, kx, ids, vn, vx),
        2,
        "coarse_rim",
        pad,
        20,
    )
    vx, tl0, tl7 = call(
        coarse_edges_kernel,
        [pair, halo, halo],
        (own(1), prm, part, low, high, ide, vx),
        2,
        "coarse_edges",
    )
    rim = None
    for n in range(2, slices):
        low, high = halos(tl0, tl7, (n - 1,), 1)
        am = send(vm, n)
        if n == 2:
            an, ax = send(vn, n), send(vx, n)
        else:
            ar = send(rim, n)
        if n == slices - 1:
            break
        vm = call(
            coarse_mid_kernel,
            [tall],
            (own(n), prm, am, an, km, ids, vm),
            2,
            "coarse_mid",
            pad,
            18,
        )[0]
        vm, rim, tl0, tl7 = call(
            coarse_outer_kernel,
            [f32(2, 4, ny, nz), halo, halo],
            (own(n), prm, am, an, ax, low, high, kn, kx, ids, ide, vn, vx),
            2,
            "coarse_outer",
            [pltpu.VMEM((2, 2, ny, nz), jnp.float32), *pad],
            26,
            through=(vm,),
        )

    out = f32(1, rows, ny, nz)
    last_own = own(slices - 1)
    oh, oc = call(
        last_rows_kernel,
        [out, out],
        (last_own, prm, am, ar, km, kn, kx, ids, vm, rim),
        2,
        "last_rows",
        pad,
        28,
    )
    out_row = pl.BlockSpec((1, 1, ny, nz), lambda i: (0, (rows - 1) * i, 0, 0))
    one = pl.BlockSpec((1, ny, nz), lambda i: (i, 0, 0))
    return tuple(
        gridded(
            last_edges_kernel,
            2,
            [out, out],
            [out_row] * 2,
            [SMEM, SMEM, whole, whole, one, out_row, out_row],
            (last_own, prm, low, high, ide, oh, oc),
            "last_edges",
            {5: 0, 6: 1},
        )
    )


def solution(mesh):
    body = functools.partial(per_device, mesh.shape["tm"], mesh.shape["space"])
    return jax.shard_map(
        body,
        mesh=mesh,
        in_specs=(
            P("tm", "space", None, None),
            P("tm", "space", None, None),
            P("space", None, None),
            P("space", None, None),
        )
        + (P(),) * 7,
        out_specs=(P("tm", "space", None, None), P("tm", "space", None, None)),
        check_vma=False,
    )
```

```python
import functools

import jax
import jax.numpy as jnp
from jax import lax
from jax.experimental import pallas as pl
from jax.experimental.pallas import tpu as pltpu
from jax.sharding import PartitionSpec as P

STEPS = 4
CHUNK = 256
MIB = 1024 * 1024
SMEM = pl.BlockSpec(memory_space=pltpu.SMEM)
VMEM = pl.BlockSpec(memory_space=pltpu.VMEM)
ANY = pl.BlockSpec(memory_space=pl.ANY)


class Tables:
    def __init__(self, prm):
        def raw(first, count):
            return [jnp.full((8, 128), prm[first + m], jnp.float32) for m in range(count)]

        cap, self.lat, self.hs = raw(0, 4), raw(4, 4), raw(8, 4)
        kp, bd, xr = raw(12, 4), raw(16, 4), raw(20, 4)
        self.sg = raw(24, 3)
        q = [(1.0 - k) / (1.0 + b) for k, b in zip(kp, bd)]
        self.icap = [1.0 / c for c in cap]
        self.den0 = [1.0 - v for v in q]
        self.den1 = [v / t for v, t in zip(q, self.lat)]
        self.hg = [x * c for x, c in zip(xr, cap)]
        self.gh = [4.0 / (1.0 + 18.0 * x) for x in xr]
        self.crh = [h * g for h, g in zip(self.hg, self.gh)]
        self.kp18 = [18.0 / k for k in kp]


class Cells:
    def __init__(self, tab, ids):
        self.tab, self.shape = tab, ids.shape
        self.b0 = (ids & 1) != 0
        self.b1 = (ids & 2) != 0
        self.p1 = (ids & 4) != 0
        self.p2 = (ids & 8) != 0

    def wide(self, tile):
        reps = self.shape[0] // 8
        return jnp.broadcast_to(tile[None], (reps, 8, 128)).reshape(self.shape)

    def alloy(self, name):
        t = [self.wide(v) for v in getattr(self.tab, name)]
        return jnp.where(self.b1, jnp.where(self.b0, t[3], t[2]), jnp.where(self.b0, t[1], t[0]))

    def solute_gain(self):
        t = [self.wide(v) for v in self.tab.sg]
        return jnp.where(self.p2, t[2], jnp.where(self.p1, t[1], t[0]))

    def fine(self):
        return self.alloy("hg"), self.solute_gain()

    def ratio(self):
        sg = self.solute_gain()
        return self.alloy("gh"), 4.0 / (1.0 + sg * self.alloy("kp18"))

    def coarse(self):
        sg = self.solute_gain()
        return self.alloy("crh"), 4.0 * sg / (1.0 + sg * self.alloy("kp18"))

    def melt(self, h, c):
        sensible = h - self.alloy("hs")
        held = jnp.minimum(jnp.maximum(sensible, 0.0), self.alloy("lat"))
        t = (h - held) * self.alloy("icap")
        return t, c / (self.alloy("den0") + self.alloy("den1") * held)


F2 = range(2)


class Fields:
    def __init__(self, *refs):
        self.refs = refs
        self.shape = (2,) + tuple(refs[0].shape)

    def __getitem__(self, key):
        return self.refs[key[0]][key[1:]]

    def __setitem__(self, key, value):
        self.refs[key[0]][key[1:]] = value


class Rows:
    def __init__(self, ref, first):
        self.ref, self.first = ref, first

    def key(self, key):
        return (key[0], key[1] + self.first, *key[2:])

    def __getitem__(self, key):
        return self.ref[self.key(key)]

    def __setitem__(self, key, value):
        self.ref[self.key(key)] = value


class Tile:
    def __init__(self, y, n):
        self.y, self.n = y, n
        self.at = pl.ds(y, n)

    def pad(self, by=0):
        return pl.ds(self.y + (8 + by), self.n)


def tiles(count, ny, body):
    n = CHUNK if ny % CHUNK == 0 else ny
    per = ny // n

    def run(k, carry):
        body(k // per, Tile(pl.multiple_of((k % per) * n, n), n))
        return carry

    lax.fori_loop(0, count * per, run, 0)


def clear_rims(pad):
    rows, long = pad.shape[1], pad.shape[2]
    for f in F2:
        for r in range(rows):
            pad[f, r, 0:8, :] = jnp.zeros((8, 128), jnp.float32)
            pad[f, r, long - 8 : long, :] = jnp.zeros((8, 128), jnp.float32)


def clear_ends(pad):
    def body(i, t):
        for f in F2:
            pad[f, i * (pad.shape[1] - 1), t.pad(), :] = jnp.zeros((t.n, 128), jnp.float32)

    tiles(2, pad.shape[2] - 16, body)


def put_melt(tab, pad, r, t, ids, h, c):
    values = Cells(tab, ids).melt(h, c)
    for f in F2:
        pad[f, r, t.pad(), :] = values[f]


def lap(pad, f, r, t):
    mid = pad[f, r, t.pad(), :]
    lane = lax.broadcasted_iota(jnp.int32, mid.shape, 1)
    total = pad[f, r, t.pad(-1), :] + pad[f, r, t.pad(1), :]
    total = total + jnp.where(lane == 0, 0.0, pltpu.roll(mid, 1, 1))
    total = total + jnp.where(lane == 127, 0.0, pltpu.roll(mid, 127, 1))
    return total - 6.0 * mid + pad[f, r - 1, t.pad(), :] + pad[f, r + 1, t.pad(), :]


def fine(tab, pad, r, t, ids, now):
    rate = Cells(tab, ids).fine()
    return [now[f] + rate[f] * lap(pad, f, r, t) for f in F2]


def coarse(tab, pad, r, t, ids, now):
    rate = Cells(tab, ids).coarse()
    return [now[f] + rate[f] * lap(pad, f, r, t) for f in F2]


class Parts:
    def __init__(self, mid):
        self.mid, self.rows = mid, mid + 4

    def each(self, ny, body, which="mnx"):
        if "x" in which:
            tiles(2, ny, lambda i, t: body("x", i, i * (self.rows - 1), t))
        if "n" in which:
            tiles(2, ny, lambda i, t: body("n", i, 1 + i * (self.rows - 3), t))
        if "m" in which:
            tiles(self.mid, ny, lambda i, t: body("m", i, i + 2, t))


def first_edges_kernel(prm, h, c, mat, tl0, tl7, later0, later7):
    tab = Tables(prm)
    side = pl.program_id(0)

    def body(i, t):
        values = Cells(tab, mat[0, t.at, :]).melt(h[0, t.at, :], c[0, t.at, :])

        @pl.when(side == 0)
        def _():
            for f in F2:
                tl0[f, t.at, :] = values[f]
                later0[f, t.at, :] = values[f]

        @pl.when(side == 1)
        def _():
            for f in F2:
                tl7[f, t.at, :] = values[f]
                later7[f, t.at, :] = values[f]

    tiles(1, h.shape[1], body)


def first_step_kernel(prm, h, c, mat, ph, sm, sn, part, ids, ide, pad):
    tab = Tables(prm)
    rows, ny = h.shape[0], h.shape[1]
    outs = {"m": sm, "n": sn, "x": part}
    clear_rims(pad)
    clear_ends(pad)

    def melt(r, t):
        cell = mat[r, t.at, :] + 4 * ph[r, t.at, :]
        ids[r, t.at, :] = cell
        put_melt(tab, pad, r + 1, t, cell, h[r, t.at, :], c[r, t.at, :])

    def update(part_name, i, r, t):
        new = fine(tab, pad, r + 1, t, ids[r, t.at, :], (h[r, t.at, :], c[r, t.at, :]))
        for f in F2:
            outs[part_name][f, i, t.at, :] = new[f]

    tiles(rows, ny, melt)
    ide[0] = ids[0]
    ide[1] = ids[rows - 1]
    Parts(rows - 4).each(ny, update)


def step_body(prm, sm, sn, sx, ids, outs, pad):
    tab = Tables(prm)
    ny = sm.shape[2]
    now = {"m": sm, "n": sn, "x": sx}
    block = Parts(sm.shape[1])
    clear_rims(pad)
    clear_ends(pad)

    def at(name, i, t):
        return [now[name][f, i, t.at, :] for f in F2]

    def melt(name, i, r, t):
        put_melt(tab, pad, r + 1, t, ids[r, t.at, :], *at(name, i, t))

    def update(name, i, r, t):
        new = fine(tab, pad, r + 1, t, ids[r, t.at, :], at(name, i, t))
        for f in F2:
            outs[name][f, i, t.at, :] = new[f]

    block.each(ny, melt)
    block.each(ny, update, outs)


def step_kernel(prm, sm, sn, sx, ids, nm, nn, part, pad):
    step_body(prm, sm, sn, sx, ids, {"x": part, "n": nn, "m": nm}, pad)


def step_apart_kernel(prm, sm, sn, sx, ids, mh, mc, nn, part, pad):
    step_body(prm, sm, sn, sx, ids, {"x": part, "n": nn, "m": Fields(mh, mc)}, pad)


def step_joined_kernel(prm, mh, mc, sn, sx, ids, nm, nn, part, pad):
    step_body(prm, Fields(mh, mc), sn, sx, ids, {"x": part, "n": nn, "m": nm}, pad)


def replay_kernel(own, prm, mh, mc, sn, sx, ids, km, om, am, an, nm, pad):
    @pl.when(own[0] != 0)
    def _():
        step_body(prm, Fields(mh, mc), sn, sx, ids, {"n": an, "m": am}, pad)
        coarse_body(
            prm, {"n": an, "m": am}, {"m": km}, {"m": om}, ids, into({"m": nm}), "m", pad, False
        )

    @pl.when(own[0] == 0)
    def _():
        nm[...] = om[...]


def edges_body(prm, gains, part, low, high, ide, edge, tl0, tl7):
    tab = Tables(prm)
    for e, (halo, tl) in enumerate(((low, tl0), (high, tl7))):

        def body(i, t, e=e, halo=halo, tl=tl):
            cells = Cells(tab, ide[e, t.at, :])
            rate = getattr(cells, gains)()
            new = [part[f, e, t.at, :] + rate[f] * halo[f, t.at, :] for f in F2]
            values = cells.melt(*new)
            for f in F2:
                edge[f, e, t.at, :] = new[f]
                tl[f, t.at, :] = values[f]

        tiles(1, part.shape[2], body)


class Sum:
    def __init__(self, one, other):
        self.one, self.other = one, other

    def __getitem__(self, key):
        return self.one[key] + self.other[key]


def nothing_kernel():
    pass


def edges_kernel(prm, part, low, high, ide, edge, tl0, tl7):
    edges_body(prm, "fine", part, low, high, ide, edge, tl0, tl7)


def edges_kernel_of_two(prm, part, low, high, low2, high2, ide, edge, tl0, tl7):
    edges_body(prm, "fine", part, Sum(low, low2), Sum(high, high2), ide, edge, tl0, tl7)


def coarse_edges_kernel(own, prm, part, low, high, ide, old, *refs):
    edge, tl0, tl7 = refs

    @pl.when(own[0] != 0)
    def _():
        edges_body(prm, "coarse", part, low, high, ide, edge, tl0, tl7)

    @pl.when(own[0] == 0)
    def _():
        edge[...] = old[...]


def base_kernel(prm, h, c, sm, sn, sx, ids, km, kn, kx):
    tab = Tables(prm)
    first = {"m": sm, "n": sn, "x": sx}
    outs = {"m": km, "n": kn, "x": kx}

    def body(name, i, r, t):
        ratio = Cells(tab, ids[r, t.at, :]).ratio()
        for f, u in enumerate((h[r, t.at, :], c[r, t.at, :])):
            outs[name][f, i, t.at, :] = u + ratio[f] * (first[name][f, i, t.at, :] - u)

    Parts(sm.shape[1]).each(h.shape[1], body)


def coarse_body(prm, arrived, base, old, ids, put, which, pad, edge_less):
    tab = Tables(prm)
    mid, ny = arrived["m"].shape[1], arrived["m"].shape[2]
    block = Parts(mid)
    clear_rims(pad)
    if edge_less:
        clear_ends(pad)

    def at(ref, i, t):
        return [ref[f, i, t.at, :] for f in F2]

    def melt(name, i, r, t):
        put_melt(tab, pad, r + 1, t, ids[r, t.at, :], *at(arrived[name], i, t))

    def update(name, i, r, t):
        new = coarse(tab, pad, r + 1, t, ids[r, t.at, :], at(arrived[name], i, t))
        change = at(old[name], i, t)
        if base is not None:
            change = [v - w for v, w in zip(change, at(base[name], i, t))]
        for f in F2:
            put(name, f, i, r, t, new[f] + change[f])

    if "m" in which:
        block.each(ny, melt, arrived)
    else:
        block.each(ny, melt, "nx")
        tiles(2, ny, lambda i, t: melt("m", i * (mid - 1), 2 + i * (mid - 1), t))
    block.each(ny, update, which)


def into(outs):
    def put(name, f, i, r, t, value):
        outs[name][f, i, t.at, :] = value

    return put


def coarse_mid_kernel(own, prm, am, an, km, ids, om, nm, pad):
    @pl.when(own[0] != 0)
    def _():
        coarse_body(
            prm, {"n": an, "m": am}, {"m": km}, {"m": om}, ids, into({"m": nm}), "m", pad, False
        )

    @pl.when(own[0] == 0)
    def _():
        nm[...] = om[...]


def coarse_rim_kernel(own, prm, am, an, ax, kn, kx, ids, on, ox, nn, part, pad):
    @pl.when(own[0] != 0)
    def _():
        coarse_body(
            prm,
            {"x": ax, "n": an, "m": am},
            {"n": kn, "x": kx},
            {"n": on, "x": ox},
            ids,
            into({"n": nn, "x": part}),
            "xn",
            pad,
            True,
        )

    @pl.when(own[0] == 0)
    def _():
        nn[...] = on[...]


def drift_kernel(prm, on, ox, kn, kx, d):
    def body(i, t):
        for f in F2:
            d[f, i, t.at, :] = ox[f, i, t.at, :] - kx[f, i, t.at, :]
            d[f, 2 + i, t.at, :] = on[f, i, t.at, :] - kn[f, i, t.at, :]

    tiles(2, on.shape[2], body)


def next_rim_kernel(own, prm, vm, vn, vx, d, ids, nn, part, pad):
    @pl.when(own[0] != 0)
    def _():
        coarse_body(
            prm,
            {"x": vx, "n": vn, "m": vm},
            None,
            {"n": Rows(d, 2), "x": Rows(d, 0)},
            ids,
            into({"n": nn, "x": part}),
            "xn",
            pad,
            True,
        )


def next_edges_kernel(own, prm, part, low, high, ide, edge, tl0, tl7):
    @pl.when(own[0] != 0)
    def _():
        edges_body(prm, "coarse", part, low, high, ide, edge, tl0, tl7)


def last_mid_kernel(own, prm, am, an, km, ids, om, oh, oc, pad):
    out = (oh, oc)

    @pl.when(own[0] != 0)
    def _():
        def put(name, f, i, r, t, value):
            out[f][0, r, t.at, :] = value

        coarse_body(prm, {"n": an, "m": am}, {"m": km}, {"m": om}, ids, put, "m", pad, False)

    @pl.when(own[0] == 0)
    def _():
        def body(i, t):
            for f in F2:
                out[f][0, i + 2, t.at, :] = om[f, i, t.at, :]

        tiles(om.shape[1], om.shape[2], body)


def last_outer_kernel(
    role, prm, am, an, ax, low, high, kn, kx, on, ox, gn, gx, idm, idn, idx, oh, oc, nh, nc, pad
):
    e = pl.program_id(0)
    ny = ax.shape[2]
    out = (nh, nc)

    @pl.when(role[0] == 2)
    def _():
        tab = Tables(prm)
        clear_rims(pad)
        first = e == 0

        def zero(i, t):
            for f in F2:
                pad[f, 0, t.pad(), :] = jnp.zeros((t.n, 128), jnp.float32)

        tiles(1, ny, zero)
        for k, (now, ids) in enumerate(((ax, idx), (an, idn), (am, idm))):

            def melt(i, t, k=k, now=now, ids=ids):
                values = [now[f, 0, t.at, :] for f in F2]
                put_melt(tab, pad, k + 1, t, ids[0, t.at, :], *values)

            tiles(1, ny, melt)
        for k, (now, ids, end, start) in enumerate(((ax, idx, ox, kx), (an, idn, on, kn))):

            def update(i, t, k=k, now=now, ids=ids, end=end, start=start):
                rate = Cells(tab, ids[0, t.at, :]).coarse()
                for f in F2:
                    total = lap(pad, f, k + 1, t)
                    if k == 0:
                        total = total + jnp.where(first, low[f, t.at, :], high[f, t.at, :])
                    new = now[f, 0, t.at, :] + rate[f] * total
                    new = new + (end[f, 0, t.at, :] - start[f, 0, t.at, :])
                    out[f][0, e if k == 0 else 1 - e, t.at, :] = new

            tiles(1, ny, update)

    def keep(n, x):
        for f in F2:
            out[f][0, e] = x[f, 0]
            out[f][0, 1 - e] = n[f, 0]

    @pl.when(role[0] == 1)
    def _():
        keep(gn, gx)

    @pl.when(role[0] == 0)
    def _():
        keep(on, ox)


def f32(*shape):
    return jax.ShapeDtypeStruct(shape, jnp.float32)


def i32(*shape):
    return jax.ShapeDtypeStruct(shape, jnp.int32)


TINY = pl.CostEstimate(flops=1000, bytes_accessed=1000, transcendentals=0)


def call(kernel, outs, args, smem, name, scratch=(), limit=8, after=(), through=(), flops=1000):
    after = (*after, *through)
    first = len(args) + len(after) - len(through)
    run = kernel
    if after:
        count = len(args)

        def run(*refs):
            kernel(*refs[:count], *refs[count + len(after) + len(through) :])

    return pl.pallas_call(
        run,
        out_shape=[f32(*x.shape) for x in through] + list(outs),
        in_specs=[SMEM] * smem + [VMEM] * (len(args) - smem) + [ANY] * len(after),
        out_specs=[ANY] * len(through) + [VMEM] * len(outs),
        input_output_aliases={first + i: i for i in range(len(through))},
        scratch_shapes=scratch,
        compiler_params=pltpu.CompilerParams(vmem_limit_bytes=limit * MIB),
        cost_estimate=pl.CostEstimate(flops=flops, bytes_accessed=1000, transcendentals=0),
        name=name,
    )(*args, *after)


def per_device(slices, parts, enthalpy, solute, material, phase_flag, *params):
    rows, ny, nz = material.shape
    mid = rows - 4
    h0 = enthalpy.reshape(rows, ny, nz)
    c0 = solute.reshape(rows, ny, nz)
    prm = jnp.concatenate(params)
    slot = lax.axis_index("tm")
    pair, tall = f32(2, 2, ny, nz), f32(2, mid, ny, nz)
    halo = f32(2, ny, nz)
    pad = [pltpu.VMEM((2, rows + 2, ny + 16, nz), jnp.float32)]

    def move(x, tms, up, by):
        pairs = [
            (t * parts + s, (t + up) * parts + s + by)
            for t in tms
            for s in range(parts)
            if 0 <= s + by < parts
        ]
        return lax.ppermute(x, ("tm", "space"), pairs)

    def halos(tl0, tl7, tms, up):
        return move(tl7, tms, up, 1), move(tl0, tms, up, -1)

    def send(x, n):
        return move(x, (n - 1,), 1, 0)

    def own(n):
        return (slot == n).astype(jnp.int32).reshape(1)

    def gridded(kernel, steps, outs, out_specs, in_specs, args, name, aliases={}):
        return pl.pallas_call(
            kernel,
            grid=(steps,),
            out_shape=outs,
            in_specs=in_specs,
            out_specs=out_specs,
            input_output_aliases=aliases,
            compiler_params=pltpu.CompilerParams(vmem_limit_bytes=8 * MIB),
            cost_estimate=TINY,
            name=name,
        )(*args)

    edge_row = pl.BlockSpec((1, ny, nz), lambda i: ((rows - 1) * i, 0, 0))
    whole = pl.BlockSpec((2, ny, nz), lambda i: (0, 0, 0))
    far = [pltpu.with_memory_space_constraint(x, pltpu.HBM) for x in (h0, c0, material)]
    tl0, tl7, later0, later7 = gridded(
        first_edges_kernel,
        2,
        [halo] * 4,
        [whole] * 4,
        [SMEM] + [edge_row] * 3,
        (prm, *far),
        "first_edges",
    )
    every = range(slices)
    even = halos(tl0, tl7, every[::2], 0)
    later0, later7, sm, sn, part, ids, ide = call(
        first_step_kernel,
        [tall, pair, pair, i32(rows, ny, nz), i32(2, ny, nz)],
        (prm, h0, c0, material, phase_flag),
        1,
        "first_step",
        pad,
        26,
        through=(later0, later7),
    )
    odd = halos(later0, later7, every[1::2], 0)
    even = call(nothing_kernel, [], (), 0, "even_arrived", through=even, flops=10**11)

    def fine_edges(part, sides, after=()):
        return call(
            edges_kernel if len(sides) == 2 else edges_kernel_of_two,
            [pair, halo, halo],
            (prm, part, *sides, ide),
            1,
            "edges",
            after=after,
        )

    base = ()
    sides = (*even, *odd)
    for k in range(STEPS - 1):
        sx, tl0, tl7 = fine_edges(part, sides, base)
        sides = halos(tl0, tl7, every, 0)
        if k == 0:
            base = call(
                base_kernel,
                [tall, pair, pair],
                (prm, h0, c0, sm, sn, sx, ids),
                1,
                "base",
                limit=16,
            )
        if k == STEPS - 3:
            *sm, sn, part = call(
                step_apart_kernel,
                [f32(mid, ny, nz)] * 2 + [pair, pair],
                (prm, sm, sn, sx, ids),
                1,
                "step_apart",
                pad,
                18,
            )
        elif k == STEPS - 2:
            last = (*sm, sn, sx)
            sm, sn, part = call(
                step_joined_kernel,
                [tall, pair, pair],
                (prm, *sm, sn, sx, ids),
                1,
                "step_joined",
                pad,
                18,
            )
        else:
            sm, sn, part = call(
                step_kernel, [tall, pair, pair], (prm, sm, sn, sx, ids), 1, "step", pad, 18
            )
    km, kn, kx = base

    am, an, vm = call(
        replay_kernel,
        [tall, pair, tall],
        (own(1), prm, *(send(x, 1) for x in last), ids, km, sm),
        2,
        "replay",
        pad,
        24,
    )
    vn = sn
    vx, tl0, tl7 = fine_edges(part, sides, (vm,))
    low, high = halos(tl0, tl7, (0,), 1)
    ax = send(vx, 1)
    d = move(
        call(drift_kernel, [f32(2, 4, ny, nz)], (prm, vn, vx, kn, kx), 1, "drift", limit=12)[0],
        (2,),
        -1,
        0,
    )
    vn, part = call(
        coarse_rim_kernel,
        [pair, pair],
        (own(1), prm, am, an, ax, kn, kx, ids, vn, vx),
        2,
        "coarse_rim",
        pad,
        20,
    )
    vx, tl0, tl7 = call(
        coarse_edges_kernel,
        [pair, halo, halo],
        (own(1), prm, part, low, high, ide, vx),
        2,
        "coarse_edges",
    )
    vn0, vx0 = vn, vx
    am, an = send(vm, 2), send(vn, 2)

    low, high = halos(tl0, tl7, (1,), 0)
    n2, part = call(
        next_rim_kernel,
        [pair, pair],
        (own(1), prm, vm, vn, vx, d, ids),
        2,
        "next_rim",
        pad,
        20,
    )
    x2, tl0, tl7 = call(
        next_edges_kernel,
        [pair, halo, halo],
        (own(1), prm, part, low, high, ide),
        2,
        "next_edges",
    )
    vm = call(
        coarse_mid_kernel,
        [tall],
        (own(2), prm, am, an, km, ids, vm),
        2,
        "coarse_mid",
        pad,
        18,
        after=(x2,),
    )[0]
    low, high = halos(tl0, tl7, (1,), 2)
    ax, an, am = move(x2, (1,), 2, 0), move(n2, (1,), 2, 0), send(vm, 3)

    out = f32(1, rows, ny, nz)
    oh, oc = call(
        last_mid_kernel,
        [out, out],
        (own(3), prm, am, an, km, ids, vm),
        2,
        "last_mid",
        pad,
        24,
    )
    far_oh = pltpu.with_memory_space_constraint(oh, pltpu.HBM)
    low, high = call(
        nothing_kernel, [], (), 0, "last_arrived", after=(far_oh,), through=(low, high), flops=10**11
    )
    gx, gn = move(ax, (3,), -1, 0), move(an, (3,), -1, 0)
    outer = pl.BlockSpec((1, 2, ny, nz), lambda i: (0, (rows // 2 - 1) * i, 0, 0))
    side = pl.BlockSpec((2, 1, ny, nz), lambda i: (0, i, 0, 0))
    inside = pl.BlockSpec((2, 1, ny, nz), lambda i: (0, (mid - 1) * i, 0, 0))

    def id_row(k):
        return pl.BlockSpec((1, ny, nz), lambda i: (k + (rows - 1 - 2 * k) * i, 0, 0))

    role = jnp.where(slot == 3, 2, jnp.where(slot == 2, 1, 0)).astype(jnp.int32).reshape(1)
    return tuple(
        pl.pallas_call(
            last_outer_kernel,
            grid=(2,),
            out_shape=[out, out],
            in_specs=[SMEM, SMEM, inside, side, side, whole, whole]
            + [side] * 6
            + [id_row(2), id_row(1), id_row(0), ANY, ANY],
            out_specs=[outer] * 2,
            scratch_shapes=[pltpu.VMEM((2, 5, ny + 16, nz), jnp.float32)],
            input_output_aliases={16: 0, 17: 1},
            compiler_params=pltpu.CompilerParams(vmem_limit_bytes=26 * MIB),
            cost_estimate=TINY,
            name="last_outer",
        )(role, prm, am, an, ax, low, high, kn, kx, vn0, vx0, gn, gx, ids, ids, ids, oh, oc)
    )


def solution(mesh):
    body = functools.partial(per_device, mesh.shape["tm"], mesh.shape["space"])
    return jax.shard_map(
        body,
        mesh=mesh,
        in_specs=(
            P("tm", "space", None, None),
            P("tm", "space", None, None),
            P("space", None, None),
            P("space", None, None),
        )
        + (P(),) * 7,
        out_specs=(P("tm", "space", None, None), P("tm", "space", None, None)),
        check_vma=False,
    )
```

```python
import functools

import jax
import jax.numpy as jnp
from jax import lax
from jax.experimental import pallas as pl
from jax.experimental.pallas import tpu as pltpu
from jax.sharding import PartitionSpec as P

STEPS = 4
TILE = [256]
MIB = 1024 * 1024
SMEM = pl.BlockSpec(memory_space=pltpu.SMEM)
VMEM = pl.BlockSpec(memory_space=pltpu.VMEM)
ANY = pl.BlockSpec(memory_space=pl.ANY)


class Tables:
    def __init__(self, prm):
        def raw(first, count):
            return [jnp.full((8, 128), prm[first + m], jnp.float32) for m in range(count)]

        cap, self.lat, self.hs = raw(0, 4), raw(4, 4), raw(8, 4)
        kp, bd, xr = raw(12, 4), raw(16, 4), raw(20, 4)
        self.sg = raw(24, 3)
        q = [(1.0 - k) / (1.0 + b) for k, b in zip(kp, bd)]
        self.icap = [1.0 / c for c in cap]
        self.den0 = [1.0 - v for v in q]
        self.den1 = [v / t for v, t in zip(q, self.lat)]
        self.hg = [x * c for x, c in zip(xr, cap)]
        self.gh = [4.0 / (1.0 + 18.0 * x) for x in xr]
        self.crh = [h * g for h, g in zip(self.hg, self.gh)]
        self.kp18 = [18.0 / k for k in kp]


class Cells:
    def __init__(self, tab, ids):
        self.tab, self.shape = tab, ids.shape
        self.b0 = (ids & 1) != 0
        self.b1 = (ids & 2) != 0
        self.p1 = (ids & 4) != 0
        self.p2 = (ids & 8) != 0

    def wide(self, tile):
        reps = self.shape[0] // 8
        return jnp.broadcast_to(tile[None], (reps, 8, 128)).reshape(self.shape)

    def alloy(self, name):
        t = [self.wide(v) for v in getattr(self.tab, name)]
        return jnp.where(self.b1, jnp.where(self.b0, t[3], t[2]), jnp.where(self.b0, t[1], t[0]))

    def solute_gain(self):
        t = [self.wide(v) for v in self.tab.sg]
        return jnp.where(self.p2, t[2], jnp.where(self.p1, t[1], t[0]))

    def fine(self):
        return self.alloy("hg"), self.solute_gain()

    def ratio(self):
        sg = self.solute_gain()
        return self.alloy("gh"), 4.0 / (1.0 + sg * self.alloy("kp18"))

    def coarse(self):
        sg = self.solute_gain()
        return self.alloy("crh"), 4.0 * sg / (1.0 + sg * self.alloy("kp18"))

    def melt(self, h, c):
        sensible = h - self.alloy("hs")
        held = jnp.minimum(jnp.maximum(sensible, 0.0), self.alloy("lat"))
        t = (h - held) * self.alloy("icap")
        return t, c / (self.alloy("den0") + self.alloy("den1") * held)


F2 = range(2)


class Fields:
    def __init__(self, *refs):
        self.refs = refs
        self.shape = (2,) + tuple(refs[0].shape)

    def __getitem__(self, key):
        return self.refs[key[0]][key[1:]]

    def __setitem__(self, key, value):
        self.refs[key[0]][key[1:]] = value


class Rows:
    def __init__(self, ref, first, by=1):
        self.ref, self.first, self.by = ref, first, by

    def key(self, key):
        return (key[0], self.first + self.by * key[1], *key[2:])

    def __getitem__(self, key):
        return self.ref[self.key(key)]

    def __setitem__(self, key, value):
        self.ref[self.key(key)] = value


class Tile:
    def __init__(self, y, n):
        self.y, self.n = y, n
        self.at = pl.ds(y, n)

    def pad(self, by=0):
        return pl.ds(self.y + (8 + by), self.n)


def tiles(count, ny, body):
    n = TILE[-1] if ny % TILE[-1] == 0 else ny
    per = ny // n

    def run(k, carry):
        body(k // per, Tile(pl.multiple_of((k % per) * n, n), n))
        return carry

    lax.fori_loop(0, count * per, run, 0)


def clear_rims(pad):
    rows, long = pad.shape[1], pad.shape[2]
    for f in F2:
        for r in range(rows):
            pad[f, r, 0:8, :] = jnp.zeros((8, 128), jnp.float32)
            pad[f, r, long - 8 : long, :] = jnp.zeros((8, 128), jnp.float32)


def clear_ends(pad):
    def body(i, t):
        for f in F2:
            pad[f, i * (pad.shape[1] - 1), t.pad(), :] = jnp.zeros((t.n, 128), jnp.float32)

    tiles(2, pad.shape[2] - 16, body)


def put_melt(tab, pad, r, t, ids, h, c):
    values = Cells(tab, ids).melt(h, c)
    for f in F2:
        pad[f, r, t.pad(), :] = values[f]


def lap(pad, f, r, t):
    mid = pad[f, r, t.pad(), :]
    lane = lax.broadcasted_iota(jnp.int32, mid.shape, 1)
    total = pad[f, r, t.pad(-1), :] + pad[f, r, t.pad(1), :]
    total = total + jnp.where(lane == 0, 0.0, pltpu.roll(mid, 1, 1))
    total = total + jnp.where(lane == 127, 0.0, pltpu.roll(mid, 127, 1))
    return total - 6.0 * mid + pad[f, r - 1, t.pad(), :] + pad[f, r + 1, t.pad(), :]


def fine(tab, pad, r, t, ids, now):
    rate = Cells(tab, ids).fine()
    return [now[f] + rate[f] * lap(pad, f, r, t) for f in F2]


def coarse(tab, pad, r, t, ids, now):
    rate = Cells(tab, ids).coarse()
    return [now[f] + rate[f] * lap(pad, f, r, t) for f in F2]


class Parts:
    def __init__(self, mid):
        self.mid, self.rows = mid, mid + 4

    def each(self, ny, body, which="mnx"):
        if "x" in which:
            tiles(2, ny, lambda i, t: body("x", i, i * (self.rows - 1), t))
        if "n" in which:
            tiles(2, ny, lambda i, t: body("n", i, 1 + i * (self.rows - 3), t))
        if "m" in which:
            tiles(self.mid, ny, lambda i, t: body("m", i, i + 2, t))


def first_edges_kernel(prm, h, c, mat, tl0, tl7, later0, later7):
    tab = Tables(prm)
    side = pl.program_id(0)

    def body(i, t):
        values = Cells(tab, mat[0, t.at, :]).melt(h[0, t.at, :], c[0, t.at, :])

        @pl.when(side == 0)
        def _():
            for f in F2:
                tl0[f, t.at, :] = values[f]
                later0[f, t.at, :] = values[f]

        @pl.when(side == 1)
        def _():
            for f in F2:
                tl7[f, t.at, :] = values[f]
                later7[f, t.at, :] = values[f]

    tiles(1, h.shape[1], body)


def first_step_kernel(prm, h, c, mat, ph, sm, sn, part, ids, ide, pad):
    tab = Tables(prm)
    rows, ny = h.shape[0], h.shape[1]
    outs = {"m": sm, "n": sn, "x": part}
    clear_rims(pad)
    clear_ends(pad)

    def melt(r, t):
        cell = mat[r, t.at, :] + 4 * ph[r, t.at, :]
        ids[r, t.at, :] = cell
        put_melt(tab, pad, r + 1, t, cell, h[r, t.at, :], c[r, t.at, :])

    def update(part_name, i, r, t):
        new = fine(tab, pad, r + 1, t, ids[r, t.at, :], (h[r, t.at, :], c[r, t.at, :]))
        for f in F2:
            outs[part_name][f, i, t.at, :] = new[f]

    tiles(rows, ny, melt)
    ide[0] = ids[0]
    ide[1] = ids[rows - 1]
    Parts(rows - 4).each(ny, update)


def step_body(prm, sm, sn, sx, ids, outs, pad):
    tab = Tables(prm)
    ny = sm.shape[2]
    now = {"m": sm, "n": sn, "x": sx}
    block = Parts(sm.shape[1])
    clear_rims(pad)
    clear_ends(pad)

    def at(name, i, t):
        return [now[name][f, i, t.at, :] for f in F2]

    def melt(name, i, r, t):
        put_melt(tab, pad, r + 1, t, ids[r, t.at, :], *at(name, i, t))

    def update(name, i, r, t):
        new = fine(tab, pad, r + 1, t, ids[r, t.at, :], at(name, i, t))
        for f in F2:
            outs[name][f, i, t.at, :] = new[f]

    block.each(ny, melt)
    block.each(ny, update, outs)


def step_kernel(prm, sm, sn, sx, ids, nm, nn, part, pad):
    step_body(prm, sm, sn, sx, ids, {"x": part, "n": nn, "m": nm}, pad)


def step_apart_kernel(prm, sm, sn, sx, ids, mh, mc, nn, part, pad):
    step_body(prm, sm, sn, sx, ids, {"x": part, "n": nn, "m": Fields(mh, mc)}, pad)


def step_joined_kernel(prm, mh, mc, sn, sx, ids, nm, nn, part, pad):
    step_body(prm, Fields(mh, mc), sn, sx, ids, {"x": part, "n": nn, "m": nm}, pad)


def replay_kernel(own, prm, mh, mc, sn, sx, ids, km, om, am, an, nm, pad):
    @pl.when(own[0] != 0)
    def _():
        step_body(prm, Fields(mh, mc), sn, sx, ids, {"n": an, "m": am}, pad)
        coarse_body(
            prm, {"n": an, "m": am}, {"m": km}, {"m": om}, ids, into({"m": nm}), "m", pad, False
        )

    @pl.when(own[0] == 0)
    def _():
        nm[...] = om[...]


def edges_body(prm, gains, part, low, high, ide, edge, tl0, tl7):
    tab = Tables(prm)
    for e, (halo, tl) in enumerate(((low, tl0), (high, tl7))):

        def body(i, t, e=e, halo=halo, tl=tl):
            cells = Cells(tab, ide[e, t.at, :])
            rate = getattr(cells, gains)()
            new = [part[f, e, t.at, :] + rate[f] * halo[f, t.at, :] for f in F2]
            values = cells.melt(*new)
            for f in F2:
                edge[f, e, t.at, :] = new[f]
                tl[f, t.at, :] = values[f]

        tiles(1, part.shape[2], body)


class Sum:
    def __init__(self, one, other):
        self.one, self.other = one, other

    def __getitem__(self, key):
        return self.one[key] + self.other[key]


def nothing_kernel():
    pass


def edges_kernel(prm, part, low, high, ide, edge, tl0, tl7):
    edges_body(prm, "fine", part, low, high, ide, edge, tl0, tl7)


def edges_kernel_of_two(prm, part, low, high, low2, high2, ide, edge, tl0, tl7):
    edges_body(prm, "fine", part, Sum(low, low2), Sum(high, high2), ide, edge, tl0, tl7)


def coarse_edges_kernel(own, prm, part, low, high, ide, old, *refs):
    edge, tl0, tl7 = refs

    @pl.when(own[0] != 0)
    def _():
        edges_body(prm, "coarse", part, low, high, ide, edge, tl0, tl7)

    @pl.when(own[0] == 0)
    def _():
        edge[...] = old[...]


def base_kernel(prm, h, c, sm, sn, sx, ids, km, kn, kx):
    tab = Tables(prm)
    first = {"m": sm, "n": sn, "x": sx}
    outs = {"m": km, "n": kn, "x": kx}

    def body(name, i, r, t):
        ratio = Cells(tab, ids[r, t.at, :]).ratio()
        for f, u in enumerate((h[r, t.at, :], c[r, t.at, :])):
            outs[name][f, i, t.at, :] = u + ratio[f] * (first[name][f, i, t.at, :] - u)

    Parts(sm.shape[1]).each(h.shape[1], body)


def coarse_body(prm, arrived, base, old, ids, put, which, pad, edge_less):
    tab = Tables(prm)
    mid, ny = arrived["m"].shape[1], arrived["m"].shape[2]
    block = Parts(mid)
    clear_rims(pad)
    if edge_less:
        clear_ends(pad)

    def at(ref, i, t):
        return [ref[f, i, t.at, :] for f in F2]

    def melt(name, i, r, t):
        put_melt(tab, pad, r + 1, t, ids[r, t.at, :], *at(arrived[name], i, t))

    def update(name, i, r, t):
        new = coarse(tab, pad, r + 1, t, ids[r, t.at, :], at(arrived[name], i, t))
        end, start = at(old[name], i, t), at(base[name], i, t)
        for f in F2:
            put(name, f, i, r, t, new[f] + (end[f] - start[f]))

    if "m" in which:
        block.each(ny, melt, arrived)
    else:
        block.each(ny, melt, "nx")
        tiles(2, ny, lambda i, t: melt("m", i * (mid - 1), 2 + i * (mid - 1), t))
    block.each(ny, update, which)


def into(outs):
    def put(name, f, i, r, t, value):
        outs[name][f, i, t.at, :] = value

    return put


def coarse_mid_kernel(own, prm, am, an, km, ids, om, nm, pad):
    @pl.when(own[0] != 0)
    def _():
        coarse_body(
            prm, {"n": an, "m": am}, {"m": km}, {"m": om}, ids, into({"m": nm}), "m", pad, False
        )

    @pl.when(own[0] == 0)
    def _():
        nm[...] = om[...]


def coarse_rim_kernel(own, prm, am, an, ax, kn, kx, ids, on, ox, nn, part, pad):
    @pl.when(own[0] != 0)
    def _():
        coarse_body(
            prm,
            {"x": ax, "n": an, "m": am},
            {"n": kn, "x": kx},
            {"n": on, "x": ox},
            ids,
            into({"n": nn, "x": part}),
            "xn",
            pad,
            True,
        )

    @pl.when(own[0] == 0)
    def _():
        nn[...] = on[...]


def coarse_outer_kernel(own, prm, am, an, ax, low, high, kn, kx, on, ox, idm, idn, idx, *refs):
    rim, tl0, tl7, pad = refs[-4:]
    e = pl.program_id(0)
    ny = ax.shape[2]

    @pl.when(own[0] != 0)
    def _():
        tab = Tables(prm)
        clear_rims(pad)

        def zero(i, t):
            for f in F2:
                pad[f, 0, t.pad(), :] = jnp.zeros((t.n, 128), jnp.float32)

        tiles(1, ny, zero)
        for k, (now, ids) in enumerate(((ax, idx), (an, idn), (am, idm))):

            def melt(i, t, k=k, now=now, ids=ids):
                values = [now[f, 0, t.at, :] for f in F2]
                put_melt(tab, pad, k + 1, t, ids[0, t.at, :], *values)

            tiles(1, ny, melt)
        for k, (now, ids, end, start) in enumerate(((ax, idx, ox, kx), (an, idn, on, kn))):

            def update(i, t, k=k, now=now, ids=ids, end=end, start=start):
                cells = Cells(tab, ids[0, t.at, :])
                rate = cells.coarse()
                new = []
                for f in F2:
                    total = lap(pad, f, k + 1, t)
                    if k == 0:
                        total = total + jnp.where(e == 0, low[f, t.at, :], high[f, t.at, :])
                    value = now[f, 0, t.at, :] + rate[f] * total
                    new.append(value + (end[f, 0, t.at, :] - start[f, 0, t.at, :]))
                    rim[f, k, t.at, :] = new[f]
                if k == 0:
                    values = cells.melt(*new)

                    @pl.when(e == 0)
                    def _():
                        for f in F2:
                            tl0[f, t.at, :] = values[f]

                    @pl.when(e == 1)
                    def _():
                        for f in F2:
                            tl7[f, t.at, :] = values[f]

            tiles(1, ny, update)

    @pl.when(own[0] == 0)
    def _():
        for f in F2:
            rim[f, 0] = ox[f, 0]
            rim[f, 1] = on[f, 0]


def last_rows_kernel(own, prm, am, ar, km, kn, kx, ids, om, rim, oh, oc, pad):
    out = (oh, oc)
    ax, an, ox, on = Rows(ar, 0, 2), Rows(ar, 1, 2), Rows(rim, 0, 2), Rows(rim, 1, 2)

    @pl.when(own[0] != 0)
    def _():
        def put(name, f, i, r, t, value):
            out[f][0, r, t.at, :] = value

        coarse_body(
            prm,
            {"x": ax, "n": an, "m": am},
            {"m": km, "n": kn, "x": kx},
            {"m": om, "n": on, "x": ox},
            ids,
            put,
            "mnx",
            pad,
            True,
        )

    @pl.when(own[0] == 0)
    def _():
        old = {"m": om, "n": on, "x": ox}

        def body(name, i, r, t):
            for f in F2:
                out[f][0, r, t.at, :] = old[name][f, i, t.at, :]

        Parts(om.shape[1]).each(om.shape[2], body)


def last_edges_kernel(own, prm, low, high, ide, oh, oc, nh, nc):
    first = pl.program_id(0) == 0

    @pl.when(own[0] != 0)
    def _():
        tab = Tables(prm)

        def body(i, t):
            rate = Cells(tab, ide[0, t.at, :]).coarse()
            for f, (old, new) in enumerate(((oh, nh), (oc, nc))):
                halo = jnp.where(first, low[f, t.at, :], high[f, t.at, :])
                new[0, 0, t.at, :] = old[0, 0, t.at, :] + rate[f] * halo

        tiles(1, ide.shape[1], body)

    @pl.when(own[0] == 0)
    def _():
        nh[...] = oh[...]
        nc[...] = oc[...]


def f32(*shape):
    return jax.ShapeDtypeStruct(shape, jnp.float32)


def i32(*shape):
    return jax.ShapeDtypeStruct(shape, jnp.int32)


TINY = pl.CostEstimate(flops=1000, bytes_accessed=1000, transcendentals=0)


def call(kernel, outs, args, smem, name, scratch=(), limit=8, after=(), through=(), flops=1000, tile=256):
    after = (*after, *through)
    first = len(args) + len(after) - len(through)
    count = len(args)

    def run(*refs):
        TILE.append(tile)
        kernel(*refs[:count], *refs[count + len(after) + len(through) :])
        TILE.pop()

    return pl.pallas_call(
        run,
        out_shape=[f32(*x.shape) for x in through] + list(outs),
        in_specs=[SMEM] * smem + [VMEM] * (len(args) - smem) + [ANY] * len(after),
        out_specs=[ANY] * len(through) + [VMEM] * len(outs),
        input_output_aliases={first + i: i for i in range(len(through))},
        scratch_shapes=scratch,
        compiler_params=pltpu.CompilerParams(vmem_limit_bytes=limit * MIB),
        cost_estimate=pl.CostEstimate(flops=flops, bytes_accessed=1000, transcendentals=0),
        name=name,
    )(*args, *after)


def per_device(slices, parts, enthalpy, solute, material, phase_flag, *params):
    rows, ny, nz = material.shape
    mid = rows - 4
    h0 = enthalpy.reshape(rows, ny, nz)
    c0 = solute.reshape(rows, ny, nz)
    prm = jnp.concatenate(params)
    slot = lax.axis_index("tm")
    pair, tall = f32(2, 2, ny, nz), f32(2, mid, ny, nz)
    halo = f32(2, ny, nz)
    pad = [pltpu.VMEM((2, rows + 2, ny + 16, nz), jnp.float32)]

    def move(x, tms, up, by):
        pairs = [
            (t * parts + s, (t + up) * parts + s + by)
            for t in tms
            for s in range(parts)
            if 0 <= s + by < parts
        ]
        return lax.ppermute(x, ("tm", "space"), pairs)

    def halos(tl0, tl7, tms, up):
        return move(tl7, tms, up, 1), move(tl0, tms, up, -1)

    def send(x, n):
        return move(x, (n - 1,), 1, 0)

    def own(n):
        return (slot == n).astype(jnp.int32).reshape(1)

    def gridded(kernel, steps, outs, out_specs, in_specs, args, name, aliases={}):
        return pl.pallas_call(
            kernel,
            grid=(steps,),
            out_shape=outs,
            in_specs=in_specs,
            out_specs=out_specs,
            input_output_aliases=aliases,
            compiler_params=pltpu.CompilerParams(vmem_limit_bytes=8 * MIB),
            cost_estimate=TINY,
            name=name,
        )(*args)

    edge_row = pl.BlockSpec((1, ny, nz), lambda i: ((rows - 1) * i, 0, 0))
    whole = pl.BlockSpec((2, ny, nz), lambda i: (0, 0, 0))
    far = [pltpu.with_memory_space_constraint(x, pltpu.HBM) for x in (h0, c0, material)]
    tl0, tl7, later0, later7 = gridded(
        first_edges_kernel,
        2,
        [halo] * 4,
        [whole] * 4,
        [SMEM] + [edge_row] * 3,
        (prm, *far),
        "first_edges",
    )
    every = range(slices)
    even = halos(tl0, tl7, every[::2], 0)
    later0, later7, sm, sn, part, ids, ide = call(
        first_step_kernel,
        [tall, pair, pair, i32(rows, ny, nz), i32(2, ny, nz)],
        (prm, h0, c0, material, phase_flag),
        1,
        "first_step",
        pad,
        26,
        tile=128,
        through=(later0, later7),
    )
    odd = halos(later0, later7, every[1::2], 0)
    even = call(nothing_kernel, [], (), 0, "even_arrived", through=even, flops=10**11)

    def fine_edges(part, sides, after=()):
        return call(
            edges_kernel if len(sides) == 2 else edges_kernel_of_two,
            [pair, halo, halo],
            (prm, part, *sides, ide),
            1,
            "edges",
            after=after,
        )

    base = ()
    sides = (*even, *odd)
    for k in range(STEPS - 1):
        sx, tl0, tl7 = fine_edges(part, sides, base)
        sides = halos(tl0, tl7, every, 0)
        if k == 0:
            base = call(
                base_kernel,
                [tall, pair, pair],
                (prm, h0, c0, sm, sn, sx, ids),
                1,
                "base",
                limit=16,
                tile=128,
            )
        if k == STEPS - 3:
            *sm, sn, part = call(
                step_apart_kernel,
                [f32(mid, ny, nz)] * 2 + [pair, pair],
                (prm, sm, sn, sx, ids),
                1,
                "step_apart",
                pad,
                18,
                tile=128,
            )
        elif k == STEPS - 2:
            last = (*sm, sn, sx)
            sm, sn, part = call(
                step_joined_kernel,
                [tall, pair, pair],
                (prm, *sm, sn, sx, ids),
                1,
                "step_joined",
                pad,
                18,
                tile=512,
            )
        else:
            sm, sn, part = call(
                step_kernel, [tall, pair, pair], (prm, sm, sn, sx, ids), 1, "step", pad, 18, tile=128
            )
    km, kn, kx = base

    am, an, vm = call(
        replay_kernel,
        [tall, pair, tall],
        (own(1), prm, *(send(x, 1) for x in last), ids, km, sm),
        2,
        "replay",
        pad,
        24,
        tile=512,
    )
    vn = sn
    vx, tl0, tl7 = fine_edges(part, sides, (vm,))
    low, high = halos(tl0, tl7, (0,), 1)
    ax = send(vx, 1)
    vn, part = call(
        coarse_rim_kernel,
        [pair, pair],
        (own(1), prm, am, an, ax, kn, kx, ids, vn, vx),
        2,
        "coarse_rim",
        pad,
        20,
        tile=512,
    )
    vx, tl0, tl7 = call(
        coarse_edges_kernel,
        [pair, halo, halo],
        (own(1), prm, part, low, high, ide, vx),
        2,
        "coarse_edges",
    )
    side = pl.BlockSpec((2, 1, ny, nz), lambda i: (0, i, 0, 0))
    two = pl.BlockSpec((2, 2, ny, nz), lambda i: (0, i, 0, 0))
    inside = pl.BlockSpec((2, 1, ny, nz), lambda i: (0, (mid - 1) * i, 0, 0))

    def id_row(k):
        return pl.BlockSpec((1, ny, nz), lambda i: (k + (rows - 1 - 2 * k) * i, 0, 0))

    rim = None
    for n in range(2, slices):
        low, high = halos(tl0, tl7, (n - 1,), 1)
        am = send(vm, n)
        if n == 2:
            an, ax = send(vn, n), send(vx, n)
        else:
            ar = send(rim, n)
        if n == slices - 1:
            break
        vm = call(
            coarse_mid_kernel,
            [tall],
            (own(n), prm, am, an, km, ids, vm),
            2,
            "coarse_mid",
            pad,
            18,
        )[0]
        vm, rim, tl0, tl7 = pl.pallas_call(
            coarse_outer_kernel,
            grid=(2,),
            out_shape=[tall, f32(2, 4, ny, nz), halo, halo],
            in_specs=[SMEM, SMEM, inside, side, side, whole, whole]
            + [side] * 4
            + [id_row(2), id_row(1), id_row(0), ANY],
            out_specs=[ANY, two, whole, whole],
            scratch_shapes=[pltpu.VMEM((2, 5, ny + 16, nz), jnp.float32)],
            input_output_aliases={14: 0},
            compiler_params=pltpu.CompilerParams(vmem_limit_bytes=26 * MIB),
            cost_estimate=TINY,
            name="coarse_outer",
        )(own(n), prm, am, an, ax, low, high, kn, kx, vn, vx, ids, ids, ids, vm)

    out = f32(1, rows, ny, nz)
    last_own = own(slices - 1)
    oh, oc = call(
        last_rows_kernel,
        [out, out],
        (last_own, prm, am, ar, km, kn, kx, ids, vm, rim),
        2,
        "last_rows",
        pad,
        28,
    )
    out_row = pl.BlockSpec((1, 1, ny, nz), lambda i: (0, (rows - 1) * i, 0, 0))
    one = pl.BlockSpec((1, ny, nz), lambda i: (i, 0, 0))
    return tuple(
        gridded(
            last_edges_kernel,
            2,
            [out, out],
            [out_row] * 2,
            [SMEM, SMEM, whole, whole, one, out_row, out_row],
            (last_own, prm, low, high, ide, oh, oc),
            "last_edges",
            {5: 0, 6: 1},
        )
    )


def solution(mesh):
    body = functools.partial(per_device, mesh.shape["tm"], mesh.shape["space"])
    return jax.shard_map(
        body,
        mesh=mesh,
        in_specs=(
            P("tm", "space", None, None),
            P("tm", "space", None, None),
            P("space", None, None),
            P("space", None, None),
        )
        + (P(),) * 7,
        out_specs=(P("tm", "space", None, None), P("tm", "space", None, None)),
        check_vma=False,
    )
```

```python
import functools

import jax
import jax.numpy as jnp
from jax import lax
from jax.experimental import pallas as pl
from jax.experimental.pallas import tpu as pltpu
from jax.sharding import PartitionSpec as P

STEPS = 4
TILE = [256]
MIB = 1024 * 1024
SMEM = pl.BlockSpec(memory_space=pltpu.SMEM)
VMEM = pl.BlockSpec(memory_space=pltpu.VMEM)
ANY = pl.BlockSpec(memory_space=pl.ANY)


class Tables:
    def __init__(self, prm):
        def raw(first, count):
            return [jnp.full((8, 128), prm[first + m], jnp.float32) for m in range(count)]

        cap, self.lat, self.hs = raw(0, 4), raw(4, 4), raw(8, 4)
        kp, bd, xr = raw(12, 4), raw(16, 4), raw(20, 4)
        self.sg = raw(24, 3)
        q = [(1.0 - k) / (1.0 + b) for k, b in zip(kp, bd)]
        self.icap = [1.0 / c for c in cap]
        self.den0 = [1.0 - v for v in q]
        self.den1 = [v / t for v, t in zip(q, self.lat)]
        self.hg = [x * c for x, c in zip(xr, cap)]
        self.gh = [4.0 / (1.0 + 18.0 * x) for x in xr]
        self.crh = [h * g for h, g in zip(self.hg, self.gh)]
        self.kp18 = [18.0 / k for k in kp]


class Cells:
    def __init__(self, tab, ids):
        self.tab, self.shape = tab, ids.shape
        self.b0 = (ids & 1) != 0
        self.b1 = (ids & 2) != 0
        self.p1 = (ids & 4) != 0
        self.p2 = (ids & 8) != 0

    def wide(self, tile):
        reps = self.shape[0] // 8
        return jnp.broadcast_to(tile[None], (reps, 8, 128)).reshape(self.shape)

    def alloy(self, name):
        t = [self.wide(v) for v in getattr(self.tab, name)]
        return jnp.where(self.b1, jnp.where(self.b0, t[3], t[2]), jnp.where(self.b0, t[1], t[0]))

    def solute_gain(self):
        t = [self.wide(v) for v in self.tab.sg]
        return jnp.where(self.p2, t[2], jnp.where(self.p1, t[1], t[0]))

    def fine(self):
        return self.alloy("hg"), self.solute_gain()

    def ratio(self):
        sg = self.solute_gain()
        return self.alloy("gh"), 4.0 / (1.0 + sg * self.alloy("kp18"))

    def coarse(self):
        sg = self.solute_gain()
        return self.alloy("crh"), 4.0 * sg / (1.0 + sg * self.alloy("kp18"))

    def melt(self, h, c):
        sensible = h - self.alloy("hs")
        held = jnp.minimum(jnp.maximum(sensible, 0.0), self.alloy("lat"))
        t = (h - held) * self.alloy("icap")
        return t, c / (self.alloy("den0") + self.alloy("den1") * held)


F2 = range(2)


class Fields:
    def __init__(self, *refs):
        self.refs = refs
        self.shape = (2,) + tuple(refs[0].shape)

    def __getitem__(self, key):
        return self.refs[key[0]][key[1:]]

    def __setitem__(self, key, value):
        self.refs[key[0]][key[1:]] = value


class Rows:
    def __init__(self, ref, first, by=1):
        self.ref, self.first, self.by = ref, first, by

    def key(self, key):
        return (key[0], self.first + self.by * key[1], *key[2:])

    def __getitem__(self, key):
        return self.ref[self.key(key)]

    def __setitem__(self, key, value):
        self.ref[self.key(key)] = value


class Tile:
    def __init__(self, y, n):
        self.y, self.n = y, n
        self.at = pl.ds(y, n)

    def pad(self, by=0):
        return pl.ds(self.y + (8 + by), self.n)


def tiles(count, ny, body):
    n = TILE[-1] if ny % TILE[-1] == 0 else ny
    per = ny // n

    def run(k, carry):
        body(k // per, Tile(pl.multiple_of((k % per) * n, n), n))
        return carry

    lax.fori_loop(0, count * per, run, 0)


def clear_rims(pad):
    rows, long = pad.shape[1], pad.shape[2]
    for f in F2:
        for r in range(rows):
            pad[f, r, 0:8, :] = jnp.zeros((8, 128), jnp.float32)
            pad[f, r, long - 8 : long, :] = jnp.zeros((8, 128), jnp.float32)


def clear_ends(pad):
    def body(i, t):
        for f in F2:
            pad[f, i * (pad.shape[1] - 1), t.pad(), :] = jnp.zeros((t.n, 128), jnp.float32)

    tiles(2, pad.shape[2] - 16, body)


def put_melt(tab, pad, r, t, ids, h, c):
    values = Cells(tab, ids).melt(h, c)
    for f in F2:
        pad[f, r, t.pad(), :] = values[f]


def lap(pad, f, r, t):
    mid = pad[f, r, t.pad(), :]
    lane = lax.broadcasted_iota(jnp.int32, mid.shape, 1)
    total = pad[f, r, t.pad(-1), :] + pad[f, r, t.pad(1), :]
    total = total + jnp.where(lane == 0, 0.0, pltpu.roll(mid, 1, 1))
    total = total + jnp.where(lane == 127, 0.0, pltpu.roll(mid, 127, 1))
    return total - 6.0 * mid + pad[f, r - 1, t.pad(), :] + pad[f, r + 1, t.pad(), :]


def fine(tab, pad, r, t, ids, now):
    rate = Cells(tab, ids).fine()
    return [now[f] + rate[f] * lap(pad, f, r, t) for f in F2]


def coarse(tab, pad, r, t, ids, now):
    rate = Cells(tab, ids).coarse()
    return [now[f] + rate[f] * lap(pad, f, r, t) for f in F2]


class Parts:
    def __init__(self, mid):
        self.mid, self.rows = mid, mid + 4

    def each(self, ny, body, which="mnx"):
        if "x" in which:
            tiles(2, ny, lambda i, t: body("x", i, i * (self.rows - 1), t))
        if "n" in which:
            tiles(2, ny, lambda i, t: body("n", i, 1 + i * (self.rows - 3), t))
        if "m" in which:
            tiles(self.mid, ny, lambda i, t: body("m", i, i + 2, t))


def first_edges_kernel(prm, h, c, mat, tl0, tl7, later0, later7):
    tab = Tables(prm)
    side = pl.program_id(0)

    def body(i, t):
        values = Cells(tab, mat[0, t.at, :]).melt(h[0, t.at, :], c[0, t.at, :])

        @pl.when(side == 0)
        def _():
            for f in F2:
                tl0[f, t.at, :] = values[f]
                later0[f, t.at, :] = values[f]

        @pl.when(side == 1)
        def _():
            for f in F2:
                tl7[f, t.at, :] = values[f]
                later7[f, t.at, :] = values[f]

    tiles(1, h.shape[1], body)


def first_step_kernel(prm, h, c, mat, ph, sm, sn, part, ids, ide, pad):
    tab = Tables(prm)
    rows, ny = h.shape[0], h.shape[1]
    outs = {"m": sm, "n": sn, "x": part}
    clear_rims(pad)
    clear_ends(pad)

    def melt(r, t):
        cell = mat[r, t.at, :] + 4 * ph[r, t.at, :]
        ids[r, t.at, :] = cell
        put_melt(tab, pad, r + 1, t, cell, h[r, t.at, :], c[r, t.at, :])

    def update(part_name, i, r, t):
        new = fine(tab, pad, r + 1, t, ids[r, t.at, :], (h[r, t.at, :], c[r, t.at, :]))
        for f in F2:
            outs[part_name][f, i, t.at, :] = new[f]

    tiles(rows, ny, melt)
    ide[0] = ids[0]
    ide[1] = ids[rows - 1]
    Parts(rows - 4).each(ny, update)


def step_body(prm, sm, sn, sx, ids, outs, pad):
    tab = Tables(prm)
    ny = sm.shape[2]
    now = {"m": sm, "n": sn, "x": sx}
    block = Parts(sm.shape[1])
    clear_rims(pad)
    clear_ends(pad)

    def at(name, i, t):
        return [now[name][f, i, t.at, :] for f in F2]

    def melt(name, i, r, t):
        put_melt(tab, pad, r + 1, t, ids[r, t.at, :], *at(name, i, t))

    def update(name, i, r, t):
        new = fine(tab, pad, r + 1, t, ids[r, t.at, :], at(name, i, t))
        for f in F2:
            outs[name][f, i, t.at, :] = new[f]

    block.each(ny, melt)
    block.each(ny, update, outs)


def step_kernel(prm, sm, sn, sx, ids, nm, nn, part, pad):
    step_body(prm, sm, sn, sx, ids, {"x": part, "n": nn, "m": nm}, pad)


def step_apart_kernel(prm, sm, sn, sx, ids, mh, mc, nn, part, pad):
    step_body(prm, sm, sn, sx, ids, {"x": part, "n": nn, "m": Fields(mh, mc)}, pad)


def step_joined_kernel(prm, mh, mc, sn, sx, ids, nm, nn, part, pad):
    step_body(prm, Fields(mh, mc), sn, sx, ids, {"x": part, "n": nn, "m": nm}, pad)


def replay_kernel(own, prm, mh, mc, sn, sx, ids, km, om, am, an, nm, pad):
    @pl.when(own[0] != 0)
    def _():
        step_body(prm, Fields(mh, mc), sn, sx, ids, {"n": an, "m": am}, pad)
        coarse_body(
            prm, {"n": an, "m": am}, {"m": km}, {"m": om}, ids, into({"m": nm}), "m", pad, False
        )

    @pl.when(own[0] == 0)
    def _():
        nm[...] = om[...]


def edges_body(prm, gains, part, low, high, ide, edge, tl0, tl7):
    tab = Tables(prm)
    for e, (halo, tl) in enumerate(((low, tl0), (high, tl7))):

        def body(i, t, e=e, halo=halo, tl=tl):
            cells = Cells(tab, ide[e, t.at, :])
            rate = getattr(cells, gains)()
            new = [part[f, e, t.at, :] + rate[f] * halo[f, t.at, :] for f in F2]
            values = cells.melt(*new)
            for f in F2:
                edge[f, e, t.at, :] = new[f]
                tl[f, t.at, :] = values[f]

        tiles(1, part.shape[2], body)


class Sum:
    def __init__(self, one, other):
        self.one, self.other = one, other

    def __getitem__(self, key):
        return self.one[key] + self.other[key]


def nothing_kernel():
    pass


def edges_kernel(prm, part, low, high, ide, edge, tl0, tl7):
    edges_body(prm, "fine", part, low, high, ide, edge, tl0, tl7)


def edges_kernel_of_two(prm, part, low, high, low2, high2, ide, edge, tl0, tl7):
    edges_body(prm, "fine", part, Sum(low, low2), Sum(high, high2), ide, edge, tl0, tl7)


def coarse_edges_kernel(own, prm, part, low, high, ide, old, *refs):
    edge, tl0, tl7 = refs

    @pl.when(own[0] != 0)
    def _():
        edges_body(prm, "coarse", part, low, high, ide, edge, tl0, tl7)

    @pl.when(own[0] == 0)
    def _():
        edge[...] = old[...]


def base_kernel(prm, h, c, sm, sn, sx, ids, km, kn, kx):
    tab = Tables(prm)
    first = {"m": sm, "n": sn, "x": sx}
    outs = {"m": km, "n": kn, "x": kx}

    def body(name, i, r, t):
        ratio = Cells(tab, ids[r, t.at, :]).ratio()
        for f, u in enumerate((h[r, t.at, :], c[r, t.at, :])):
            outs[name][f, i, t.at, :] = u + ratio[f] * (first[name][f, i, t.at, :] - u)

    Parts(sm.shape[1]).each(h.shape[1], body)


def coarse_body(prm, arrived, base, old, ids, put, which, pad, edge_less):
    tab = Tables(prm)
    mid, ny = arrived["m"].shape[1], arrived["m"].shape[2]
    block = Parts(mid)
    clear_rims(pad)
    if edge_less:
        clear_ends(pad)

    def at(ref, i, t):
        return [ref[f, i, t.at, :] for f in F2]

    def melt(name, i, r, t):
        put_melt(tab, pad, r + 1, t, ids[r, t.at, :], *at(arrived[name], i, t))

    def update(name, i, r, t):
        new = coarse(tab, pad, r + 1, t, ids[r, t.at, :], at(arrived[name], i, t))
        end, start = at(old[name], i, t), at(base[name], i, t)
        for f in F2:
            put(name, f, i, r, t, new[f] + (end[f] - start[f]))

    if "m" in which:
        block.each(ny, melt, arrived)
    else:
        block.each(ny, melt, "nx")
        tiles(2, ny, lambda i, t: melt("m", i * (mid - 1), 2 + i * (mid - 1), t))
    block.each(ny, update, which)


def into(outs):
    def put(name, f, i, r, t, value):
        outs[name][f, i, t.at, :] = value

    return put


def coarse_mid_kernel(own, prm, am, an, km, ids, om, nm, pad):
    @pl.when(own[0] != 0)
    def _():
        coarse_body(
            prm, {"n": an, "m": am}, {"m": km}, {"m": om}, ids, into({"m": nm}), "m", pad, False
        )

    @pl.when(own[0] == 0)
    def _():
        nm[...] = om[...]


def coarse_rim_kernel(own, prm, am, an, ax, kn, kx, ids, on, ox, nn, part, pad):
    @pl.when(own[0] != 0)
    def _():
        coarse_body(
            prm,
            {"x": ax, "n": an, "m": am},
            {"n": kn, "x": kx},
            {"n": on, "x": ox},
            ids,
            into({"n": nn, "x": part}),
            "xn",
            pad,
            True,
        )

    @pl.when(own[0] == 0)
    def _():
        nn[...] = on[...]


def coarse_outer_kernel(own, prm, am, an, ax, low, high, kn, kx, on, ox, idm, idn, idx, *refs):
    rim, tl0, tl7, pad = refs[-4:]
    e = pl.program_id(0)
    ny = ax.shape[2]

    @pl.when(own[0] != 0)
    def _():
        tab = Tables(prm)
        clear_rims(pad)

        def zero(i, t):
            for f in F2:
                pad[f, 0, t.pad(), :] = jnp.zeros((t.n, 128), jnp.float32)

        tiles(1, ny, zero)
        for k, (now, ids) in enumerate(((ax, idx), (an, idn), (am, idm))):

            def melt(i, t, k=k, now=now, ids=ids):
                values = [now[f, 0, t.at, :] for f in F2]
                put_melt(tab, pad, k + 1, t, ids[0, t.at, :], *values)

            tiles(1, ny, melt)
        for k, (now, ids, end, start) in enumerate(((ax, idx, ox, kx), (an, idn, on, kn))):

            def update(i, t, k=k, now=now, ids=ids, end=end, start=start):
                cells = Cells(tab, ids[0, t.at, :])
                rate = cells.coarse()
                new = []
                for f in F2:
                    total = lap(pad, f, k + 1, t)
                    if k == 0:
                        total = total + jnp.where(e == 0, low[f, t.at, :], high[f, t.at, :])
                    value = now[f, 0, t.at, :] + rate[f] * total
                    new.append(value + (end[f, 0, t.at, :] - start[f, 0, t.at, :]))
                    rim[f, k, t.at, :] = new[f]
                if k == 0:
                    values = cells.melt(*new)

                    @pl.when(e == 0)
                    def _():
                        for f in F2:
                            tl0[f, t.at, :] = values[f]

                    @pl.when(e == 1)
                    def _():
                        for f in F2:
                            tl7[f, t.at, :] = values[f]

            tiles(1, ny, update)

    @pl.when(own[0] == 0)
    def _():
        for f in F2:
            rim[f, 0] = ox[f, 0]
            rim[f, 1] = on[f, 0]


def last_rows_kernel(own, prm, am, aq, ar, km, kn, kx, ids, idq, om, rim, oh, oc, pad):
    out = (oh, oc)
    e = pl.program_id(0)
    half, ny = am.shape[1], am.shape[2]
    count = half + 2

    def place(k):
        return jnp.where(e == 0, k, count - 1 - k)

    def inner(j):
        return jnp.where(e == 0, j, half - 1 - j)

    def each(body):
        tiles(1, ny, lambda i, t: body(0, t, 0, "x"))
        tiles(1, ny, lambda i, t: body(1, t, 0, "n"))
        tiles(half, ny, lambda j, t: body(j + 2, t, inner(j), "m"))

    def at(ref, i, t):
        return [ref[f, i, t.at, :] for f in F2]

    arrived = {"x": Rows(ar, 0), "n": Rows(ar, 1), "m": am}
    old = {"x": Rows(rim, 0), "n": Rows(rim, 1), "m": om}
    base = {"x": kx, "n": kn, "m": km}

    @pl.when(own[0] != 0)
    def _():
        tab = Tables(prm)
        clear_rims(pad)

        def zero(i, t):
            for f in F2:
                pad[f, 0, t.pad(), :] = jnp.zeros((t.n, 128), jnp.float32)

        def melt(k, t, i, name):
            put_melt(tab, pad, k + 1, t, ids[place(k), t.at, :], *at(arrived[name], i, t))

        def beyond(i, t):
            put_melt(tab, pad, count + 1, t, idq[0, t.at, :], *at(aq, 0, t))

        def update(k, t, i, name):
            new = coarse(tab, pad, k + 1, t, ids[place(k), t.at, :], at(arrived[name], i, t))
            end, start = at(old[name], i, t), at(base[name], i, t)
            for f in F2:
                out[f][0, place(k), t.at, :] = new[f] + (end[f] - start[f])

        tiles(1, ny, zero)
        each(melt)
        tiles(1, ny, beyond)
        each(update)

    @pl.when(own[0] == 0)
    def _():
        def keep(k, t, i, name):
            for f in F2:
                out[f][0, place(k), t.at, :] = old[name][f, i, t.at, :]

        each(keep)


def last_edges_kernel(own, prm, low, high, ide, oh, oc, nh, nc):
    first = pl.program_id(0) == 0

    @pl.when(own[0] != 0)
    def _():
        tab = Tables(prm)

        def body(i, t):
            rate = Cells(tab, ide[0, t.at, :]).coarse()
            for f, (old, new) in enumerate(((oh, nh), (oc, nc))):
                halo = jnp.where(first, low[f, t.at, :], high[f, t.at, :])
                new[0, 0, t.at, :] = old[0, 0, t.at, :] + rate[f] * halo

        tiles(1, ide.shape[1], body)

    @pl.when(own[0] == 0)
    def _():
        nh[...] = oh[...]
        nc[...] = oc[...]


def f32(*shape):
    return jax.ShapeDtypeStruct(shape, jnp.float32)


def i32(*shape):
    return jax.ShapeDtypeStruct(shape, jnp.int32)


TINY = pl.CostEstimate(flops=1000, bytes_accessed=1000, transcendentals=0)


def call(kernel, outs, args, smem, name, scratch=(), limit=8, after=(), through=(), flops=1000, tile=256):
    after = (*after, *through)
    first = len(args) + len(after) - len(through)
    count = len(args)

    def run(*refs):
        TILE.append(tile)
        kernel(*refs[:count], *refs[count + len(after) + len(through) :])
        TILE.pop()

    return pl.pallas_call(
        run,
        out_shape=[f32(*x.shape) for x in through] + list(outs),
        in_specs=[SMEM] * smem + [VMEM] * (len(args) - smem) + [ANY] * len(after),
        out_specs=[ANY] * len(through) + [VMEM] * len(outs),
        input_output_aliases={first + i: i for i in range(len(through))},
        scratch_shapes=scratch,
        compiler_params=pltpu.CompilerParams(vmem_limit_bytes=limit * MIB),
        cost_estimate=pl.CostEstimate(flops=flops, bytes_accessed=1000, transcendentals=0),
        name=name,
    )(*args, *after)


def per_device(slices, parts, enthalpy, solute, material, phase_flag, *params):
    rows, ny, nz = material.shape
    mid = rows - 4
    h0 = enthalpy.reshape(rows, ny, nz)
    c0 = solute.reshape(rows, ny, nz)
    prm = jnp.concatenate(params)
    slot = lax.axis_index("tm")
    pair, tall = f32(2, 2, ny, nz), f32(2, mid, ny, nz)
    halo = f32(2, ny, nz)
    pad = [pltpu.VMEM((2, rows + 2, ny + 16, nz), jnp.float32)]

    def move(x, tms, up, by):
        pairs = [
            (t * parts + s, (t + up) * parts + s + by)
            for t in tms
            for s in range(parts)
            if 0 <= s + by < parts
        ]
        return lax.ppermute(x, ("tm", "space"), pairs)

    def halos(tl0, tl7, tms, up):
        return move(tl7, tms, up, 1), move(tl0, tms, up, -1)

    def hbm(x):
        return pltpu.with_memory_space_constraint(x, pltpu.HBM)

    def send(x, n):
        return move(x, (n - 1,), 1, 0)

    def own(n):
        return (slot == n).astype(jnp.int32).reshape(1)

    def gridded(kernel, steps, outs, out_specs, in_specs, args, name, aliases={}):
        return pl.pallas_call(
            kernel,
            grid=(steps,),
            out_shape=outs,
            in_specs=in_specs,
            out_specs=out_specs,
            input_output_aliases=aliases,
            compiler_params=pltpu.CompilerParams(vmem_limit_bytes=8 * MIB),
            cost_estimate=TINY,
            name=name,
        )(*args)

    edge_row = pl.BlockSpec((1, ny, nz), lambda i: ((rows - 1) * i, 0, 0))
    whole = pl.BlockSpec((2, ny, nz), lambda i: (0, 0, 0))
    far = [pltpu.with_memory_space_constraint(x, pltpu.HBM) for x in (h0, c0, material)]
    tl0, tl7, later0, later7 = gridded(
        first_edges_kernel,
        2,
        [halo] * 4,
        [whole] * 4,
        [SMEM] + [edge_row] * 3,
        (prm, *far),
        "first_edges",
    )
    every = range(slices)
    even = halos(tl0, tl7, every[::2], 0)
    later0, later7, sm, sn, part, ids, ide = call(
        first_step_kernel,
        [tall, pair, pair, i32(rows, ny, nz), i32(2, ny, nz)],
        (prm, h0, c0, material, phase_flag),
        1,
        "first_step",
        pad,
        26,
        tile=128,
        through=(later0, later7),
    )
    odd = halos(later0, later7, every[1::2], 0)
    even = call(nothing_kernel, [], (), 0, "even_arrived", through=even, flops=10**11)

    def fine_edges(part, sides, after=()):
        return call(
            edges_kernel if len(sides) == 2 else edges_kernel_of_two,
            [pair, halo, halo],
            (prm, part, *sides, ide),
            1,
            "edges",
            after=after,
        )

    base = ()
    sides = (*even, *odd)
    for k in range(STEPS - 1):
        sx, tl0, tl7 = fine_edges(part, sides, base)
        sides = halos(tl0, tl7, every, 0)
        if k == 0:
            base = call(
                base_kernel,
                [tall, pair, pair],
                (prm, h0, c0, sm, sn, sx, ids),
                1,
                "base",
                limit=16,
                tile=128,
            )
        if k == STEPS - 3:
            *sm, sn, part = call(
                step_apart_kernel,
                [f32(mid, ny, nz)] * 2 + [pair, pair],
                (prm, sm, sn, sx, ids),
                1,
                "step_apart",
                pad,
                18,
                tile=128,
            )
        elif k == STEPS - 2:
            sm = [hbm(x) for x in sm]
            last = (*sm, sn, sx)
            sm, sn, part = call(
                step_joined_kernel,
                [tall, pair, pair],
                (prm, *sm, sn, sx, ids),
                1,
                "step_joined",
                pad,
                18,
                tile=512,
            )
        else:
            sm, sn, part = call(
                step_kernel, [tall, pair, pair], (prm, sm, sn, sx, ids), 1, "step", pad, 18, tile=128
            )
    km, kn, kx = base

    am, an, vm = call(
        replay_kernel,
        [tall, pair, tall],
        (own(1), prm, *(hbm(send(x, 1)) for x in last), ids, hbm(km), sm),
        2,
        "replay",
        pad,
        24,
        tile=512,
    )
    vn = sn
    vx, tl0, tl7 = fine_edges(part, sides, (vm,))
    low, high = halos(tl0, tl7, (0,), 1)
    ax = send(vx, 1)
    vn, part = call(
        coarse_rim_kernel,
        [pair, pair],
        (own(1), prm, am, an, ax, kn, kx, ids, vn, vx),
        2,
        "coarse_rim",
        pad,
        20,
        tile=512,
    )
    vx, tl0, tl7 = call(
        coarse_edges_kernel,
        [pair, halo, halo],
        (own(1), prm, part, low, high, ide, vx),
        2,
        "coarse_edges",
    )
    side = pl.BlockSpec((2, 1, ny, nz), lambda i: (0, i, 0, 0))
    two = pl.BlockSpec((2, 2, ny, nz), lambda i: (0, i, 0, 0))
    inside = pl.BlockSpec((2, 1, ny, nz), lambda i: (0, (mid - 1) * i, 0, 0))

    def id_row(k):
        return pl.BlockSpec((1, ny, nz), lambda i: (k + (rows - 1 - 2 * k) * i, 0, 0))

    rim = None
    for n in range(2, slices):
        low, high = halos(tl0, tl7, (n - 1,), 1)
        am = send(vm, n)
        if n == 2:
            an, ax = send(vn, n), send(vx, n)
        else:
            ar = send(rim, n)
        if n == slices - 1:
            break
        vm = call(
            coarse_mid_kernel,
            [tall],
            (own(n), prm, am, an, km, ids, vm),
            2,
            "coarse_mid",
            pad,
            18,
        )[0]
        vm, rim, tl0, tl7 = pl.pallas_call(
            coarse_outer_kernel,
            grid=(2,),
            out_shape=[tall, f32(2, 4, ny, nz), halo, halo],
            in_specs=[SMEM, SMEM, inside, side, side, whole, whole]
            + [side] * 4
            + [id_row(2), id_row(1), id_row(0), ANY],
            out_specs=[ANY, two, whole, whole],
            scratch_shapes=[pltpu.VMEM((2, 5, ny + 16, nz), jnp.float32)],
            input_output_aliases={14: 0},
            compiler_params=pltpu.CompilerParams(vmem_limit_bytes=26 * MIB),
            cost_estimate=TINY,
            name="coarse_outer",
        )(own(n), prm, am, an, ax, low, high, kn, kx, vn, vx, ids, ids, ids, vm)

    out = f32(1, rows, ny, nz)
    last_own = own(slices - 1)
    half = pl.BlockSpec((2, mid // 2, ny, nz), lambda i: (0, i, 0, 0))
    beyond = pl.BlockSpec((2, 1, ny, nz), lambda i: (0, mid // 2 - i, 0, 0))
    id_half = pl.BlockSpec((rows // 2, ny, nz), lambda i: (i, 0, 0))
    id_beyond = pl.BlockSpec((1, ny, nz), lambda i: (rows // 2 - i, 0, 0))
    oh, oc = pl.pallas_call(
        last_rows_kernel,
        grid=(2,),
        out_shape=[out, out],
        in_specs=[SMEM, SMEM, half, beyond, two, half, side, side, id_half, id_beyond, half, two],
        out_specs=[pl.BlockSpec((1, rows // 2, ny, nz), lambda i: (0, i, 0, 0))] * 2,
        scratch_shapes=[pltpu.VMEM((2, rows // 2 + 2, ny + 16, nz), jnp.float32)],
        compiler_params=pltpu.CompilerParams(vmem_limit_bytes=30 * MIB),
        cost_estimate=TINY,
        name="last_rows",
    )(last_own, prm, am, am, ar, hbm(km), hbm(kn), hbm(kx), ids, ids, vm, rim)
    out_row = pl.BlockSpec((1, 1, ny, nz), lambda i: (0, (rows - 1) * i, 0, 0))
    one = pl.BlockSpec((1, ny, nz), lambda i: (i, 0, 0))
    return tuple(
        gridded(
            last_edges_kernel,
            2,
            [out, out],
            [out_row] * 2,
            [SMEM, SMEM, whole, whole, one, out_row, out_row],
            (last_own, prm, low, high, ide, oh, oc),
            "last_edges",
            {5: 0, 6: 1},
        )
    )


def solution(mesh):
    body = functools.partial(per_device, mesh.shape["tm"], mesh.shape["space"])
    return jax.shard_map(
        body,
        mesh=mesh,
        in_specs=(
            P("tm", "space", None, None),
            P("tm", "space", None, None),
            P("space", None, None),
            P("space", None, None),
        )
        + (P(),) * 7,
        out_specs=(P("tm", "space", None, None), P("tm", "space", None, None)),
        check_vma=False,
    )
```

```python
import functools

import jax
import jax.numpy as jnp
from jax import lax
from jax.experimental import pallas as pl
from jax.experimental.pallas import tpu as pltpu
from jax.sharding import PartitionSpec as P

STEPS = 4
TILE = [256]
MIB = 1024 * 1024
SMEM = pl.BlockSpec(memory_space=pltpu.SMEM)
VMEM = pl.BlockSpec(memory_space=pltpu.VMEM)
ANY = pl.BlockSpec(memory_space=pl.ANY)


class Tables:
    def __init__(self, prm):
        def raw(first, count):
            return [jnp.full((8, 128), prm[first + m], jnp.float32) for m in range(count)]

        cap, self.lat, self.hs = raw(0, 4), raw(4, 4), raw(8, 4)
        kp, bd, xr = raw(12, 4), raw(16, 4), raw(20, 4)
        self.sg = raw(24, 3)
        q = [(1.0 - k) / (1.0 + b) for k, b in zip(kp, bd)]
        self.icap = [1.0 / c for c in cap]
        self.den0 = [1.0 - v for v in q]
        self.den1 = [v / t for v, t in zip(q, self.lat)]
        self.hg = [x * c for x, c in zip(xr, cap)]
        self.gh = [4.0 / (1.0 + 18.0 * x) for x in xr]
        self.crh = [h * g for h, g in zip(self.hg, self.gh)]
        self.kp18 = [18.0 / k for k in kp]


class Cells:
    def __init__(self, tab, ids):
        self.tab, self.shape = tab, ids.shape
        self.b0 = (ids & 1) != 0
        self.b1 = (ids & 2) != 0
        self.p1 = (ids & 4) != 0
        self.p2 = (ids & 8) != 0

    def wide(self, tile):
        reps = self.shape[0] // 8
        return jnp.broadcast_to(tile[None], (reps, 8, 128)).reshape(self.shape)

    def alloy(self, name):
        t = [self.wide(v) for v in getattr(self.tab, name)]
        return jnp.where(self.b1, jnp.where(self.b0, t[3], t[2]), jnp.where(self.b0, t[1], t[0]))

    def solute_gain(self):
        t = [self.wide(v) for v in self.tab.sg]
        return jnp.where(self.p2, t[2], jnp.where(self.p1, t[1], t[0]))

    def fine(self):
        return self.alloy("hg"), self.solute_gain()

    def ratio(self):
        sg = self.solute_gain()
        return self.alloy("gh"), 4.0 / (1.0 + sg * self.alloy("kp18"))

    def coarse(self):
        sg = self.solute_gain()
        return self.alloy("crh"), 4.0 * sg / (1.0 + sg * self.alloy("kp18"))

    def melt(self, h, c):
        sensible = h - self.alloy("hs")
        held = jnp.minimum(jnp.maximum(sensible, 0.0), self.alloy("lat"))
        t = (h - held) * self.alloy("icap")
        return t, c / (self.alloy("den0") + self.alloy("den1") * held)


F2 = range(2)


class Fields:
    def __init__(self, *refs):
        self.refs = refs
        self.shape = (2,) + tuple(refs[0].shape)

    def __getitem__(self, key):
        return self.refs[key[0]][key[1:]]

    def __setitem__(self, key, value):
        self.refs[key[0]][key[1:]] = value


class Rows:
    def __init__(self, ref, first, by=1):
        self.ref, self.first, self.by = ref, first, by

    def key(self, key):
        return (key[0], self.first + self.by * key[1], *key[2:])

    def __getitem__(self, key):
        return self.ref[self.key(key)]

    def __setitem__(self, key, value):
        self.ref[self.key(key)] = value


class Tile:
    def __init__(self, y, n):
        self.y, self.n = y, n
        self.at = pl.ds(y, n)

    def pad(self, by=0):
        return pl.ds(self.y + (8 + by), self.n)


def tiles(count, ny, body):
    n = TILE[-1] if ny % TILE[-1] == 0 else ny
    per = ny // n

    def run(k, carry):
        body(k // per, Tile(pl.multiple_of((k % per) * n, n), n))
        return carry

    lax.fori_loop(0, count * per, run, 0)


def clear_rims(pad):
    rows, long = pad.shape[1], pad.shape[2]
    for f in F2:
        for r in range(rows):
            pad[f, r, 0:8, :] = jnp.zeros((8, 128), jnp.float32)
            pad[f, r, long - 8 : long, :] = jnp.zeros((8, 128), jnp.float32)


def clear_ends(pad):
    def body(i, t):
        for f in F2:
            pad[f, i * (pad.shape[1] - 1), t.pad(), :] = jnp.zeros((t.n, 128), jnp.float32)

    tiles(2, pad.shape[2] - 16, body)


def put_melt(tab, pad, r, t, ids, h, c):
    values = Cells(tab, ids).melt(h, c)
    for f in F2:
        pad[f, r, t.pad(), :] = values[f]


def lap(pad, f, r, t):
    mid = pad[f, r, t.pad(), :]
    lane = lax.broadcasted_iota(jnp.int32, mid.shape, 1)
    total = pad[f, r, t.pad(-1), :] + pad[f, r, t.pad(1), :]
    total = total + jnp.where(lane == 0, 0.0, pltpu.roll(mid, 1, 1))
    total = total + jnp.where(lane == 127, 0.0, pltpu.roll(mid, 127, 1))
    return total - 6.0 * mid + pad[f, r - 1, t.pad(), :] + pad[f, r + 1, t.pad(), :]


def fine(tab, pad, r, t, ids, now):
    rate = Cells(tab, ids).fine()
    return [now[f] + rate[f] * lap(pad, f, r, t) for f in F2]


def coarse(tab, pad, r, t, ids, now):
    rate = Cells(tab, ids).coarse()
    return [now[f] + rate[f] * lap(pad, f, r, t) for f in F2]


class Parts:
    def __init__(self, mid):
        self.mid, self.rows = mid, mid + 4

    def each(self, ny, body, which="mnx"):
        if "x" in which:
            tiles(2, ny, lambda i, t: body("x", i, i * (self.rows - 1), t))
        if "n" in which:
            tiles(2, ny, lambda i, t: body("n", i, 1 + i * (self.rows - 3), t))
        if "m" in which:
            tiles(self.mid, ny, lambda i, t: body("m", i, i + 2, t))


def first_edges_kernel(prm, h, c, mat, tl0, tl7, later0, later7):
    tab = Tables(prm)
    side = pl.program_id(0)

    def body(i, t):
        values = Cells(tab, mat[0, t.at, :]).melt(h[0, t.at, :], c[0, t.at, :])

        @pl.when(side == 0)
        def _():
            for f in F2:
                tl0[f, t.at, :] = values[f]
                later0[f, t.at, :] = values[f]

        @pl.when(side == 1)
        def _():
            for f in F2:
                tl7[f, t.at, :] = values[f]
                later7[f, t.at, :] = values[f]

    tiles(1, h.shape[1], body)


def first_step_kernel(prm, h, c, mat, ph, sm, sn, part, ids, ide, pad):
    tab = Tables(prm)
    rows, ny = h.shape[0], h.shape[1]
    outs = {"m": sm, "n": sn, "x": part}
    clear_rims(pad)
    clear_ends(pad)

    def melt(r, t):
        cell = mat[r, t.at, :] + 4 * ph[r, t.at, :]
        ids[r, t.at, :] = cell
        put_melt(tab, pad, r + 1, t, cell, h[r, t.at, :], c[r, t.at, :])

    def update(part_name, i, r, t):
        new = fine(tab, pad, r + 1, t, ids[r, t.at, :], (h[r, t.at, :], c[r, t.at, :]))
        for f in F2:
            outs[part_name][f, i, t.at, :] = new[f]

    tiles(rows, ny, melt)
    ide[0] = ids[0]
    ide[1] = ids[rows - 1]
    Parts(rows - 4).each(ny, update)


def step_body(prm, sm, sn, sx, ids, outs, pad):
    tab = Tables(prm)
    ny = sm.shape[2]
    now = {"m": sm, "n": sn, "x": sx}
    block = Parts(sm.shape[1])
    clear_rims(pad)
    clear_ends(pad)

    def at(name, i, t):
        return [now[name][f, i, t.at, :] for f in F2]

    def melt(name, i, r, t):
        put_melt(tab, pad, r + 1, t, ids[r, t.at, :], *at(name, i, t))

    def update(name, i, r, t):
        new = fine(tab, pad, r + 1, t, ids[r, t.at, :], at(name, i, t))
        for f in F2:
            outs[name][f, i, t.at, :] = new[f]

    block.each(ny, melt)
    block.each(ny, update, outs)


def step_kernel(prm, sm, sn, sx, ids, nm, nn, part, pad):
    step_body(prm, sm, sn, sx, ids, {"x": part, "n": nn, "m": nm}, pad)


def step_apart_kernel(prm, sm, sn, sx, ids, mh, mc, nn, part, pad):
    step_body(prm, sm, sn, sx, ids, {"x": part, "n": nn, "m": Fields(mh, mc)}, pad)


def step_joined_kernel(prm, mh, mc, sn, sx, ids, nm, nn, part, pad):
    step_body(prm, Fields(mh, mc), sn, sx, ids, {"x": part, "n": nn, "m": nm}, pad)


def replay_kernel(own, prm, mh, mc, sn, sx, ids, km, om, am, an, nm, pad):
    @pl.when(own[0] != 0)
    def _():
        step_body(prm, Fields(mh, mc), sn, sx, ids, {"n": an, "m": am}, pad)
        coarse_body(
            prm, {"n": an, "m": am}, {"m": km}, {"m": om}, ids, into({"m": nm}), "m", pad, False
        )

    @pl.when(own[0] == 0)
    def _():
        nm[...] = om[...]


def edges_body(prm, gains, part, low, high, ide, edge, tl0, tl7):
    tab = Tables(prm)
    for e, (halo, tl) in enumerate(((low, tl0), (high, tl7))):

        def body(i, t, e=e, halo=halo, tl=tl):
            cells = Cells(tab, ide[e, t.at, :])
            rate = getattr(cells, gains)()
            new = [part[f, e, t.at, :] + rate[f] * halo[f, t.at, :] for f in F2]
            values = cells.melt(*new)
            for f in F2:
                edge[f, e, t.at, :] = new[f]
                tl[f, t.at, :] = values[f]

        tiles(1, part.shape[2], body)


class Sum:
    def __init__(self, one, other):
        self.one, self.other = one, other

    def __getitem__(self, key):
        return self.one[key] + self.other[key]


def nothing_kernel():
    pass


def edges_kernel(prm, part, low, high, ide, edge, tl0, tl7):
    edges_body(prm, "fine", part, low, high, ide, edge, tl0, tl7)


def edges_apart_kernel(prm, part, low, high, ide, edge, tl0, tl7, eh, ec):
    edges_body(prm, "fine", part, low, high, ide, edge, tl0, tl7)
    eh[...] = edge[0]
    ec[...] = edge[1]


def edges_kernel_of_two(prm, part, low, high, low2, high2, ide, edge, tl0, tl7):
    edges_body(prm, "fine", part, Sum(low, low2), Sum(high, high2), ide, edge, tl0, tl7)


def coarse_edges_kernel(own, prm, part, low, high, ide, old, *refs):
    edge, tl0, tl7 = refs

    @pl.when(own[0] != 0)
    def _():
        edges_body(prm, "coarse", part, low, high, ide, edge, tl0, tl7)

    @pl.when(own[0] == 0)
    def _():
        edge[...] = old[...]


def base_kernel(prm, h, c, sm, sn, sx, ids, km, kn, kx):
    tab = Tables(prm)
    first = {"m": sm, "n": sn, "x": sx}
    outs = {"m": km, "n": kn, "x": kx}

    def body(name, i, r, t):
        ratio = Cells(tab, ids[r, t.at, :]).ratio()
        for f, u in enumerate((h[r, t.at, :], c[r, t.at, :])):
            outs[name][f, i, t.at, :] = u + ratio[f] * (first[name][f, i, t.at, :] - u)

    Parts(sm.shape[1]).each(h.shape[1], body)


def coarse_body(prm, arrived, base, old, ids, put, which, pad, edge_less):
    tab = Tables(prm)
    mid, ny = arrived["m"].shape[1], arrived["m"].shape[2]
    block = Parts(mid)
    clear_rims(pad)
    if edge_less:
        clear_ends(pad)

    def at(ref, i, t):
        return [ref[f, i, t.at, :] for f in F2]

    def melt(name, i, r, t):
        put_melt(tab, pad, r + 1, t, ids[r, t.at, :], *at(arrived[name], i, t))

    def update(name, i, r, t):
        new = coarse(tab, pad, r + 1, t, ids[r, t.at, :], at(arrived[name], i, t))
        end, start = at(old[name], i, t), at(base[name], i, t)
        for f in F2:
            put(name, f, i, r, t, new[f] + (end[f] - start[f]))

    if "m" in which:
        block.each(ny, melt, arrived)
    else:
        block.each(ny, melt, "nx")
        tiles(2, ny, lambda i, t: melt("m", i * (mid - 1), 2 + i * (mid - 1), t))
    block.each(ny, update, which)


def into(outs):
    def put(name, f, i, r, t, value):
        outs[name][f, i, t.at, :] = value

    return put


def coarse_mid_kernel(own, prm, am, an, km, ids, om, nm, pad):
    @pl.when(own[0] != 0)
    def _():
        coarse_body(
            prm, {"n": an, "m": am}, {"m": km}, {"m": om}, ids, into({"m": nm}), "m", pad, False
        )

    @pl.when(own[0] == 0)
    def _():
        nm[...] = om[...]


def coarse_rim_kernel(own, prm, am, an, xh, xc, kn, kx, ids, on, ox, nn, part, pad):
    ax = Fields(xh, xc)

    @pl.when(own[0] != 0)
    def _():
        coarse_body(
            prm,
            {"x": ax, "n": an, "m": am},
            {"n": kn, "x": kx},
            {"n": on, "x": ox},
            ids,
            into({"n": nn, "x": part}),
            "xn",
            pad,
            True,
        )

    @pl.when(own[0] == 0)
    def _():
        nn[...] = on[...]


def coarse_outer_kernel(own, prm, am, an, ax, low, high, kn, kx, on, ox, idm, idn, idx, *refs):
    rim, tl0, tl7, pad = refs[-4:]
    e = pl.program_id(0)
    ny = ax.shape[2]

    @pl.when(own[0] != 0)
    def _():
        tab = Tables(prm)
        clear_rims(pad)

        def zero(i, t):
            for f in F2:
                pad[f, 0, t.pad(), :] = jnp.zeros((t.n, 128), jnp.float32)

        tiles(1, ny, zero)
        for k, (now, ids) in enumerate(((ax, idx), (an, idn), (am, idm))):

            def melt(i, t, k=k, now=now, ids=ids):
                values = [now[f, 0, t.at, :] for f in F2]
                put_melt(tab, pad, k + 1, t, ids[0, t.at, :], *values)

            tiles(1, ny, melt)
        for k, (now, ids, end, start) in enumerate(((ax, idx, ox, kx), (an, idn, on, kn))):

            def update(i, t, k=k, now=now, ids=ids, end=end, start=start):
                cells = Cells(tab, ids[0, t.at, :])
                rate = cells.coarse()
                new = []
                for f in F2:
                    total = lap(pad, f, k + 1, t)
                    if k == 0:
                        total = total + jnp.where(e == 0, low[f, t.at, :], high[f, t.at, :])
                    value = now[f, 0, t.at, :] + rate[f] * total
                    new.append(value + (end[f, 0, t.at, :] - start[f, 0, t.at, :]))
                    rim[f, k, t.at, :] = new[f]
                if k == 0:
                    values = cells.melt(*new)

                    @pl.when(e == 0)
                    def _():
                        for f in F2:
                            tl0[f, t.at, :] = values[f]

                    @pl.when(e == 1)
                    def _():
                        for f in F2:
                            tl7[f, t.at, :] = values[f]

            tiles(1, ny, update)

    @pl.when(own[0] == 0)
    def _():
        for f in F2:
            rim[f, 0] = ox[f, 0]
            rim[f, 1] = on[f, 0]


def last_rows_kernel(own, prm, am, aq, ar, km, kn, kx, ids, idq, om, rim, oh, oc, pad):
    out = (oh, oc)
    e = pl.program_id(0)
    half, ny = am.shape[1], am.shape[2]
    count = half + 2

    def place(k):
        return jnp.where(e == 0, k, count - 1 - k)

    def inner(j):
        return jnp.where(e == 0, j, half - 1 - j)

    def each(body):
        tiles(1, ny, lambda i, t: body(0, t, 0, "x"))
        tiles(1, ny, lambda i, t: body(1, t, 0, "n"))
        tiles(half, ny, lambda j, t: body(j + 2, t, inner(j), "m"))

    def at(ref, i, t):
        return [ref[f, i, t.at, :] for f in F2]

    arrived = {"x": Rows(ar, 0), "n": Rows(ar, 1), "m": am}
    old = {"x": Rows(rim, 0), "n": Rows(rim, 1), "m": om}
    base = {"x": kx, "n": kn, "m": km}

    @pl.when(own[0] != 0)
    def _():
        tab = Tables(prm)
        clear_rims(pad)

        def zero(i, t):
            for f in F2:
                pad[f, 0, t.pad(), :] = jnp.zeros((t.n, 128), jnp.float32)

        def melt(k, t, i, name):
            put_melt(tab, pad, k + 1, t, ids[place(k), t.at, :], *at(arrived[name], i, t))

        def beyond(i, t):
            put_melt(tab, pad, count + 1, t, idq[0, t.at, :], *at(aq, 0, t))

        def update(k, t, i, name):
            new = coarse(tab, pad, k + 1, t, ids[place(k), t.at, :], at(arrived[name], i, t))
            end, start = at(old[name], i, t), at(base[name], i, t)
            for f in F2:
                out[f][0, place(k), t.at, :] = new[f] + (end[f] - start[f])

        tiles(1, ny, zero)
        each(melt)
        tiles(1, ny, beyond)
        each(update)

    @pl.when(own[0] == 0)
    def _():
        def keep(k, t, i, name):
            for f in F2:
                out[f][0, place(k), t.at, :] = old[name][f, i, t.at, :]

        each(keep)


def last_edges_kernel(own, prm, low, high, ide, oh, oc, nh, nc):
    first = pl.program_id(0) == 0

    @pl.when(own[0] != 0)
    def _():
        tab = Tables(prm)

        def body(i, t):
            rate = Cells(tab, ide[0, t.at, :]).coarse()
            for f, (old, new) in enumerate(((oh, nh), (oc, nc))):
                halo = jnp.where(first, low[f, t.at, :], high[f, t.at, :])
                new[0, 0, t.at, :] = old[0, 0, t.at, :] + rate[f] * halo

        tiles(1, ide.shape[1], body)

    @pl.when(own[0] == 0)
    def _():
        nh[...] = oh[...]
        nc[...] = oc[...]


def f32(*shape):
    return jax.ShapeDtypeStruct(shape, jnp.float32)


def i32(*shape):
    return jax.ShapeDtypeStruct(shape, jnp.int32)


TINY = pl.CostEstimate(flops=1000, bytes_accessed=1000, transcendentals=0)


def tiled(kernel, tile):
    def run(*refs):
        TILE.append(tile)
        kernel(*refs)
        TILE.pop()

    return run


def call(kernel, outs, args, smem, name, scratch=(), limit=8, after=(), through=(), flops=1000, tile=256):
    after = (*after, *through)
    first = len(args) + len(after) - len(through)
    count = len(args)

    def run(*refs):
        TILE.append(tile)
        kernel(*refs[:count], *refs[count + len(after) + len(through) :])
        TILE.pop()

    return pl.pallas_call(
        run,
        out_shape=[f32(*x.shape) for x in through] + list(outs),
        in_specs=[SMEM] * smem + [VMEM] * (len(args) - smem) + [ANY] * len(after),
        out_specs=[ANY] * len(through) + [VMEM] * len(outs),
        input_output_aliases={first + i: i for i in range(len(through))},
        scratch_shapes=scratch,
        compiler_params=pltpu.CompilerParams(vmem_limit_bytes=limit * MIB),
        cost_estimate=pl.CostEstimate(flops=flops, bytes_accessed=1000, transcendentals=0),
        name=name,
    )(*args, *after)


def per_device(slices, parts, enthalpy, solute, material, phase_flag, *params):
    rows, ny, nz = material.shape
    mid = rows - 4
    h0 = enthalpy.reshape(rows, ny, nz)
    c0 = solute.reshape(rows, ny, nz)
    prm = jnp.concatenate(params)
    slot = lax.axis_index("tm")
    pair, tall = f32(2, 2, ny, nz), f32(2, mid, ny, nz)
    halo = f32(2, ny, nz)
    pad = [pltpu.VMEM((2, rows + 2, ny + 16, nz), jnp.float32)]

    def move(x, tms, up, by):
        pairs = [
            (t * parts + s, (t + up) * parts + s + by)
            for t in tms
            for s in range(parts)
            if 0 <= s + by < parts
        ]
        return lax.ppermute(x, ("tm", "space"), pairs)

    def halos(tl0, tl7, tms, up):
        return move(tl7, tms, up, 1), move(tl0, tms, up, -1)

    def hbm(x):
        return pltpu.with_memory_space_constraint(x, pltpu.HBM)

    def send(x, n):
        return move(x, (n - 1,), 1, 0)

    def own(n):
        return (slot == n).astype(jnp.int32).reshape(1)

    def gridded(kernel, steps, outs, out_specs, in_specs, args, name, aliases={}):
        return pl.pallas_call(
            kernel,
            grid=(steps,),
            out_shape=outs,
            in_specs=in_specs,
            out_specs=out_specs,
            input_output_aliases=aliases,
            compiler_params=pltpu.CompilerParams(vmem_limit_bytes=8 * MIB),
            cost_estimate=TINY,
            name=name,
        )(*args)

    edge_row = pl.BlockSpec((1, ny, nz), lambda i: ((rows - 1) * i, 0, 0))
    whole = pl.BlockSpec((2, ny, nz), lambda i: (0, 0, 0))
    far = [pltpu.with_memory_space_constraint(x, pltpu.HBM) for x in (h0, c0, material)]
    tl0, tl7, later0, later7 = gridded(
        first_edges_kernel,
        2,
        [halo] * 4,
        [whole] * 4,
        [SMEM] + [edge_row] * 3,
        (prm, *far),
        "first_edges",
    )
    every = range(slices)
    even = halos(tl0, tl7, every[::2], 0)
    later0, later7, sm, sn, part, ids, ide = call(
        first_step_kernel,
        [tall, pair, pair, i32(rows, ny, nz), i32(2, ny, nz)],
        (prm, h0, c0, material, phase_flag),
        1,
        "first_step",
        pad,
        26,
        tile=128,
        through=(later0, later7),
    )
    odd = halos(later0, later7, every[1::2], 0)
    even = call(nothing_kernel, [], (), 0, "even_arrived", through=even, flops=10**11)

    def fine_edges(part, sides, after=()):
        return call(
            edges_kernel if len(sides) == 2 else edges_kernel_of_two,
            [pair, halo, halo],
            (prm, part, *sides, ide),
            1,
            "edges",
            after=after,
        )

    base = ()
    sides = (*even, *odd)
    for k in range(STEPS - 1):
        sx, tl0, tl7 = fine_edges(part, sides, base)
        sides = halos(tl0, tl7, every, 0)
        if k == 0:
            base = call(
                base_kernel,
                [tall, pair, pair],
                (prm, h0, c0, sm, sn, sx, ids),
                1,
                "base",
                limit=16,
                tile=128,
            )
        if k == STEPS - 3:
            *sm, sn, part = call(
                step_apart_kernel,
                [f32(mid, ny, nz)] * 2 + [pair, pair],
                (prm, sm, sn, sx, ids),
                1,
                "step_apart",
                pad,
                18,
                tile=128,
            )
        elif k == STEPS - 2:
            sm = [hbm(x) for x in sm]
            last = (*sm, sn, sx)
            sm, sn, part = call(
                step_joined_kernel,
                [tall, pair, pair],
                (prm, *sm, sn, sx, ids),
                1,
                "step_joined",
                pad,
                18,
                tile=512,
            )
        else:
            sm, sn, part = call(
                step_kernel, [tall, pair, pair], (prm, sm, sn, sx, ids), 1, "step", pad, 18, tile=128
            )
    km, kn, kx = base

    am, an, vm = call(
        replay_kernel,
        [tall, pair, tall],
        (own(1), prm, *(hbm(send(x, 1)) for x in last), ids, hbm(km), sm),
        2,
        "replay",
        pad,
        24,
        tile=512,
    )
    vn = sn
    vx, tl0, tl7, *apart = call(
        edges_apart_kernel,
        [pair, halo, halo, halo, halo],
        (prm, part, *sides, ide),
        1,
        "edges_apart",
        after=(vm,),
    )
    low, high = halos(tl0, tl7, (0,), 1)
    ax = [send(x, 1) for x in apart]
    vn, part = call(
        coarse_rim_kernel,
        [pair, pair],
        (own(1), prm, am, an, *ax, kn, kx, ids, vn, vx),
        2,
        "coarse_rim",
        pad,
        20,
        tile=512,
    )
    vx, tl0, tl7 = call(
        coarse_edges_kernel,
        [pair, halo, halo],
        (own(1), prm, part, low, high, ide, vx),
        2,
        "coarse_edges",
    )
    side = pl.BlockSpec((2, 1, ny, nz), lambda i: (0, i, 0, 0))
    two = pl.BlockSpec((2, 2, ny, nz), lambda i: (0, i, 0, 0))
    inside = pl.BlockSpec((2, 1, ny, nz), lambda i: (0, (mid - 1) * i, 0, 0))

    def id_row(k):
        return pl.BlockSpec((1, ny, nz), lambda i: (k + (rows - 1 - 2 * k) * i, 0, 0))

    rim = None
    for n in range(2, slices):
        low, high = halos(tl0, tl7, (n - 1,), 1)
        if n == 2:
            am, an, ax = send(vm, n), send(vn, n), send(vx, n)
        else:
            am, ar = am3, send(rim, n)
        if n == slices - 1:
            break
        vm = call(
            coarse_mid_kernel,
            [tall],
            (own(n), prm, am, an, km, ids, vm),
            2,
            "coarse_mid",
            pad,
            18,
        )[0]
        vm = hbm(vm)
        am3 = hbm(send(vm, n + 1))
        low, high = call(
            nothing_kernel, [], (), 0, "arrived", through=(low, high), flops=10**11
        )
        rim, tl0, tl7 = pl.pallas_call(
            tiled(coarse_outer_kernel, 512),
            grid=(2,),
            out_shape=[f32(2, 4, ny, nz), halo, halo],
            in_specs=[SMEM, SMEM, inside, side, side, whole, whole]
            + [side] * 4
            + [id_row(2), id_row(1), id_row(0), ANY],
            out_specs=[two, whole, whole],
            scratch_shapes=[pltpu.VMEM((2, 5, ny + 16, nz), jnp.float32)],
            compiler_params=pltpu.CompilerParams(vmem_limit_bytes=26 * MIB),
            cost_estimate=TINY,
            name="coarse_outer",
        )(own(n), prm, am, an, ax, low, high, hbm(kn), hbm(kx), hbm(vn), hbm(vx), ids, ids, ids, am3)

    out = f32(1, rows, ny, nz)
    last_own = own(slices - 1)
    half = pl.BlockSpec((2, mid // 2, ny, nz), lambda i: (0, i, 0, 0))
    beyond = pl.BlockSpec((2, 1, ny, nz), lambda i: (0, mid // 2 - i, 0, 0))
    id_half = pl.BlockSpec((rows // 2, ny, nz), lambda i: (i, 0, 0))
    id_beyond = pl.BlockSpec((1, ny, nz), lambda i: (rows // 2 - i, 0, 0))
    oh, oc = pl.pallas_call(
        tiled(last_rows_kernel, 512),
        grid=(2,),
        out_shape=[out, out],
        in_specs=[SMEM, SMEM, half, beyond, two, half, side, side, id_half, id_beyond, half, two],
        out_specs=[pl.BlockSpec((1, rows // 2, ny, nz), lambda i: (0, i, 0, 0))] * 2,
        scratch_shapes=[pltpu.VMEM((2, rows // 2 + 2, ny + 16, nz), jnp.float32)],
        compiler_params=pltpu.CompilerParams(vmem_limit_bytes=30 * MIB),
        cost_estimate=TINY,
        name="last_rows",
    )(last_own, prm, am, am, ar, hbm(km), hbm(kn), hbm(kx), ids, ids, hbm(vm), rim)
    out_row = pl.BlockSpec((1, 1, ny, nz), lambda i: (0, (rows - 1) * i, 0, 0))
    one = pl.BlockSpec((1, ny, nz), lambda i: (i, 0, 0))
    return tuple(
        gridded(
            last_edges_kernel,
            2,
            [out, out],
            [out_row] * 2,
            [SMEM, SMEM, whole, whole, one, out_row, out_row],
            (last_own, prm, low, high, ide, oh, oc),
            "last_edges",
            {5: 0, 6: 1},
        )
    )


def solution(mesh):
    body = functools.partial(per_device, mesh.shape["tm"], mesh.shape["space"])
    return jax.shard_map(
        body,
        mesh=mesh,
        in_specs=(
            P("tm", "space", None, None),
            P("tm", "space", None, None),
            P("space", None, None),
            P("space", None, None),
        )
        + (P(),) * 7,
        out_specs=(P("tm", "space", None, None), P("tm", "space", None, None)),
        check_vma=False,
    )
```

```python
import functools

import jax
import jax.numpy as jnp
from jax import lax
from jax.experimental import pallas as pl
from jax.experimental.pallas import tpu as pltpu
from jax.sharding import PartitionSpec as P

STEPS = 4
TILE = [256]
MIB = 1024 * 1024
SMEM = pl.BlockSpec(memory_space=pltpu.SMEM)
VMEM = pl.BlockSpec(memory_space=pltpu.VMEM)
ANY = pl.BlockSpec(memory_space=pl.ANY)


class Tables:
    def __init__(self, prm):
        def raw(first, count):
            return [jnp.full((8, 128), prm[first + m], jnp.float32) for m in range(count)]

        cap, self.lat, self.hs = raw(0, 4), raw(4, 4), raw(8, 4)
        kp, bd, xr = raw(12, 4), raw(16, 4), raw(20, 4)
        self.sg = raw(24, 3)
        q = [(1.0 - k) / (1.0 + b) for k, b in zip(kp, bd)]
        self.icap = [1.0 / c for c in cap]
        self.den0 = [1.0 - v for v in q]
        self.den1 = [v / t for v, t in zip(q, self.lat)]
        self.hg = [x * c for x, c in zip(xr, cap)]
        self.gh = [4.0 / (1.0 + 18.0 * x) for x in xr]
        self.crh = [h * g for h, g in zip(self.hg, self.gh)]
        self.kp18 = [18.0 / k for k in kp]


class Cells:
    def __init__(self, tab, ids):
        self.tab, self.shape = tab, ids.shape
        self.b0 = (ids & 1) != 0
        self.b1 = (ids & 2) != 0
        self.p1 = (ids & 4) != 0
        self.p2 = (ids & 8) != 0

    def wide(self, tile):
        reps = self.shape[0] // 8
        return jnp.broadcast_to(tile[None], (reps, 8, 128)).reshape(self.shape)

    def alloy(self, name):
        t = [self.wide(v) for v in getattr(self.tab, name)]
        return jnp.where(self.b1, jnp.where(self.b0, t[3], t[2]), jnp.where(self.b0, t[1], t[0]))

    def solute_gain(self):
        t = [self.wide(v) for v in self.tab.sg]
        return jnp.where(self.p2, t[2], jnp.where(self.p1, t[1], t[0]))

    def fine(self):
        return self.alloy("hg"), self.solute_gain()

    def ratio(self):
        sg = self.solute_gain()
        return self.alloy("gh"), 4.0 / (1.0 + sg * self.alloy("kp18"))

    def coarse(self):
        sg = self.solute_gain()
        return self.alloy("crh"), 4.0 * sg / (1.0 + sg * self.alloy("kp18"))

    def melt(self, h, c):
        sensible = h - self.alloy("hs")
        held = jnp.minimum(jnp.maximum(sensible, 0.0), self.alloy("lat"))
        t = (h - held) * self.alloy("icap")
        return t, c / (self.alloy("den0") + self.alloy("den1") * held)


F2 = range(2)


class Fields:
    def __init__(self, *refs):
        self.refs = refs
        self.shape = (2,) + tuple(refs[0].shape)

    def __getitem__(self, key):
        return self.refs[key[0]][key[1:]]

    def __setitem__(self, key, value):
        self.refs[key[0]][key[1:]] = value


class Rows:
    def __init__(self, ref, first, by=1):
        self.ref, self.first, self.by = ref, first, by

    def key(self, key):
        return (key[0], self.first + self.by * key[1], *key[2:])

    def __getitem__(self, key):
        return self.ref[self.key(key)]

    def __setitem__(self, key, value):
        self.ref[self.key(key)] = value


class Tile:
    def __init__(self, y, n):
        self.y, self.n = y, n
        self.at = pl.ds(y, n)

    def pad(self, by=0):
        return pl.ds(self.y + (8 + by), self.n)


def tiles(count, ny, body):
    n = TILE[-1] if ny % TILE[-1] == 0 else ny
    per = ny // n

    def run(k, carry):
        body(k // per, Tile(pl.multiple_of((k % per) * n, n), n))
        return carry

    lax.fori_loop(0, count * per, run, 0)


def clear_rims(pad):
    rows, long = pad.shape[1], pad.shape[2]
    for f in F2:
        for r in range(rows):
            pad[f, r, 0:8, :] = jnp.zeros((8, 128), jnp.float32)
            pad[f, r, long - 8 : long, :] = jnp.zeros((8, 128), jnp.float32)


def clear_ends(pad):
    def body(i, t):
        for f in F2:
            pad[f, i * (pad.shape[1] - 1), t.pad(), :] = jnp.zeros((t.n, 128), jnp.float32)

    tiles(2, pad.shape[2] - 16, body)


def put_melt(tab, pad, r, t, ids, h, c):
    values = Cells(tab, ids).melt(h, c)
    for f in F2:
        pad[f, r, t.pad(), :] = values[f]


def lap(pad, f, r, t):
    mid = pad[f, r, t.pad(), :]
    lane = lax.broadcasted_iota(jnp.int32, mid.shape, 1)
    total = pad[f, r, t.pad(-1), :] + pad[f, r, t.pad(1), :]
    total = total + jnp.where(lane == 0, 0.0, pltpu.roll(mid, 1, 1))
    total = total + jnp.where(lane == 127, 0.0, pltpu.roll(mid, 127, 1))
    return total - 6.0 * mid + pad[f, r - 1, t.pad(), :] + pad[f, r + 1, t.pad(), :]


def fine(tab, pad, r, t, ids, now):
    rate = Cells(tab, ids).fine()
    return [now[f] + rate[f] * lap(pad, f, r, t) for f in F2]


def coarse(tab, pad, r, t, ids, now):
    rate = Cells(tab, ids).coarse()
    return [now[f] + rate[f] * lap(pad, f, r, t) for f in F2]


class Parts:
    def __init__(self, mid):
        self.mid, self.rows = mid, mid + 4

    def each(self, ny, body, which="mnx"):
        if "x" in which:
            tiles(2, ny, lambda i, t: body("x", i, i * (self.rows - 1), t))
        if "n" in which:
            tiles(2, ny, lambda i, t: body("n", i, 1 + i * (self.rows - 3), t))
        if "m" in which:
            tiles(self.mid, ny, lambda i, t: body("m", i, i + 2, t))


def first_edges_kernel(prm, h, c, mat, tl0, tl7, later0, later7):
    tab = Tables(prm)
    side = pl.program_id(0)

    def body(i, t):
        values = Cells(tab, mat[0, t.at, :]).melt(h[0, t.at, :], c[0, t.at, :])

        @pl.when(side == 0)
        def _():
            for f in F2:
                tl0[f, t.at, :] = values[f]
                later0[f, t.at, :] = values[f]

        @pl.when(side == 1)
        def _():
            for f in F2:
                tl7[f, t.at, :] = values[f]
                later7[f, t.at, :] = values[f]

    tiles(1, h.shape[1], body)


def first_step_kernel(prm, h, c, mat, ph, sm, sn, part, ids, ide, pad):
    tab = Tables(prm)
    rows, ny = h.shape[0], h.shape[1]
    outs = {"m": sm, "n": sn, "x": part}
    clear_rims(pad)
    clear_ends(pad)

    def melt(r, t):
        cell = mat[r, t.at, :] + 4 * ph[r, t.at, :]
        ids[r, t.at, :] = cell
        put_melt(tab, pad, r + 1, t, cell, h[r, t.at, :], c[r, t.at, :])

    def update(part_name, i, r, t):
        new = fine(tab, pad, r + 1, t, ids[r, t.at, :], (h[r, t.at, :], c[r, t.at, :]))
        for f in F2:
            outs[part_name][f, i, t.at, :] = new[f]

    tiles(rows, ny, melt)
    ide[0] = ids[0]
    ide[1] = ids[rows - 1]
    Parts(rows - 4).each(ny, update)


def step_body(prm, sm, sn, sx, ids, outs, pad):
    tab = Tables(prm)
    ny = sm.shape[2]
    now = {"m": sm, "n": sn, "x": sx}
    block = Parts(sm.shape[1])
    clear_rims(pad)
    clear_ends(pad)

    def at(name, i, t):
        return [now[name][f, i, t.at, :] for f in F2]

    def melt(name, i, r, t):
        put_melt(tab, pad, r + 1, t, ids[r, t.at, :], *at(name, i, t))

    def update(name, i, r, t):
        new = fine(tab, pad, r + 1, t, ids[r, t.at, :], at(name, i, t))
        for f in F2:
            outs[name][f, i, t.at, :] = new[f]

    block.each(ny, melt)
    block.each(ny, update, outs)


def step_kernel(prm, sm, sn, sx, ids, nm, nn, part, pad):
    step_body(prm, sm, sn, sx, ids, {"x": part, "n": nn, "m": nm}, pad)


def step_apart_kernel(prm, sm, sn, sx, ids, mh, mc, nn, part, pad):
    step_body(prm, sm, sn, sx, ids, {"x": part, "n": nn, "m": Fields(mh, mc)}, pad)


def step_joined_kernel(prm, mh, mc, sn, sx, ids, nm, nn, part, pad):
    step_body(prm, Fields(mh, mc), sn, sx, ids, {"x": part, "n": nn, "m": nm}, pad)


def replay_kernel(own, prm, mh, mc, sn, sx, ids, km, om, am, an, nm, pad):
    @pl.when(own[0] != 0)
    def _():
        step_body(prm, Fields(mh, mc), sn, sx, ids, {"n": an, "m": am}, pad)
        coarse_body(
            prm, {"n": an, "m": am}, {"m": km}, {"m": om}, ids, into({"m": nm}), "m", pad, False
        )

    @pl.when(own[0] == 0)
    def _():
        nm[...] = om[...]


def edges_body(prm, gains, part, low, high, ide, edge, tl0, tl7):
    tab = Tables(prm)
    for e, (halo, tl) in enumerate(((low, tl0), (high, tl7))):

        def body(i, t, e=e, halo=halo, tl=tl):
            cells = Cells(tab, ide[e, t.at, :])
            rate = getattr(cells, gains)()
            new = [part[f, e, t.at, :] + rate[f] * halo[f, t.at, :] for f in F2]
            values = cells.melt(*new)
            for f in F2:
                edge[f, e, t.at, :] = new[f]
                tl[f, t.at, :] = values[f]

        tiles(1, part.shape[2], body)


class Sum:
    def __init__(self, one, other):
        self.one, self.other = one, other

    def __getitem__(self, key):
        return self.one[key] + self.other[key]


def nothing_kernel():
    pass


def edges_kernel(prm, part, low, high, ide, edge, tl0, tl7):
    edges_body(prm, "fine", part, low, high, ide, edge, tl0, tl7)


def edges_apart_kernel(prm, part, low, high, ide, edge, tl0, tl7, eh, ec):
    edges_body(prm, "fine", part, low, high, ide, edge, tl0, tl7)
    eh[...] = edge[0]
    ec[...] = edge[1]


def edges_kernel_of_two(prm, part, low, high, low2, high2, ide, edge, tl0, tl7):
    edges_body(prm, "fine", part, Sum(low, low2), Sum(high, high2), ide, edge, tl0, tl7)


def coarse_edges_kernel(own, prm, part, low, high, ide, old, *refs):
    edge, tl0, tl7 = refs

    @pl.when(own[0] != 0)
    def _():
        edges_body(prm, "coarse", part, low, high, ide, edge, tl0, tl7)

    @pl.when(own[0] == 0)
    def _():
        edge[...] = old[...]


def base_kernel(prm, h, c, sm, sn, sx, ids, km, kn, kx):
    tab = Tables(prm)
    first = {"m": sm, "n": sn, "x": sx}
    outs = {"m": km, "n": kn, "x": kx}

    def body(name, i, r, t):
        ratio = Cells(tab, ids[r, t.at, :]).ratio()
        for f, u in enumerate((h[r, t.at, :], c[r, t.at, :])):
            outs[name][f, i, t.at, :] = u + ratio[f] * (first[name][f, i, t.at, :] - u)

    Parts(sm.shape[1]).each(h.shape[1], body)


def coarse_body(prm, arrived, base, old, ids, put, which, pad, edge_less):
    tab = Tables(prm)
    mid, ny = arrived["m"].shape[1], arrived["m"].shape[2]
    block = Parts(mid)
    clear_rims(pad)
    if edge_less:
        clear_ends(pad)

    def at(ref, i, t):
        return [ref[f, i, t.at, :] for f in F2]

    def melt(name, i, r, t):
        put_melt(tab, pad, r + 1, t, ids[r, t.at, :], *at(arrived[name], i, t))

    def update(name, i, r, t):
        new = coarse(tab, pad, r + 1, t, ids[r, t.at, :], at(arrived[name], i, t))
        end, start = at(old[name], i, t), at(base[name], i, t)
        for f in F2:
            put(name, f, i, r, t, new[f] + (end[f] - start[f]))

    if "m" in which:
        block.each(ny, melt, arrived)
    else:
        block.each(ny, melt, "nx")
        tiles(2, ny, lambda i, t: melt("m", i * (mid - 1), 2 + i * (mid - 1), t))
    block.each(ny, update, which)


def into(outs):
    def put(name, f, i, r, t, value):
        outs[name][f, i, t.at, :] = value

    return put


def coarse_mid_kernel(own, prm, am, an, km, ids, om, nm, pad):
    @pl.when(own[0] != 0)
    def _():
        coarse_body(
            prm, {"n": an, "m": am}, {"m": km}, {"m": om}, ids, into({"m": nm}), "m", pad, False
        )

    @pl.when(own[0] == 0)
    def _():
        nm[...] = om[...]


def coarse_rim_kernel(own, prm, am, an, xh, xc, kn, kx, ids, on, ox, nn, part, pad):
    ax = Fields(xh, xc)

    @pl.when(own[0] != 0)
    def _():
        coarse_body(
            prm,
            {"x": ax, "n": an, "m": am},
            {"n": kn, "x": kx},
            {"n": on, "x": ox},
            ids,
            into({"n": nn, "x": part}),
            "xn",
            pad,
            True,
        )

    @pl.when(own[0] == 0)
    def _():
        nn[...] = on[...]


def coarse_outer_kernel(own, prm, am, an, ax, low, high, kn, kx, on, ox, idm, idn, idx, *refs):
    rim, tl0, tl7, pad = refs[-4:]
    e = pl.program_id(0)
    ny = ax.shape[2]

    @pl.when(own[0] != 0)
    def _():
        tab = Tables(prm)
        clear_rims(pad)

        def zero(i, t):
            for f in F2:
                pad[f, 0, t.pad(), :] = jnp.zeros((t.n, 128), jnp.float32)

        tiles(1, ny, zero)
        for k, (now, ids) in enumerate(((ax, idx), (an, idn), (am, idm))):

            def melt(i, t, k=k, now=now, ids=ids):
                values = [now[f, 0, t.at, :] for f in F2]
                put_melt(tab, pad, k + 1, t, ids[0, t.at, :], *values)

            tiles(1, ny, melt)
        for k, (now, ids, end, start) in enumerate(((ax, idx, ox, kx), (an, idn, on, kn))):

            def update(i, t, k=k, now=now, ids=ids, end=end, start=start):
                cells = Cells(tab, ids[0, t.at, :])
                rate = cells.coarse()
                new = []
                for f in F2:
                    total = lap(pad, f, k + 1, t)
                    if k == 0:
                        total = total + jnp.where(e == 0, low[f, t.at, :], high[f, t.at, :])
                    value = now[f, 0, t.at, :] + rate[f] * total
                    new.append(value + (end[f, 0, t.at, :] - start[f, 0, t.at, :]))
                    rim[f, k, t.at, :] = new[f]
                if k == 0:
                    values = cells.melt(*new)

                    @pl.when(e == 0)
                    def _():
                        for f in F2:
                            tl0[f, t.at, :] = values[f]

                    @pl.when(e == 1)
                    def _():
                        for f in F2:
                            tl7[f, t.at, :] = values[f]

            tiles(1, ny, update)

    @pl.when(own[0] == 0)
    def _():
        for f in F2:
            rim[f, 0] = ox[f, 0]
            rim[f, 1] = on[f, 0]


def last_rows_kernel(own, prm, am, aq, ar, km, kn, kx, ids, idq, om, rim, oh, oc, pad):
    out = (oh, oc)
    e = pl.program_id(0)
    half, ny = am.shape[1], am.shape[2]
    count = half + 2

    def place(k):
        return jnp.where(e == 0, k, count - 1 - k)

    def inner(j):
        return jnp.where(e == 0, j, half - 1 - j)

    def each(body):
        tiles(1, ny, lambda i, t: body(0, t, 0, "x"))
        tiles(1, ny, lambda i, t: body(1, t, 0, "n"))
        tiles(half, ny, lambda j, t: body(j + 2, t, inner(j), "m"))

    def at(ref, i, t):
        return [ref[f, i, t.at, :] for f in F2]

    arrived = {"x": Rows(ar, 0), "n": Rows(ar, 1), "m": am}
    old = {"x": Rows(rim, 0), "n": Rows(rim, 1), "m": om}
    base = {"x": kx, "n": kn, "m": km}

    @pl.when(own[0] != 0)
    def _():
        tab = Tables(prm)
        clear_rims(pad)

        def zero(i, t):
            for f in F2:
                pad[f, 0, t.pad(), :] = jnp.zeros((t.n, 128), jnp.float32)

        def melt(k, t, i, name):
            put_melt(tab, pad, k + 1, t, ids[place(k), t.at, :], *at(arrived[name], i, t))

        def beyond(i, t):
            put_melt(tab, pad, count + 1, t, idq[0, t.at, :], *at(aq, 0, t))

        def update(k, t, i, name):
            new = coarse(tab, pad, k + 1, t, ids[place(k), t.at, :], at(arrived[name], i, t))
            end, start = at(old[name], i, t), at(base[name], i, t)
            for f in F2:
                out[f][0, place(k), t.at, :] = new[f] + (end[f] - start[f])

        tiles(1, ny, zero)
        each(melt)
        tiles(1, ny, beyond)
        each(update)

    @pl.when(own[0] == 0)
    def _():
        def keep(k, t, i, name):
            for f in F2:
                out[f][0, place(k), t.at, :] = old[name][f, i, t.at, :]

        each(keep)


def last_edges_kernel(own, prm, low, high, ide, oh, oc, nh, nc):
    first = pl.program_id(0) == 0

    @pl.when(own[0] != 0)
    def _():
        tab = Tables(prm)

        def body(i, t):
            rate = Cells(tab, ide[0, t.at, :]).coarse()
            for f, (old, new) in enumerate(((oh, nh), (oc, nc))):
                halo = jnp.where(first, low[f, t.at, :], high[f, t.at, :])
                new[0, 0, t.at, :] = old[0, 0, t.at, :] + rate[f] * halo

        tiles(1, ide.shape[1], body)

    @pl.when(own[0] == 0)
    def _():
        nh[...] = oh[...]
        nc[...] = oc[...]


def f32(*shape):
    return jax.ShapeDtypeStruct(shape, jnp.float32)


def i32(*shape):
    return jax.ShapeDtypeStruct(shape, jnp.int32)


TINY = pl.CostEstimate(flops=1000, bytes_accessed=1000, transcendentals=0)


def tiled(kernel, tile):
    def run(*refs):
        TILE.append(tile)
        kernel(*refs)
        TILE.pop()

    return run


def call(kernel, outs, args, smem, name, scratch=(), limit=8, after=(), through=(), flops=1000, tile=256):
    after = (*after, *through)
    first = len(args) + len(after) - len(through)
    count = len(args)

    def run(*refs):
        TILE.append(tile)
        kernel(*refs[:count], *refs[count + len(after) + len(through) :])
        TILE.pop()

    return pl.pallas_call(
        run,
        out_shape=[f32(*x.shape) for x in through] + list(outs),
        in_specs=[SMEM] * smem + [VMEM] * (len(args) - smem) + [ANY] * len(after),
        out_specs=[ANY] * len(through) + [VMEM] * len(outs),
        input_output_aliases={first + i: i for i in range(len(through))},
        scratch_shapes=scratch,
        compiler_params=pltpu.CompilerParams(vmem_limit_bytes=limit * MIB),
        cost_estimate=pl.CostEstimate(flops=flops, bytes_accessed=1000, transcendentals=0),
        name=name,
    )(*args, *after)


def per_device(slices, parts, enthalpy, solute, material, phase_flag, *params):
    rows, ny, nz = material.shape
    mid = rows - 4
    h0 = enthalpy.reshape(rows, ny, nz)
    c0 = solute.reshape(rows, ny, nz)
    prm = jnp.concatenate(params)
    slot = lax.axis_index("tm")
    pair, tall = f32(2, 2, ny, nz), f32(2, mid, ny, nz)
    halo = f32(2, ny, nz)
    pad = [pltpu.VMEM((2, rows + 2, ny + 16, nz), jnp.float32)]

    def move(x, tms, up, by):
        pairs = [
            (t * parts + s, (t + up) * parts + s + by)
            for t in tms
            for s in range(parts)
            if 0 <= s + by < parts
        ]
        return lax.ppermute(x, ("tm", "space"), pairs)

    def halos(tl0, tl7, tms, up):
        return move(tl7, tms, up, 1), move(tl0, tms, up, -1)

    def hbm(x):
        return pltpu.with_memory_space_constraint(x, pltpu.HBM)

    def send(x, n):
        return move(x, (n - 1,), 1, 0)

    def own(n):
        return (slot == n).astype(jnp.int32).reshape(1)

    def gridded(kernel, steps, outs, out_specs, in_specs, args, name, aliases={}):
        return pl.pallas_call(
            kernel,
            grid=(steps,),
            out_shape=outs,
            in_specs=in_specs,
            out_specs=out_specs,
            input_output_aliases=aliases,
            compiler_params=pltpu.CompilerParams(vmem_limit_bytes=8 * MIB),
            cost_estimate=TINY,
            name=name,
        )(*args)

    edge_row = pl.BlockSpec((1, ny, nz), lambda i: ((rows - 1) * i, 0, 0))
    whole = pl.BlockSpec((2, ny, nz), lambda i: (0, 0, 0))
    far = [pltpu.with_memory_space_constraint(x, pltpu.HBM) for x in (h0, c0, material)]
    tl0, tl7, later0, later7 = gridded(
        first_edges_kernel,
        2,
        [halo] * 4,
        [whole] * 4,
        [SMEM] + [edge_row] * 3,
        (prm, *far),
        "first_edges",
    )
    every = range(slices)
    even = halos(tl0, tl7, every[::2], 0)
    later0, later7, sm, sn, part, ids, ide = call(
        first_step_kernel,
        [tall, pair, pair, i32(rows, ny, nz), i32(2, ny, nz)],
        (prm, h0, c0, material, phase_flag),
        1,
        "first_step",
        pad,
        26,
        tile=128,
        through=(later0, later7),
    )
    odd = halos(later0, later7, every[1::2], 0)
    even = call(nothing_kernel, [], (), 0, "even_arrived", through=even, flops=10**11)

    def fine_edges(part, sides, after=()):
        return call(
            edges_kernel if len(sides) == 2 else edges_kernel_of_two,
            [pair, halo, halo],
            (prm, part, *sides, ide),
            1,
            "edges",
            after=after,
        )

    base = ()
    sides = (*even, *odd)
    for k in range(STEPS - 1):
        sx, tl0, tl7 = fine_edges(part, sides, base)
        sides = halos(tl0, tl7, every, 0)
        if k == 0:
            base = call(
                base_kernel,
                [tall, pair, pair],
                (prm, h0, c0, sm, sn, sx, ids),
                1,
                "base",
                limit=16,
                tile=128,
            )
        if k == STEPS - 3:
            *sm, sn, part = call(
                step_apart_kernel,
                [pltpu.HBM((mid, ny, nz), jnp.float32)] * 2 + [pair, pair],
                (prm, sm, sn, sx, ids),
                1,
                "step_apart",
                pad,
                18,
                tile=128,
            )
        elif k == STEPS - 2:
            sm = [hbm(x) for x in sm]
            last = (*sm, sn, sx)
            sm, sn, part = call(
                step_joined_kernel,
                [tall, pair, pair],
                (prm, *sm, sn, sx, ids),
                1,
                "step_joined",
                pad,
                18,
                tile=512,
            )
        else:
            sm, sn, part = call(
                step_kernel, [tall, pair, pair], (prm, sm, sn, sx, ids), 1, "step", pad, 18, tile=128
            )
    km, kn, kx = base

    am, an, vm = call(
        replay_kernel,
        [tall, pair, tall],
        (own(1), prm, *(hbm(send(x, 1)) for x in last), ids, hbm(km), sm),
        2,
        "replay",
        pad,
        24,
        tile=512,
    )
    vn = sn
    vx, tl0, tl7, *apart = call(
        edges_apart_kernel,
        [pair, halo, halo, halo, halo],
        (prm, part, *sides, ide),
        1,
        "edges_apart",
        after=(vm,),
    )
    low, high = halos(tl0, tl7, (0,), 1)
    ax = [send(x, 1) for x in apart]
    vn, part = call(
        coarse_rim_kernel,
        [pair, pair],
        (own(1), prm, am, an, *ax, kn, kx, ids, vn, vx),
        2,
        "coarse_rim",
        pad,
        20,
        tile=512,
    )
    vx, tl0, tl7 = call(
        coarse_edges_kernel,
        [pltpu.HBM(pair.shape, pair.dtype), halo, halo],
        (own(1), prm, part, low, high, ide, vx),
        2,
        "coarse_edges",
    )
    side = pl.BlockSpec((2, 1, ny, nz), lambda i: (0, i, 0, 0))
    two = pl.BlockSpec((2, 2, ny, nz), lambda i: (0, i, 0, 0))
    inside = pl.BlockSpec((2, 1, ny, nz), lambda i: (0, (mid - 1) * i, 0, 0))

    def id_row(k):
        return pl.BlockSpec((1, ny, nz), lambda i: (k + (rows - 1 - 2 * k) * i, 0, 0))

    rim = None
    for n in range(2, slices):
        low, high = halos(tl0, tl7, (n - 1,), 1)
        if n == 2:
            am, an, ax = send(vm, n), send(vn, n), send(vx, n)
        else:
            am, ar = am3, send(rim, n)
        if n == slices - 1:
            break
        vm = call(
            coarse_mid_kernel,
            [pltpu.HBM(tall.shape, tall.dtype)],
            (own(n), prm, am, an, km, ids, vm),
            2,
            "coarse_mid",
            pad,
            18,
        )[0]
        vm = hbm(vm)
        am3 = hbm(send(vm, n + 1))
        low, high = call(
            nothing_kernel, [], (), 0, "arrived", through=(low, high), flops=10**11
        )
        rim, tl0, tl7 = pl.pallas_call(
            tiled(coarse_outer_kernel, 512),
            grid=(2,),
            out_shape=[f32(2, 4, ny, nz), halo, halo],
            in_specs=[SMEM, SMEM, inside, side, side, whole, whole]
            + [side] * 4
            + [id_row(2), id_row(1), id_row(0), ANY],
            out_specs=[two, whole, whole],
            scratch_shapes=[pltpu.VMEM((2, 5, ny + 16, nz), jnp.float32)],
            compiler_params=pltpu.CompilerParams(vmem_limit_bytes=26 * MIB),
            cost_estimate=TINY,
            name="coarse_outer",
        )(own(n), prm, am, an, ax, low, high, hbm(kn), hbm(kx), hbm(vn), hbm(vx), ids, ids, ids, am3)

    out = f32(1, rows, ny, nz)
    last_own = own(slices - 1)
    half = pl.BlockSpec((2, mid // 2, ny, nz), lambda i: (0, i, 0, 0))
    beyond = pl.BlockSpec((2, 1, ny, nz), lambda i: (0, mid // 2 - i, 0, 0))
    id_half = pl.BlockSpec((rows // 2, ny, nz), lambda i: (i, 0, 0))
    id_beyond = pl.BlockSpec((1, ny, nz), lambda i: (rows // 2 - i, 0, 0))
    oh, oc = pl.pallas_call(
        tiled(last_rows_kernel, 512),
        grid=(2,),
        out_shape=[out, out],
        in_specs=[SMEM, SMEM, half, beyond, two, half, side, side, id_half, id_beyond, half, two],
        out_specs=[pl.BlockSpec((1, rows // 2, ny, nz), lambda i: (0, i, 0, 0))] * 2,
        scratch_shapes=[pltpu.VMEM((2, rows // 2 + 2, ny + 16, nz), jnp.float32)],
        compiler_params=pltpu.CompilerParams(vmem_limit_bytes=30 * MIB),
        cost_estimate=TINY,
        name="last_rows",
    )(last_own, prm, am, am, ar, hbm(km), hbm(kn), hbm(kx), ids, ids, hbm(vm), rim)
    out_row = pl.BlockSpec((1, 1, ny, nz), lambda i: (0, (rows - 1) * i, 0, 0))
    one = pl.BlockSpec((1, ny, nz), lambda i: (i, 0, 0))
    return tuple(
        gridded(
            last_edges_kernel,
            2,
            [out, out],
            [out_row] * 2,
            [SMEM, SMEM, whole, whole, one, out_row, out_row],
            (last_own, prm, low, high, ide, oh, oc),
            "last_edges",
            {5: 0, 6: 1},
        )
    )


def solution(mesh):
    body = functools.partial(per_device, mesh.shape["tm"], mesh.shape["space"])
    return jax.shard_map(
        body,
        mesh=mesh,
        in_specs=(
            P("tm", "space", None, None),
            P("tm", "space", None, None),
            P("space", None, None),
            P("space", None, None),
        )
        + (P(),) * 7,
        out_specs=(P("tm", "space", None, None), P("tm", "space", None, None)),
        check_vma=False,
    )
```

```python
import functools

import jax
import jax.numpy as jnp
from jax import lax
from jax.experimental import pallas as pl
from jax.experimental.pallas import tpu as pltpu
from jax.sharding import PartitionSpec as P

STEPS = 4
TILE = [256]
MIB = 1024 * 1024
SMEM = pl.BlockSpec(memory_space=pltpu.SMEM)
VMEM = pl.BlockSpec(memory_space=pltpu.VMEM)
ANY = pl.BlockSpec(memory_space=pl.ANY)


class Tables:
    def __init__(self, prm):
        def raw(first, count):
            return [jnp.full((8, 128), prm[first + m], jnp.float32) for m in range(count)]

        cap, self.lat, self.hs = raw(0, 4), raw(4, 4), raw(8, 4)
        kp, bd, xr = raw(12, 4), raw(16, 4), raw(20, 4)
        self.sg = raw(24, 3)
        q = [(1.0 - k) / (1.0 + b) for k, b in zip(kp, bd)]
        self.icap = [1.0 / c for c in cap]
        self.den0 = [1.0 - v for v in q]
        self.den1 = [v / t for v, t in zip(q, self.lat)]
        self.hg = [x * c for x, c in zip(xr, cap)]
        self.gh = [4.0 / (1.0 + 18.0 * x) for x in xr]
        self.crh = [h * g for h, g in zip(self.hg, self.gh)]
        self.kp18 = [18.0 / k for k in kp]


class Cells:
    def __init__(self, tab, ids):
        self.tab, self.shape = tab, ids.shape
        self.b0 = (ids & 1) != 0
        self.b1 = (ids & 2) != 0
        self.p1 = (ids & 4) != 0
        self.p2 = (ids & 8) != 0

    def wide(self, tile):
        reps = self.shape[0] // 8
        return jnp.broadcast_to(tile[None], (reps, 8, 128)).reshape(self.shape)

    def alloy(self, name):
        t = [self.wide(v) for v in getattr(self.tab, name)]
        return jnp.where(self.b1, jnp.where(self.b0, t[3], t[2]), jnp.where(self.b0, t[1], t[0]))

    def solute_gain(self):
        t = [self.wide(v) for v in self.tab.sg]
        return jnp.where(self.p2, t[2], jnp.where(self.p1, t[1], t[0]))

    def fine(self):
        return self.alloy("hg"), self.solute_gain()

    def ratio(self):
        sg = self.solute_gain()
        return self.alloy("gh"), 4.0 / (1.0 + sg * self.alloy("kp18"))

    def coarse(self):
        sg = self.solute_gain()
        return self.alloy("crh"), 4.0 * sg / (1.0 + sg * self.alloy("kp18"))

    def melt(self, h, c):
        sensible = h - self.alloy("hs")
        held = jnp.minimum(jnp.maximum(sensible, 0.0), self.alloy("lat"))
        t = (h - held) * self.alloy("icap")
        return t, c / (self.alloy("den0") + self.alloy("den1") * held)


F2 = range(2)


class Fields:
    def __init__(self, *refs):
        self.refs = refs
        self.shape = (2,) + tuple(refs[0].shape)

    def __getitem__(self, key):
        return self.refs[key[0]][key[1:]]

    def __setitem__(self, key, value):
        self.refs[key[0]][key[1:]] = value


class Rows:
    def __init__(self, ref, first, by=1):
        self.ref, self.first, self.by = ref, first, by

    def key(self, key):
        return (key[0], self.first + self.by * key[1], *key[2:])

    def __getitem__(self, key):
        return self.ref[self.key(key)]

    def __setitem__(self, key, value):
        self.ref[self.key(key)] = value


class Tile:
    def __init__(self, y, n):
        self.y, self.n = y, n
        self.at = pl.ds(y, n)

    def pad(self, by=0):
        return pl.ds(self.y + (8 + by), self.n)


def tiles(count, ny, body):
    n = TILE[-1] if ny % TILE[-1] == 0 else ny
    per = ny // n

    def run(k, carry):
        body(k // per, Tile(pl.multiple_of((k % per) * n, n), n))
        return carry

    lax.fori_loop(0, count * per, run, 0)


def clear_rims(pad):
    rows, long = pad.shape[1], pad.shape[2]
    for f in F2:
        for r in range(rows):
            pad[f, r, 0:8, :] = jnp.zeros((8, 128), jnp.float32)
            pad[f, r, long - 8 : long, :] = jnp.zeros((8, 128), jnp.float32)


def clear_ends(pad):
    def body(i, t):
        for f in F2:
            pad[f, i * (pad.shape[1] - 1), t.pad(), :] = jnp.zeros((t.n, 128), jnp.float32)

    tiles(2, pad.shape[2] - 16, body)


def put_melt(tab, pad, r, t, ids, h, c):
    values = Cells(tab, ids).melt(h, c)
    for f in F2:
        pad[f, r, t.pad(), :] = values[f]


def lap(pad, f, r, t):
    mid = pad[f, r, t.pad(), :]
    lane = lax.broadcasted_iota(jnp.int32, mid.shape, 1)
    total = pad[f, r, t.pad(-1), :] + pad[f, r, t.pad(1), :]
    total = total + jnp.where(lane == 0, 0.0, pltpu.roll(mid, 1, 1))
    total = total + jnp.where(lane == 127, 0.0, pltpu.roll(mid, 127, 1))
    return total - 6.0 * mid + pad[f, r - 1, t.pad(), :] + pad[f, r + 1, t.pad(), :]


def fine(tab, pad, r, t, ids, now):
    rate = Cells(tab, ids).fine()
    return [now[f] + rate[f] * lap(pad, f, r, t) for f in F2]


def coarse(tab, pad, r, t, ids, now):
    rate = Cells(tab, ids).coarse()
    return [now[f] + rate[f] * lap(pad, f, r, t) for f in F2]


class Parts:
    def __init__(self, mid):
        self.mid, self.rows = mid, mid + 4

    def each(self, ny, body, which="mnx"):
        if "x" in which:
            tiles(2, ny, lambda i, t: body("x", i, i * (self.rows - 1), t))
        if "n" in which:
            tiles(2, ny, lambda i, t: body("n", i, 1 + i * (self.rows - 3), t))
        if "m" in which:
            tiles(self.mid, ny, lambda i, t: body("m", i, i + 2, t))


def first_edges_kernel(prm, h, c, mat, tl0, tl7, later0, later7):
    tab = Tables(prm)
    side = pl.program_id(0)

    def body(i, t):
        values = Cells(tab, mat[0, t.at, :]).melt(h[0, t.at, :], c[0, t.at, :])

        @pl.when(side == 0)
        def _():
            for f in F2:
                tl0[f, t.at, :] = values[f]
                later0[f, t.at, :] = values[f]

        @pl.when(side == 1)
        def _():
            for f in F2:
                tl7[f, t.at, :] = values[f]
                later7[f, t.at, :] = values[f]

    tiles(1, h.shape[1], body)


def first_step_kernel(prm, h, c, mat, ph, sm, sn, part, ids, ide, pad):
    tab = Tables(prm)
    rows, ny = h.shape[0], h.shape[1]
    outs = {"m": sm, "n": sn, "x": part}
    clear_rims(pad)
    clear_ends(pad)

    def melt(r, t):
        cell = mat[r, t.at, :] + 4 * ph[r, t.at, :]
        ids[r, t.at, :] = cell
        put_melt(tab, pad, r + 1, t, cell, h[r, t.at, :], c[r, t.at, :])

    def update(part_name, i, r, t):
        new = fine(tab, pad, r + 1, t, ids[r, t.at, :], (h[r, t.at, :], c[r, t.at, :]))
        for f in F2:
            outs[part_name][f, i, t.at, :] = new[f]

    tiles(rows, ny, melt)
    ide[0] = ids[0]
    ide[1] = ids[rows - 1]
    Parts(rows - 4).each(ny, update)


def step_body(prm, sm, sn, sx, ids, outs, pad):
    tab = Tables(prm)
    ny = sm.shape[2]
    now = {"m": sm, "n": sn, "x": sx}
    block = Parts(sm.shape[1])
    clear_rims(pad)
    clear_ends(pad)

    def at(name, i, t):
        return [now[name][f, i, t.at, :] for f in F2]

    def melt(name, i, r, t):
        put_melt(tab, pad, r + 1, t, ids[r, t.at, :], *at(name, i, t))

    def update(name, i, r, t):
        new = fine(tab, pad, r + 1, t, ids[r, t.at, :], at(name, i, t))
        for f in F2:
            outs[name][f, i, t.at, :] = new[f]

    block.each(ny, melt)
    block.each(ny, update, outs)


def step_kernel(prm, sm, sn, sx, ids, nm, nn, part, pad):
    step_body(prm, sm, sn, sx, ids, {"x": part, "n": nn, "m": nm}, pad)


def step_apart_kernel(prm, sm, sn, sx, ids, mh, mc, nn, part, pad):
    step_body(prm, sm, sn, sx, ids, {"x": part, "n": nn, "m": Fields(mh, mc)}, pad)


def step_joined_kernel(prm, mh, mc, sn, sx, ids, nm, nn, part, pad):
    step_body(prm, Fields(mh, mc), sn, sx, ids, {"x": part, "n": nn, "m": nm}, pad)


def replay_kernel(own, prm, mh, mc, sn, sx, ids, km, om, am, an, nm, pad):
    @pl.when(own[0] != 0)
    def _():
        step_body(prm, Fields(mh, mc), sn, sx, ids, {"n": an, "m": am}, pad)
        coarse_body(
            prm, {"n": an, "m": am}, {"m": km}, {"m": om}, ids, into({"m": nm}), "m", pad, False
        )

    @pl.when(own[0] == 0)
    def _():
        nm[...] = om[...]


def edges_body(prm, gains, part, low, high, ide, edge, tl0, tl7):
    tab = Tables(prm)
    for e, (halo, tl) in enumerate(((low, tl0), (high, tl7))):

        def body(i, t, e=e, halo=halo, tl=tl):
            cells = Cells(tab, ide[e, t.at, :])
            rate = getattr(cells, gains)()
            new = [part[f, e, t.at, :] + rate[f] * halo[f, t.at, :] for f in F2]
            values = cells.melt(*new)
            for f in F2:
                edge[f, e, t.at, :] = new[f]
                tl[f, t.at, :] = values[f]

        tiles(1, part.shape[2], body)


class Sum:
    def __init__(self, one, other):
        self.one, self.other = one, other

    def __getitem__(self, key):
        return self.one[key] + self.other[key]


def nothing_kernel():
    pass


def edges_kernel(prm, part, low, high, ide, edge, tl0, tl7):
    edges_body(prm, "fine", part, low, high, ide, edge, tl0, tl7)


def edges_apart_kernel(prm, part, low, high, ide, edge, tl0, tl7, eh, ec):
    edges_body(prm, "fine", part, low, high, ide, edge, tl0, tl7)
    eh[...] = edge[0]
    ec[...] = edge[1]


def edges_kernel_of_two(prm, part, low, high, low2, high2, ide, edge, tl0, tl7):
    edges_body(prm, "fine", part, Sum(low, low2), Sum(high, high2), ide, edge, tl0, tl7)


def coarse_edges_kernel(own, prm, part, low, high, ide, old, *refs):
    edge, tl0, tl7 = refs

    @pl.when(own[0] != 0)
    def _():
        edges_body(prm, "coarse", part, low, high, ide, edge, tl0, tl7)

    @pl.when(own[0] == 0)
    def _():
        edge[...] = old[...]


def base_kernel(prm, h, c, sm, sn, sx, ids, km, kn, kx):
    tab = Tables(prm)
    first = {"m": sm, "n": sn, "x": sx}
    outs = {"m": km, "n": kn, "x": kx}

    def body(name, i, r, t):
        ratio = Cells(tab, ids[r, t.at, :]).ratio()
        for f, u in enumerate((h[r, t.at, :], c[r, t.at, :])):
            outs[name][f, i, t.at, :] = u + ratio[f] * (first[name][f, i, t.at, :] - u)

    Parts(sm.shape[1]).each(h.shape[1], body)


def coarse_body(prm, arrived, base, old, ids, put, which, pad, edge_less):
    tab = Tables(prm)
    mid, ny = arrived["m"].shape[1], arrived["m"].shape[2]
    block = Parts(mid)
    clear_rims(pad)
    if edge_less:
        clear_ends(pad)

    def at(ref, i, t):
        return [ref[f, i, t.at, :] for f in F2]

    def melt(name, i, r, t):
        put_melt(tab, pad, r + 1, t, ids[r, t.at, :], *at(arrived[name], i, t))

    def update(name, i, r, t):
        new = coarse(tab, pad, r + 1, t, ids[r, t.at, :], at(arrived[name], i, t))
        end, start = at(old[name], i, t), at(base[name], i, t)
        for f in F2:
            put(name, f, i, r, t, new[f] + (end[f] - start[f]))

    if "m" in which:
        block.each(ny, melt, arrived)
    else:
        block.each(ny, melt, "nx")
        tiles(2, ny, lambda i, t: melt("m", i * (mid - 1), 2 + i * (mid - 1), t))
    block.each(ny, update, which)


def into(outs):
    def put(name, f, i, r, t, value):
        outs[name][f, i, t.at, :] = value

    return put


def coarse_mid_kernel(own, prm, am, an, km, ids, om, nm, pad):
    @pl.when(own[0] != 0)
    def _():
        coarse_body(
            prm, {"n": an, "m": am}, {"m": km}, {"m": om}, ids, into({"m": nm}), "m", pad, False
        )

    @pl.when(own[0] == 0)
    def _():
        nm[...] = om[...]


def coarse_rim_kernel(own, prm, am, an, xh, xc, kn, kx, ids, on, ox, nn, part, pad):
    ax = Fields(xh, xc)

    @pl.when(own[0] != 0)
    def _():
        coarse_body(
            prm,
            {"x": ax, "n": an, "m": am},
            {"n": kn, "x": kx},
            {"n": on, "x": ox},
            ids,
            into({"n": nn, "x": part}),
            "xn",
            pad,
            True,
        )

    @pl.when(own[0] == 0)
    def _():
        nn[...] = on[...]


def coarse_outer_kernel(own, prm, am, an, ax, low, high, kn, kx, on, ox, idm, idn, idx, *refs):
    rim, tl0, tl7, pad = refs[-4:]
    e = pl.program_id(0)
    ny = ax.shape[2]

    @pl.when(own[0] != 0)
    def _():
        tab = Tables(prm)
        clear_rims(pad)

        def zero(i, t):
            for f in F2:
                pad[f, 0, t.pad(), :] = jnp.zeros((t.n, 128), jnp.float32)

        tiles(1, ny, zero)
        for k, (now, ids) in enumerate(((ax, idx), (an, idn), (am, idm))):

            def melt(i, t, k=k, now=now, ids=ids):
                values = [now[f, 0, t.at, :] for f in F2]
                put_melt(tab, pad, k + 1, t, ids[0, t.at, :], *values)

            tiles(1, ny, melt)
        for k, (now, ids, end, start) in enumerate(((ax, idx, ox, kx), (an, idn, on, kn))):

            def update(i, t, k=k, now=now, ids=ids, end=end, start=start):
                cells = Cells(tab, ids[0, t.at, :])
                rate = cells.coarse()
                new = []
                for f in F2:
                    total = lap(pad, f, k + 1, t)
                    if k == 0:
                        total = total + jnp.where(e == 0, low[f, t.at, :], high[f, t.at, :])
                    value = now[f, 0, t.at, :] + rate[f] * total
                    new.append(value + (end[f, 0, t.at, :] - start[f, 0, t.at, :]))
                    rim[f, k, t.at, :] = new[f]
                if k == 0:
                    values = cells.melt(*new)

                    @pl.when(e == 0)
                    def _():
                        for f in F2:
                            tl0[f, t.at, :] = values[f]

                    @pl.when(e == 1)
                    def _():
                        for f in F2:
                            tl7[f, t.at, :] = values[f]

            tiles(1, ny, update)

    @pl.when(own[0] == 0)
    def _():
        for f in F2:
            rim[f, 0] = ox[f, 0]
            rim[f, 1] = on[f, 0]


def last_rows_kernel(own, prm, am, aq, ar, km, kn, kx, ids, idq, om, rim, oh, oc, pad):
    out = (oh, oc)
    e = pl.program_id(0)
    half, ny = am.shape[1], am.shape[2]
    count = half + 2

    def place(k):
        return jnp.where(e == 0, k, count - 1 - k)

    def inner(j):
        return jnp.where(e == 0, j, half - 1 - j)

    def each(body):
        tiles(1, ny, lambda i, t: body(0, t, 0, "x"))
        tiles(1, ny, lambda i, t: body(1, t, 0, "n"))
        tiles(half, ny, lambda j, t: body(j + 2, t, inner(j), "m"))

    def at(ref, i, t):
        return [ref[f, i, t.at, :] for f in F2]

    arrived = {"x": Rows(ar, 0), "n": Rows(ar, 1), "m": am}
    old = {"x": Rows(rim, 0), "n": Rows(rim, 1), "m": om}
    base = {"x": kx, "n": kn, "m": km}

    @pl.when(own[0] != 0)
    def _():
        tab = Tables(prm)
        clear_rims(pad)

        def zero(i, t):
            for f in F2:
                pad[f, 0, t.pad(), :] = jnp.zeros((t.n, 128), jnp.float32)

        def melt(k, t, i, name):
            put_melt(tab, pad, k + 1, t, ids[place(k), t.at, :], *at(arrived[name], i, t))

        def beyond(i, t):
            put_melt(tab, pad, count + 1, t, idq[0, t.at, :], *at(aq, 0, t))

        def update(k, t, i, name):
            new = coarse(tab, pad, k + 1, t, ids[place(k), t.at, :], at(arrived[name], i, t))
            end, start = at(old[name], i, t), at(base[name], i, t)
            for f in F2:
                out[f][0, place(k), t.at, :] = new[f] + (end[f] - start[f])

        tiles(1, ny, zero)
        each(melt)
        tiles(1, ny, beyond)
        each(update)

    @pl.when(own[0] == 0)
    def _():
        def keep(k, t, i, name):
            for f in F2:
                out[f][0, place(k), t.at, :] = old[name][f, i, t.at, :]

        each(keep)


def last_edges_kernel(own, prm, low, high, ide, oh, oc, nh, nc):
    first = pl.program_id(0) == 0

    @pl.when(own[0] != 0)
    def _():
        tab = Tables(prm)

        def body(i, t):
            rate = Cells(tab, ide[0, t.at, :]).coarse()
            for f, (old, new) in enumerate(((oh, nh), (oc, nc))):
                halo = jnp.where(first, low[f, t.at, :], high[f, t.at, :])
                new[0, 0, t.at, :] = old[0, 0, t.at, :] + rate[f] * halo

        tiles(1, ide.shape[1], body)

    @pl.when(own[0] == 0)
    def _():
        nh[...] = oh[...]
        nc[...] = oc[...]


def f32(*shape):
    return jax.ShapeDtypeStruct(shape, jnp.float32)


def i32(*shape):
    return jax.ShapeDtypeStruct(shape, jnp.int32)


TINY = pl.CostEstimate(flops=1000, bytes_accessed=1000, transcendentals=0)


def tiled(kernel, tile):
    def run(*refs):
        TILE.append(tile)
        kernel(*refs)
        TILE.pop()

    return run


def call(kernel, outs, args, smem, name, scratch=(), limit=8, after=(), through=(), flops=1000, tile=256):
    after = (*after, *through)
    first = len(args) + len(after) - len(through)
    count = len(args)

    def run(*refs):
        TILE.append(tile)
        kernel(*refs[:count], *refs[count + len(after) + len(through) :])
        TILE.pop()

    return pl.pallas_call(
        run,
        out_shape=[f32(*x.shape) for x in through] + list(outs),
        in_specs=[SMEM] * smem + [VMEM] * (len(args) - smem) + [ANY] * len(after),
        out_specs=[ANY] * len(through) + [VMEM] * len(outs),
        input_output_aliases={first + i: i for i in range(len(through))},
        scratch_shapes=scratch,
        compiler_params=pltpu.CompilerParams(vmem_limit_bytes=limit * MIB),
        cost_estimate=pl.CostEstimate(flops=flops, bytes_accessed=1000, transcendentals=0),
        name=name,
    )(*args, *after)


def per_device(slices, parts, enthalpy, solute, material, phase_flag, *params):
    rows, ny, nz = material.shape
    mid = rows - 4
    h0 = enthalpy.reshape(rows, ny, nz)
    c0 = solute.reshape(rows, ny, nz)
    prm = jnp.concatenate(params)
    slot = lax.axis_index("tm")
    pair, tall = f32(2, 2, ny, nz), f32(2, mid, ny, nz)
    halo = f32(2, ny, nz)
    pad = [pltpu.VMEM((2, rows + 2, ny + 16, nz), jnp.float32)]

    def move(x, tms, up, by):
        pairs = [
            (t * parts + s, (t + up) * parts + s + by)
            for t in tms
            for s in range(parts)
            if 0 <= s + by < parts
        ]
        return lax.ppermute(x, ("tm", "space"), pairs)

    def halos(tl0, tl7, tms, up):
        return move(tl7, tms, up, 1), move(tl0, tms, up, -1)

    def hbm(x):
        return pltpu.with_memory_space_constraint(x, pltpu.HBM)

    def send(x, n):
        return move(x, (n - 1,), 1, 0)

    def own(n):
        return (slot == n).astype(jnp.int32).reshape(1)

    def gridded(kernel, steps, outs, out_specs, in_specs, args, name, aliases={}):
        return pl.pallas_call(
            kernel,
            grid=(steps,),
            out_shape=outs,
            in_specs=in_specs,
            out_specs=out_specs,
            input_output_aliases=aliases,
            compiler_params=pltpu.CompilerParams(vmem_limit_bytes=8 * MIB),
            cost_estimate=TINY,
            name=name,
        )(*args)

    edge_row = pl.BlockSpec((1, ny, nz), lambda i: ((rows - 1) * i, 0, 0))
    whole = pl.BlockSpec((2, ny, nz), lambda i: (0, 0, 0))
    far = [pltpu.with_memory_space_constraint(x, pltpu.HBM) for x in (h0, c0, material)]
    tl0, tl7, later0, later7 = gridded(
        first_edges_kernel,
        2,
        [halo] * 4,
        [whole] * 4,
        [SMEM] + [edge_row] * 3,
        (prm, *far),
        "first_edges",
    )
    every = range(slices)
    even = halos(tl0, tl7, every[::2], 0)
    later0, later7, sm, sn, part, ids, ide = call(
        first_step_kernel,
        [tall, pair, pair, i32(rows, ny, nz), i32(2, ny, nz)],
        (prm, h0, c0, material, phase_flag),
        1,
        "first_step",
        pad,
        26,
        tile=128,
        through=(later0, later7),
    )
    odd = halos(later0, later7, every[1::2], 0)
    even = call(nothing_kernel, [], (), 0, "even_arrived", through=even, flops=10**11)

    def fine_edges(part, sides, after=()):
        return call(
            edges_kernel if len(sides) == 2 else edges_kernel_of_two,
            [pair, halo, halo],
            (prm, part, *sides, ide),
            1,
            "edges",
            after=after,
            tile=512,
        )

    base = ()
    sides = (*even, *odd)
    for k in range(STEPS - 1):
        sx, tl0, tl7 = fine_edges(part, sides, base)
        sides = halos(tl0, tl7, every, 0)
        if k == 0:
            base = call(
                base_kernel,
                [tall, pair, pair],
                (prm, h0, c0, sm, sn, sx, ids),
                1,
                "base",
                limit=16,
                tile=128,
            )
        if k == STEPS - 3:
            *sm, sn, part = call(
                step_apart_kernel,
                [pltpu.HBM((mid, ny, nz), jnp.float32)] * 2 + [pair, pair],
                (prm, sm, sn, sx, ids),
                1,
                "step_apart",
                pad,
                18,
                tile=128,
            )
        elif k == STEPS - 2:
            sm = [hbm(x) for x in sm]
            last = (*sm, sn, sx)
            sm, sn, part = call(
                step_joined_kernel,
                [tall, pair, pair],
                (prm, *sm, sn, sx, ids),
                1,
                "step_joined",
                pad,
                18,
                tile=512,
            )
        else:
            sm, sn, part = call(
                step_kernel, [tall, pair, pair], (prm, sm, sn, sx, ids), 1, "step", pad, 18, tile=128
            )
    km, kn, kx = base

    am, an, vm = call(
        replay_kernel,
        [tall, pair, tall],
        (own(1), prm, *(hbm(send(x, 1)) for x in last), ids, hbm(km), sm),
        2,
        "replay",
        pad,
        24,
        tile=512,
    )
    vn = sn
    vx, tl0, tl7, *apart = call(
        edges_apart_kernel,
        [pair, halo, halo, halo, halo],
        (prm, part, *sides, ide),
        1,
        "edges_apart",
        tile=512,
        after=(vm,),
    )
    low, high = halos(tl0, tl7, (0,), 1)
    ax = [send(x, 1) for x in apart]
    vn, part = call(
        coarse_rim_kernel,
        [pair, pair],
        (own(1), prm, am, an, *ax, kn, kx, ids, vn, vx),
        2,
        "coarse_rim",
        pad,
        20,
        tile=512,
    )
    vx, tl0, tl7 = call(
        coarse_edges_kernel,
        [pltpu.HBM(pair.shape, pair.dtype), halo, halo],
        (own(1), prm, part, low, high, ide, vx),
        2,
        "coarse_edges",
        tile=512,
    )
    side = pl.BlockSpec((2, 1, ny, nz), lambda i: (0, i, 0, 0))
    two = pl.BlockSpec((2, 2, ny, nz), lambda i: (0, i, 0, 0))
    inside = pl.BlockSpec((2, 1, ny, nz), lambda i: (0, (mid - 1) * i, 0, 0))

    def id_row(k):
        return pl.BlockSpec((1, ny, nz), lambda i: (k + (rows - 1 - 2 * k) * i, 0, 0))

    rim = None
    for n in range(2, slices):
        low, high = halos(tl0, tl7, (n - 1,), 1)
        if n == 2:
            am, an, ax = send(vm, n), send(vn, n), send(vx, n)
        else:
            am, ar = am3, send(rim, n)
        if n == slices - 1:
            break
        vm = call(
            coarse_mid_kernel,
            [pltpu.HBM(tall.shape, tall.dtype)],
            (own(n), prm, am, an, km, ids, vm),
            2,
            "coarse_mid",
            pad,
            18,
            tile=128,
        )[0]
        vm = hbm(vm)
        am3 = hbm(send(vm, n + 1))
        low, high = call(
            nothing_kernel, [], (), 0, "arrived", through=(low, high), flops=10**11
        )
        rim, tl0, tl7 = pl.pallas_call(
            tiled(coarse_outer_kernel, 512),
            grid=(2,),
            out_shape=[f32(2, 4, ny, nz), halo, halo],
            in_specs=[SMEM, SMEM, inside, side, side, whole, whole]
            + [side] * 4
            + [id_row(2), id_row(1), id_row(0), ANY],
            out_specs=[two, whole, whole],
            scratch_shapes=[pltpu.VMEM((2, 5, ny + 16, nz), jnp.float32)],
            compiler_params=pltpu.CompilerParams(vmem_limit_bytes=26 * MIB),
            cost_estimate=TINY,
            name="coarse_outer",
        )(own(n), prm, am, an, ax, low, high, hbm(kn), hbm(kx), hbm(vn), hbm(vx), ids, ids, ids, am3)

    out = f32(1, rows, ny, nz)
    last_own = own(slices - 1)
    half = pl.BlockSpec((2, mid // 2, ny, nz), lambda i: (0, i, 0, 0))
    beyond = pl.BlockSpec((2, 1, ny, nz), lambda i: (0, mid // 2 - i, 0, 0))
    id_half = pl.BlockSpec((rows // 2, ny, nz), lambda i: (i, 0, 0))
    id_beyond = pl.BlockSpec((1, ny, nz), lambda i: (rows // 2 - i, 0, 0))
    oh, oc = pl.pallas_call(
        tiled(last_rows_kernel, 512),
        grid=(2,),
        out_shape=[out, out],
        in_specs=[SMEM, SMEM, half, beyond, two, half, side, side, id_half, id_beyond, half, two],
        out_specs=[pl.BlockSpec((1, rows // 2, ny, nz), lambda i: (0, i, 0, 0))] * 2,
        scratch_shapes=[pltpu.VMEM((2, rows // 2 + 2, ny + 16, nz), jnp.float32)],
        compiler_params=pltpu.CompilerParams(vmem_limit_bytes=30 * MIB),
        cost_estimate=TINY,
        name="last_rows",
    )(last_own, prm, am, am, ar, hbm(km), hbm(kn), hbm(kx), ids, ids, hbm(vm), rim)
    out_row = pl.BlockSpec((1, 1, ny, nz), lambda i: (0, (rows - 1) * i, 0, 0))
    one = pl.BlockSpec((1, ny, nz), lambda i: (i, 0, 0))
    return tuple(
        gridded(
            last_edges_kernel,
            2,
            [out, out],
            [out_row] * 2,
            [SMEM, SMEM, whole, whole, one, out_row, out_row],
            (last_own, prm, low, high, ide, oh, oc),
            "last_edges",
            {5: 0, 6: 1},
        )
    )


def solution(mesh):
    body = functools.partial(per_device, mesh.shape["tm"], mesh.shape["space"])
    return jax.shard_map(
        body,
        mesh=mesh,
        in_specs=(
            P("tm", "space", None, None),
            P("tm", "space", None, None),
            P("space", None, None),
            P("space", None, None),
        )
        + (P(),) * 7,
        out_specs=(P("tm", "space", None, None), P("tm", "space", None, None)),
        check_vma=False,
    )
```

```python
import functools

import jax
import jax.numpy as jnp
from jax import lax
from jax.experimental import pallas as pl
from jax.experimental.pallas import tpu as pltpu
from jax.sharding import PartitionSpec as P

STEPS = 4
TILE = [256]
MIB = 1024 * 1024
SMEM = pl.BlockSpec(memory_space=pltpu.SMEM)
VMEM = pl.BlockSpec(memory_space=pltpu.VMEM)
ANY = pl.BlockSpec(memory_space=pl.ANY)


class Tables:
    def __init__(self, prm):
        def raw(first, count):
            return [jnp.full((8, 128), prm[first + m], jnp.float32) for m in range(count)]

        cap, self.lat, self.hs = raw(0, 4), raw(4, 4), raw(8, 4)
        kp, bd, xr = raw(12, 4), raw(16, 4), raw(20, 4)
        self.sg = raw(24, 3)
        q = [(1.0 - k) / (1.0 + b) for k, b in zip(kp, bd)]
        self.icap = [1.0 / c for c in cap]
        self.den0 = [1.0 - v for v in q]
        self.den1 = [v / t for v, t in zip(q, self.lat)]
        self.hg = [x * c for x, c in zip(xr, cap)]
        self.gh = [4.0 / (1.0 + 18.0 * x) for x in xr]
        self.crh = [h * g for h, g in zip(self.hg, self.gh)]
        self.kp18 = [18.0 / k for k in kp]


class Params:
    def __init__(self, refs):
        self.refs = refs

    def __getitem__(self, i):
        k = min(i // 4, 6)
        return self.refs[k][i - 4 * k]


class Cells:
    def __init__(self, tab, ids):
        self.tab, self.shape = tab, ids.shape
        self.b0 = (ids & 1) != 0
        self.b1 = (ids & 2) != 0
        self.p1 = (ids & 4) != 0
        self.p2 = (ids & 8) != 0

    def wide(self, tile):
        reps = self.shape[0] // 8
        return jnp.broadcast_to(tile[None], (reps, 8, 128)).reshape(self.shape)

    def alloy(self, name):
        t = [self.wide(v) for v in getattr(self.tab, name)]
        return jnp.where(self.b1, jnp.where(self.b0, t[3], t[2]), jnp.where(self.b0, t[1], t[0]))

    def solute_gain(self):
        t = [self.wide(v) for v in self.tab.sg]
        return jnp.where(self.p2, t[2], jnp.where(self.p1, t[1], t[0]))

    def fine(self):
        return self.alloy("hg"), self.solute_gain()

    def ratio(self):
        sg = self.solute_gain()
        return self.alloy("gh"), 4.0 / (1.0 + sg * self.alloy("kp18"))

    def coarse(self):
        sg = self.solute_gain()
        return self.alloy("crh"), 4.0 * sg / (1.0 + sg * self.alloy("kp18"))

    def melt(self, h, c):
        sensible = h - self.alloy("hs")
        held = jnp.minimum(jnp.maximum(sensible, 0.0), self.alloy("lat"))
        t = (h - held) * self.alloy("icap")
        return t, c / (self.alloy("den0") + self.alloy("den1") * held)


F2 = range(2)


class Fields:
    def __init__(self, *refs):
        self.refs = refs
        self.shape = (2,) + tuple(refs[0].shape)

    def __getitem__(self, key):
        return self.refs[key[0]][key[1:]]

    def __setitem__(self, key, value):
        self.refs[key[0]][key[1:]] = value


class Rows:
    def __init__(self, ref, first, by=1):
        self.ref, self.first, self.by = ref, first, by

    def key(self, key):
        return (key[0], self.first + self.by * key[1], *key[2:])

    def __getitem__(self, key):
        return self.ref[self.key(key)]

    def __setitem__(self, key, value):
        self.ref[self.key(key)] = value


class Tile:
    def __init__(self, y, n):
        self.y, self.n = y, n
        self.at = pl.ds(y, n)

    def pad(self, by=0):
        return pl.ds(self.y + (8 + by), self.n)


def tiles(count, ny, body):
    n = TILE[-1] if ny % TILE[-1] == 0 else ny
    per = ny // n

    def run(k, carry):
        body(k // per, Tile(pl.multiple_of((k % per) * n, n), n))
        return carry

    lax.fori_loop(0, count * per, run, 0)


def clear_rims(pad):
    rows, long = pad.shape[1], pad.shape[2]
    for f in F2:
        for r in range(rows):
            pad[f, r, 0:8, :] = jnp.zeros((8, 128), jnp.float32)
            pad[f, r, long - 8 : long, :] = jnp.zeros((8, 128), jnp.float32)


def clear_ends(pad):
    def body(i, t):
        for f in F2:
            pad[f, i * (pad.shape[1] - 1), t.pad(), :] = jnp.zeros((t.n, 128), jnp.float32)

    tiles(2, pad.shape[2] - 16, body)


def put_melt(tab, pad, r, t, ids, h, c):
    values = Cells(tab, ids).melt(h, c)
    for f in F2:
        pad[f, r, t.pad(), :] = values[f]


def lap(pad, f, r, t):
    mid = pad[f, r, t.pad(), :]
    lane = lax.broadcasted_iota(jnp.int32, mid.shape, 1)
    total = pad[f, r, t.pad(-1), :] + pad[f, r, t.pad(1), :]
    total = total + jnp.where(lane == 0, 0.0, pltpu.roll(mid, 1, 1))
    total = total + jnp.where(lane == 127, 0.0, pltpu.roll(mid, 127, 1))
    return total - 6.0 * mid + pad[f, r - 1, t.pad(), :] + pad[f, r + 1, t.pad(), :]


def fine(tab, pad, r, t, ids, now):
    rate = Cells(tab, ids).fine()
    return [now[f] + rate[f] * lap(pad, f, r, t) for f in F2]


def coarse(tab, pad, r, t, ids, now):
    rate = Cells(tab, ids).coarse()
    return [now[f] + rate[f] * lap(pad, f, r, t) for f in F2]


class Parts:
    def __init__(self, mid):
        self.mid, self.rows = mid, mid + 4

    def each(self, ny, body, which="mnx"):
        if "x" in which:
            tiles(2, ny, lambda i, t: body("x", i, i * (self.rows - 1), t))
        if "n" in which:
            tiles(2, ny, lambda i, t: body("n", i, 1 + i * (self.rows - 3), t))
        if "m" in which:
            tiles(self.mid, ny, lambda i, t: body("m", i, i + 2, t))


def first_edges_kernel(*refs):
    h, c, mat, tl0, tl7, later0, later7 = refs[7:]
    tab = Tables(Params(refs[:7]))
    side = pl.program_id(0)

    def body(i, t):
        values = Cells(tab, mat[0, t.at, :]).melt(h[0, t.at, :], c[0, t.at, :])

        @pl.when(side == 0)
        def _():
            for f in F2:
                tl0[f, t.at, :] = values[f]
                later0[f, t.at, :] = values[f]

        @pl.when(side == 1)
        def _():
            for f in F2:
                tl7[f, t.at, :] = values[f]
                later7[f, t.at, :] = values[f]

    tiles(1, h.shape[1], body)


def first_step_kernel(prm, h, c, mat, ph, sm, sn, part, ids, ide, pad):
    tab = Tables(prm)
    rows, ny = h.shape[0], h.shape[1]
    outs = {"m": sm, "n": sn, "x": part}
    clear_rims(pad)
    clear_ends(pad)

    def melt(r, t):
        cell = mat[r, t.at, :] + 4 * ph[r, t.at, :]
        ids[r, t.at, :] = cell
        put_melt(tab, pad, r + 1, t, cell, h[r, t.at, :], c[r, t.at, :])

    def update(part_name, i, r, t):
        new = fine(tab, pad, r + 1, t, ids[r, t.at, :], (h[r, t.at, :], c[r, t.at, :]))
        for f in F2:
            outs[part_name][f, i, t.at, :] = new[f]

    tiles(rows, ny, melt)
    ide[0] = ids[0]
    ide[1] = ids[rows - 1]
    Parts(rows - 4).each(ny, update)


def step_body(prm, sm, sn, sx, ids, outs, pad):
    tab = Tables(prm)
    ny = sm.shape[2]
    now = {"m": sm, "n": sn, "x": sx}
    block = Parts(sm.shape[1])
    clear_rims(pad)
    clear_ends(pad)

    def at(name, i, t):
        return [now[name][f, i, t.at, :] for f in F2]

    def melt(name, i, r, t):
        put_melt(tab, pad, r + 1, t, ids[r, t.at, :], *at(name, i, t))

    def update(name, i, r, t):
        new = fine(tab, pad, r + 1, t, ids[r, t.at, :], at(name, i, t))
        for f in F2:
            outs[name][f, i, t.at, :] = new[f]

    block.each(ny, melt)
    block.each(ny, update, outs)


def step_kernel(prm, sm, sn, sx, ids, nm, nn, part, pad):
    step_body(prm, sm, sn, sx, ids, {"x": part, "n": nn, "m": nm}, pad)


def step_apart_kernel(prm, sm, sn, sx, ids, mh, mc, nn, part, pad):
    step_body(prm, sm, sn, sx, ids, {"x": part, "n": nn, "m": Fields(mh, mc)}, pad)


def step_joined_kernel(prm, mh, mc, sn, sx, ids, nm, nn, part, pad):
    step_body(prm, Fields(mh, mc), sn, sx, ids, {"x": part, "n": nn, "m": nm}, pad)


def replay_kernel(own, prm, mh, mc, sn, sx, ids, km, om, am, an, nm, pad):
    @pl.when(own[0] != 0)
    def _():
        step_body(prm, Fields(mh, mc), sn, sx, ids, {"n": an, "m": am}, pad)
        coarse_body(
            prm, {"n": an, "m": am}, {"m": km}, {"m": om}, ids, into({"m": nm}), "m", pad, False
        )

    @pl.when(own[0] == 0)
    def _():
        nm[...] = om[...]


def edges_body(prm, gains, part, low, high, ide, edge, tl0, tl7):
    tab = Tables(prm)
    for e, (halo, tl) in enumerate(((low, tl0), (high, tl7))):

        def body(i, t, e=e, halo=halo, tl=tl):
            cells = Cells(tab, ide[e, t.at, :])
            rate = getattr(cells, gains)()
            new = [part[f, e, t.at, :] + rate[f] * halo[f, t.at, :] for f in F2]
            values = cells.melt(*new)
            for f in F2:
                edge[f, e, t.at, :] = new[f]
                tl[f, t.at, :] = values[f]

        tiles(1, part.shape[2], body)


class Sum:
    def __init__(self, one, other):
        self.one, self.other = one, other

    def __getitem__(self, key):
        return self.one[key] + self.other[key]


def nothing_kernel():
    pass


def edges_kernel(prm, part, low, high, ide, edge, tl0, tl7):
    edges_body(prm, "fine", part, low, high, ide, edge, tl0, tl7)


def edges_apart_kernel(prm, part, low, high, ide, edge, tl0, tl7, eh, ec):
    edges_body(prm, "fine", part, low, high, ide, edge, tl0, tl7)
    eh[...] = edge[0]
    ec[...] = edge[1]


def edges_kernel_of_two(prm, part, low, high, low2, high2, ide, edge, tl0, tl7):
    edges_body(prm, "fine", part, Sum(low, low2), Sum(high, high2), ide, edge, tl0, tl7)


def coarse_edges_kernel(own, prm, part, low, high, ide, old, *refs):
    edge, tl0, tl7 = refs

    @pl.when(own[0] != 0)
    def _():
        edges_body(prm, "coarse", part, low, high, ide, edge, tl0, tl7)

    @pl.when(own[0] == 0)
    def _():
        edge[...] = old[...]


def base_kernel(prm, h, c, sm, sn, sx, ids, km, kn, kx):
    tab = Tables(prm)
    first = {"m": sm, "n": sn, "x": sx}
    outs = {"m": km, "n": kn, "x": kx}

    def body(name, i, r, t):
        ratio = Cells(tab, ids[r, t.at, :]).ratio()
        for f, u in enumerate((h[r, t.at, :], c[r, t.at, :])):
            outs[name][f, i, t.at, :] = u + ratio[f] * (first[name][f, i, t.at, :] - u)

    Parts(sm.shape[1]).each(h.shape[1], body)


def coarse_body(prm, arrived, base, old, ids, put, which, pad, edge_less):
    tab = Tables(prm)
    mid, ny = arrived["m"].shape[1], arrived["m"].shape[2]
    block = Parts(mid)
    clear_rims(pad)
    if edge_less:
        clear_ends(pad)

    def at(ref, i, t):
        return [ref[f, i, t.at, :] for f in F2]

    def melt(name, i, r, t):
        put_melt(tab, pad, r + 1, t, ids[r, t.at, :], *at(arrived[name], i, t))

    def update(name, i, r, t):
        new = coarse(tab, pad, r + 1, t, ids[r, t.at, :], at(arrived[name], i, t))
        end, start = at(old[name], i, t), at(base[name], i, t)
        for f in F2:
            put(name, f, i, r, t, new[f] + (end[f] - start[f]))

    if "m" in which:
        block.each(ny, melt, arrived)
    else:
        block.each(ny, melt, "nx")
        tiles(2, ny, lambda i, t: melt("m", i * (mid - 1), 2 + i * (mid - 1), t))
    block.each(ny, update, which)


def into(outs):
    def put(name, f, i, r, t, value):
        outs[name][f, i, t.at, :] = value

    return put


def coarse_mid_kernel(own, prm, am, an, km, ids, om, nm, pad):
    @pl.when(own[0] != 0)
    def _():
        coarse_body(
            prm, {"n": an, "m": am}, {"m": km}, {"m": om}, ids, into({"m": nm}), "m", pad, False
        )

    @pl.when(own[0] == 0)
    def _():
        nm[...] = om[...]


def coarse_rim_kernel(own, prm, am, an, xh, xc, kn, kx, ids, on, ox, nn, part, pad):
    ax = Fields(xh, xc)

    @pl.when(own[0] != 0)
    def _():
        coarse_body(
            prm,
            {"x": ax, "n": an, "m": am},
            {"n": kn, "x": kx},
            {"n": on, "x": ox},
            ids,
            into({"n": nn, "x": part}),
            "xn",
            pad,
            True,
        )

    @pl.when(own[0] == 0)
    def _():
        nn[...] = on[...]


def coarse_outer_kernel(own, prm, am, an, ax, low, high, kn, kx, on, ox, idm, idn, idx, *refs):
    rim, tl0, tl7, pad = refs[-4:]
    e = pl.program_id(0)
    ny = ax.shape[2]

    @pl.when(own[0] != 0)
    def _():
        tab = Tables(prm)
        clear_rims(pad)

        def zero(i, t):
            for f in F2:
                pad[f, 0, t.pad(), :] = jnp.zeros((t.n, 128), jnp.float32)

        tiles(1, ny, zero)
        for k, (now, ids) in enumerate(((ax, idx), (an, idn), (am, idm))):

            def melt(i, t, k=k, now=now, ids=ids):
                values = [now[f, 0, t.at, :] for f in F2]
                put_melt(tab, pad, k + 1, t, ids[0, t.at, :], *values)

            tiles(1, ny, melt)
        for k, (now, ids, end, start) in enumerate(((ax, idx, ox, kx), (an, idn, on, kn))):

            def update(i, t, k=k, now=now, ids=ids, end=end, start=start):
                cells = Cells(tab, ids[0, t.at, :])
                rate = cells.coarse()
                new = []
                for f in F2:
                    total = lap(pad, f, k + 1, t)
                    if k == 0:
                        total = total + jnp.where(e == 0, low[f, t.at, :], high[f, t.at, :])
                    value = now[f, 0, t.at, :] + rate[f] * total
                    new.append(value + (end[f, 0, t.at, :] - start[f, 0, t.at, :]))
                    rim[f, k, t.at, :] = new[f]
                if k == 0:
                    values = cells.melt(*new)

                    @pl.when(e == 0)
                    def _():
                        for f in F2:
                            tl0[f, t.at, :] = values[f]

                    @pl.when(e == 1)
                    def _():
                        for f in F2:
                            tl7[f, t.at, :] = values[f]

            tiles(1, ny, update)

    @pl.when(own[0] == 0)
    def _():
        for f in F2:
            rim[f, 0] = ox[f, 0]
            rim[f, 1] = on[f, 0]


def last_rows_kernel(own, prm, am, aq, ar, km, kn, kx, ids, idq, om, rim, oh, oc, pad):
    out = (oh, oc)
    e = pl.program_id(0)
    half, ny = am.shape[1], am.shape[2]
    count = half + 2

    def place(k):
        return jnp.where(e == 0, k, count - 1 - k)

    def inner(j):
        return jnp.where(e == 0, j, half - 1 - j)

    def each(body):
        tiles(1, ny, lambda i, t: body(0, t, 0, "x"))
        tiles(1, ny, lambda i, t: body(1, t, 0, "n"))
        tiles(half, ny, lambda j, t: body(j + 2, t, inner(j), "m"))

    def at(ref, i, t):
        return [ref[f, i, t.at, :] for f in F2]

    arrived = {"x": Rows(ar, 0), "n": Rows(ar, 1), "m": am}
    old = {"x": Rows(rim, 0), "n": Rows(rim, 1), "m": om}
    base = {"x": kx, "n": kn, "m": km}

    @pl.when(own[0] != 0)
    def _():
        tab = Tables(prm)
        clear_rims(pad)

        def zero(i, t):
            for f in F2:
                pad[f, 0, t.pad(), :] = jnp.zeros((t.n, 128), jnp.float32)

        def melt(k, t, i, name):
            put_melt(tab, pad, k + 1, t, ids[place(k), t.at, :], *at(arrived[name], i, t))

        def beyond(i, t):
            put_melt(tab, pad, count + 1, t, idq[0, t.at, :], *at(aq, 0, t))

        def update(k, t, i, name):
            new = coarse(tab, pad, k + 1, t, ids[place(k), t.at, :], at(arrived[name], i, t))
            end, start = at(old[name], i, t), at(base[name], i, t)
            for f in F2:
                out[f][0, place(k), t.at, :] = new[f] + (end[f] - start[f])

        tiles(1, ny, zero)
        each(melt)
        tiles(1, ny, beyond)
        each(update)

    @pl.when(own[0] == 0)
    def _():
        def keep(k, t, i, name):
            for f in F2:
                out[f][0, place(k), t.at, :] = old[name][f, i, t.at, :]

        each(keep)


def last_edges_kernel(own, prm, low, high, ide, oh, oc, nh, nc):
    first = pl.program_id(0) == 0

    @pl.when(own[0] != 0)
    def _():
        tab = Tables(prm)

        def body(i, t):
            rate = Cells(tab, ide[0, t.at, :]).coarse()
            for f, (old, new) in enumerate(((oh, nh), (oc, nc))):
                halo = jnp.where(first, low[f, t.at, :], high[f, t.at, :])
                new[0, 0, t.at, :] = old[0, 0, t.at, :] + rate[f] * halo

        tiles(1, ide.shape[1], body)

    @pl.when(own[0] == 0)
    def _():
        nh[...] = oh[...]
        nc[...] = oc[...]


def f32(*shape):
    return jax.ShapeDtypeStruct(shape, jnp.float32)


def i32(*shape):
    return jax.ShapeDtypeStruct(shape, jnp.int32)


TINY = pl.CostEstimate(flops=1000, bytes_accessed=1000, transcendentals=0)


def tiled(kernel, tile):
    def run(*refs):
        TILE.append(tile)
        kernel(*refs)
        TILE.pop()

    return run


def call(kernel, outs, args, smem, name, scratch=(), limit=8, after=(), through=(), flops=1000, tile=256):
    after = (*after, *through)
    first = len(args) + len(after) - len(through)
    count = len(args)

    def run(*refs):
        TILE.append(tile)
        kernel(*refs[:count], *refs[count + len(after) + len(through) :])
        TILE.pop()

    return pl.pallas_call(
        run,
        out_shape=[f32(*x.shape) for x in through] + list(outs),
        in_specs=[SMEM] * smem + [VMEM] * (len(args) - smem) + [ANY] * len(after),
        out_specs=[ANY] * len(through) + [VMEM] * len(outs),
        input_output_aliases={first + i: i for i in range(len(through))},
        scratch_shapes=scratch,
        compiler_params=pltpu.CompilerParams(vmem_limit_bytes=limit * MIB),
        cost_estimate=pl.CostEstimate(flops=flops, bytes_accessed=1000, transcendentals=0),
        name=name,
    )(*args, *after)


def per_device(slices, parts, enthalpy, solute, material, phase_flag, *params):
    rows, ny, nz = material.shape
    mid = rows - 4
    h0 = enthalpy.reshape(rows, ny, nz)
    c0 = solute.reshape(rows, ny, nz)
    prm = jnp.concatenate(params)
    slot = lax.axis_index("tm")
    pair, tall = f32(2, 2, ny, nz), f32(2, mid, ny, nz)
    halo = f32(2, ny, nz)
    pad = [pltpu.VMEM((2, rows + 2, ny + 16, nz), jnp.float32)]

    def move(x, tms, up, by):
        pairs = [
            (t * parts + s, (t + up) * parts + s + by)
            for t in tms
            for s in range(parts)
            if 0 <= s + by < parts
        ]
        return lax.ppermute(x, ("tm", "space"), pairs)

    def halos(tl0, tl7, tms, up):
        return move(tl7, tms, up, 1), move(tl0, tms, up, -1)

    def hbm(x):
        return pltpu.with_memory_space_constraint(x, pltpu.HBM)

    def send(x, n):
        return move(x, (n - 1,), 1, 0)

    def own(n):
        return (slot == n).astype(jnp.int32).reshape(1)

    def gridded(kernel, steps, outs, out_specs, in_specs, args, name, aliases={}):
        return pl.pallas_call(
            kernel,
            grid=(steps,),
            out_shape=outs,
            in_specs=in_specs,
            out_specs=out_specs,
            input_output_aliases=aliases,
            compiler_params=pltpu.CompilerParams(vmem_limit_bytes=8 * MIB),
            cost_estimate=TINY,
            name=name,
        )(*args)

    edge_row = pl.BlockSpec((1, ny, nz), lambda i: ((rows - 1) * i, 0, 0))
    whole = pl.BlockSpec((2, ny, nz), lambda i: (0, 0, 0))
    far = [pltpu.with_memory_space_constraint(x, pltpu.HBM) for x in (h0, c0, material)]
    tl0, tl7, later0, later7 = gridded(
        first_edges_kernel,
        2,
        [halo] * 4,
        [whole] * 4,
        [SMEM] * 7 + [edge_row] * 3,
        (*params, *far),
        "first_edges",
    )
    every = range(slices)
    even = halos(tl0, tl7, every[::2], 0)
    later0, later7, sm, sn, part, ids, ide = call(
        first_step_kernel,
        [tall, pair, pair, i32(rows, ny, nz), i32(2, ny, nz)],
        (prm, h0, c0, material, phase_flag),
        1,
        "first_step",
        pad,
        26,
        tile=128,
        through=(later0, later7),
    )
    odd = halos(later0, later7, every[1::2], 0)
    even = call(nothing_kernel, [], (), 0, "even_arrived", through=even, flops=10**11)

    def fine_edges(part, sides, after=()):
        return call(
            edges_kernel if len(sides) == 2 else edges_kernel_of_two,
            [pair, halo, halo],
            (prm, part, *sides, ide),
            1,
            "edges",
            after=after,
            tile=512,
        )

    base = ()
    sides = (*even, *odd)
    for k in range(STEPS - 1):
        sx, tl0, tl7 = fine_edges(part, sides, base)
        sides = halos(tl0, tl7, every, 0)
        if k == 0:
            base = call(
                base_kernel,
                [tall, pair, pair],
                (prm, h0, c0, sm, sn, sx, ids),
                1,
                "base",
                limit=16,
                tile=128,
            )
        if k == STEPS - 3:
            *sm, sn, part = call(
                step_apart_kernel,
                [pltpu.HBM((mid, ny, nz), jnp.float32)] * 2 + [pair, pair],
                (prm, sm, sn, sx, ids),
                1,
                "step_apart",
                pad,
                18,
                tile=128,
            )
        elif k == STEPS - 2:
            sm = [hbm(x) for x in sm]
            last = (*sm, sn, sx)
            sm, sn, part = call(
                step_joined_kernel,
                [tall, pair, pair],
                (prm, *sm, sn, sx, ids),
                1,
                "step_joined",
                pad,
                18,
                tile=512,
            )
        else:
            sm, sn, part = call(
                step_kernel, [tall, pair, pair], (prm, sm, sn, sx, ids), 1, "step", pad, 18, tile=128
            )
    km, kn, kx = base

    am, an, vm = call(
        replay_kernel,
        [tall, pair, tall],
        (own(1), prm, *(hbm(send(x, 1)) for x in last), ids, hbm(km), sm),
        2,
        "replay",
        pad,
        24,
        tile=512,
    )
    vn = sn
    vx, tl0, tl7, *apart = call(
        edges_apart_kernel,
        [pair, halo, halo, halo, halo],
        (prm, part, *sides, ide),
        1,
        "edges_apart",
        tile=512,
        after=(vm,),
    )
    low, high = halos(tl0, tl7, (0,), 1)
    ax = [send(x, 1) for x in apart]
    vn, part = call(
        coarse_rim_kernel,
        [pair, pair],
        (own(1), prm, am, an, *ax, kn, kx, ids, vn, vx),
        2,
        "coarse_rim",
        pad,
        20,
        tile=512,
    )
    vx, tl0, tl7 = call(
        coarse_edges_kernel,
        [pltpu.HBM(pair.shape, pair.dtype), halo, halo],
        (own(1), prm, part, low, high, ide, vx),
        2,
        "coarse_edges",
        tile=512,
    )
    side = pl.BlockSpec((2, 1, ny, nz), lambda i: (0, i, 0, 0))
    two = pl.BlockSpec((2, 2, ny, nz), lambda i: (0, i, 0, 0))
    inside = pl.BlockSpec((2, 1, ny, nz), lambda i: (0, (mid - 1) * i, 0, 0))

    def id_row(k):
        return pl.BlockSpec((1, ny, nz), lambda i: (k + (rows - 1 - 2 * k) * i, 0, 0))

    rim = None
    for n in range(2, slices):
        low, high = halos(tl0, tl7, (n - 1,), 1)
        if n == 2:
            am, an, ax = send(vm, n), send(vn, n), send(vx, n)
        else:
            am, ar = am3, send(rim, n)
        if n == slices - 1:
            break
        vm = call(
            coarse_mid_kernel,
            [pltpu.HBM(tall.shape, tall.dtype)],
            (own(n), prm, am, an, km, ids, vm),
            2,
            "coarse_mid",
            pad,
            18,
            tile=128,
        )[0]
        vm = hbm(vm)
        am3 = hbm(send(vm, n + 1))
        low, high = call(
            nothing_kernel, [], (), 0, "arrived", through=(low, high), flops=10**11
        )
        rim, tl0, tl7 = pl.pallas_call(
            tiled(coarse_outer_kernel, 512),
            grid=(2,),
            out_shape=[f32(2, 4, ny, nz), halo, halo],
            in_specs=[SMEM, SMEM, inside, side, side, whole, whole]
            + [side] * 4
            + [id_row(2), id_row(1), id_row(0), ANY],
            out_specs=[two, whole, whole],
            scratch_shapes=[pltpu.VMEM((2, 5, ny + 16, nz), jnp.float32)],
            compiler_params=pltpu.CompilerParams(vmem_limit_bytes=26 * MIB),
            cost_estimate=TINY,
            name="coarse_outer",
        )(own(n), prm, am, an, ax, low, high, hbm(kn), hbm(kx), hbm(vn), hbm(vx), ids, ids, ids, am3)

    out = f32(1, rows, ny, nz)
    last_own = own(slices - 1)
    half = pl.BlockSpec((2, mid // 2, ny, nz), lambda i: (0, i, 0, 0))
    beyond = pl.BlockSpec((2, 1, ny, nz), lambda i: (0, mid // 2 - i, 0, 0))
    id_half = pl.BlockSpec((rows // 2, ny, nz), lambda i: (i, 0, 0))
    id_beyond = pl.BlockSpec((1, ny, nz), lambda i: (rows // 2 - i, 0, 0))
    oh, oc = pl.pallas_call(
        tiled(last_rows_kernel, 512),
        grid=(2,),
        out_shape=[out, out],
        in_specs=[SMEM, SMEM, half, beyond, two, half, side, side, id_half, id_beyond, half, two],
        out_specs=[pl.BlockSpec((1, rows // 2, ny, nz), lambda i: (0, i, 0, 0))] * 2,
        scratch_shapes=[pltpu.VMEM((2, rows // 2 + 2, ny + 16, nz), jnp.float32)],
        compiler_params=pltpu.CompilerParams(vmem_limit_bytes=30 * MIB),
        cost_estimate=TINY,
        name="last_rows",
    )(last_own, prm, am, am, ar, hbm(km), hbm(kn), hbm(kx), ids, ids, hbm(vm), rim)
    out_row = pl.BlockSpec((1, 1, ny, nz), lambda i: (0, (rows - 1) * i, 0, 0))
    one = pl.BlockSpec((1, ny, nz), lambda i: (i, 0, 0))
    return tuple(
        gridded(
            last_edges_kernel,
            2,
            [out, out],
            [out_row] * 2,
            [SMEM, SMEM, whole, whole, one, out_row, out_row],
            (last_own, prm, low, high, ide, oh, oc),
            "last_edges",
            {5: 0, 6: 1},
        )
    )


def solution(mesh):
    body = functools.partial(per_device, mesh.shape["tm"], mesh.shape["space"])
    return jax.shard_map(
        body,
        mesh=mesh,
        in_specs=(
            P("tm", "space", None, None),
            P("tm", "space", None, None),
            P("space", None, None),
            P("space", None, None),
        )
        + (P(),) * 7,
        out_specs=(P("tm", "space", None, None), P("tm", "space", None, None)),
        check_vma=False,
    )
```

```python
import functools

import jax
import jax.numpy as jnp
from jax import lax
from jax.experimental import pallas as pl
from jax.experimental.pallas import tpu as pltpu
from jax.sharding import PartitionSpec as P

STEPS = 4
TILE = [256]
MIB = 1024 * 1024
SMEM = pl.BlockSpec(memory_space=pltpu.SMEM)
VMEM = pl.BlockSpec(memory_space=pltpu.VMEM)
ANY = pl.BlockSpec(memory_space=pl.ANY)


class Tables:
    def __init__(self, prm):
        def raw(first, count):
            return [jnp.full((8, 128), prm[first + m], jnp.float32) for m in range(count)]

        cap, self.lat, self.hs = raw(0, 4), raw(4, 4), raw(8, 4)
        kp, bd, xr = raw(12, 4), raw(16, 4), raw(20, 4)
        self.sg = raw(24, 3)
        q = [(1.0 - k) / (1.0 + b) for k, b in zip(kp, bd)]
        self.icap = [1.0 / c for c in cap]
        self.den0 = [1.0 - v for v in q]
        self.den1 = [v / t for v, t in zip(q, self.lat)]
        self.hg = [x * c for x, c in zip(xr, cap)]
        self.gh = [4.0 / (1.0 + 18.0 * x) for x in xr]
        self.crh = [h * g for h, g in zip(self.hg, self.gh)]
        self.kp18 = [18.0 / k for k in kp]


class Cells:
    def __init__(self, tab, ids):
        self.tab, self.shape = tab, ids.shape
        self.b0 = (ids & 1) != 0
        self.b1 = (ids & 2) != 0
        self.p1 = (ids & 4) != 0
        self.p2 = (ids & 8) != 0

    def wide(self, tile):
        reps = self.shape[0] // 8
        return jnp.broadcast_to(tile[None], (reps, 8, 128)).reshape(self.shape)

    def alloy(self, name):
        t = [self.wide(v) for v in getattr(self.tab, name)]
        return jnp.where(self.b1, jnp.where(self.b0, t[3], t[2]), jnp.where(self.b0, t[1], t[0]))

    def solute_gain(self):
        t = [self.wide(v) for v in self.tab.sg]
        return jnp.where(self.p2, t[2], jnp.where(self.p1, t[1], t[0]))

    def fine(self):
        return self.alloy("hg"), self.solute_gain()

    def ratio(self):
        sg = self.solute_gain()
        return self.alloy("gh"), 4.0 / (1.0 + sg * self.alloy("kp18"))

    def coarse(self):
        sg = self.solute_gain()
        return self.alloy("crh"), 4.0 * sg / (1.0 + sg * self.alloy("kp18"))

    def melt(self, h, c):
        sensible = h - self.alloy("hs")
        held = jnp.minimum(jnp.maximum(sensible, 0.0), self.alloy("lat"))
        t = (h - held) * self.alloy("icap")
        return t, c / (self.alloy("den0") + self.alloy("den1") * held)


F2 = range(2)


class Fields:
    def __init__(self, *refs):
        self.refs = refs
        self.shape = (2,) + tuple(refs[0].shape)

    def __getitem__(self, key):
        return self.refs[key[0]][key[1:]]

    def __setitem__(self, key, value):
        self.refs[key[0]][key[1:]] = value


class Rows:
    def __init__(self, ref, first, by=1):
        self.ref, self.first, self.by = ref, first, by

    def key(self, key):
        return (key[0], self.first + self.by * key[1], *key[2:])

    def __getitem__(self, key):
        return self.ref[self.key(key)]

    def __setitem__(self, key, value):
        self.ref[self.key(key)] = value


class Tile:
    def __init__(self, y, n):
        self.y, self.n = y, n
        self.at = pl.ds(y, n)

    def pad(self, by=0):
        return pl.ds(self.y + (8 + by), self.n)


def tiles(count, ny, body):
    n = TILE[-1] if ny % TILE[-1] == 0 else ny
    per = ny // n

    def run(k, carry):
        body(k // per, Tile(pl.multiple_of((k % per) * n, n), n))
        return carry

    lax.fori_loop(0, count * per, run, 0)


def clear_rims(pad):
    rows, long = pad.shape[1], pad.shape[2]
    for f in F2:
        for r in range(rows):
            pad[f, r, 0:8, :] = jnp.zeros((8, 128), jnp.float32)
            pad[f, r, long - 8 : long, :] = jnp.zeros((8, 128), jnp.float32)


def clear_ends(pad):
    def body(i, t):
        for f in F2:
            pad[f, i * (pad.shape[1] - 1), t.pad(), :] = jnp.zeros((t.n, 128), jnp.float32)

    tiles(2, pad.shape[2] - 16, body)


def put_melt(tab, pad, r, t, ids, h, c):
    values = Cells(tab, ids).melt(h, c)
    for f in F2:
        pad[f, r, t.pad(), :] = values[f]


def lap(pad, f, r, t):
    mid = pad[f, r, t.pad(), :]
    lane = lax.broadcasted_iota(jnp.int32, mid.shape, 1)
    total = pad[f, r, t.pad(-1), :] + pad[f, r, t.pad(1), :]
    total = total + jnp.where(lane == 0, 0.0, pltpu.roll(mid, 1, 1))
    total = total + jnp.where(lane == 127, 0.0, pltpu.roll(mid, 127, 1))
    return total - 6.0 * mid + pad[f, r - 1, t.pad(), :] + pad[f, r + 1, t.pad(), :]


def fine(tab, pad, r, t, ids, now):
    rate = Cells(tab, ids).fine()
    return [now[f] + rate[f] * lap(pad, f, r, t) for f in F2]


def coarse(tab, pad, r, t, ids, now):
    rate = Cells(tab, ids).coarse()
    return [now[f] + rate[f] * lap(pad, f, r, t) for f in F2]


class Parts:
    def __init__(self, mid):
        self.mid, self.rows = mid, mid + 4

    def each(self, ny, body, which="mnx"):
        if "x" in which:
            tiles(2, ny, lambda i, t: body("x", i, i * (self.rows - 1), t))
        if "n" in which:
            tiles(2, ny, lambda i, t: body("n", i, 1 + i * (self.rows - 3), t))
        if "m" in which:
            tiles(self.mid, ny, lambda i, t: body("m", i, i + 2, t))


def first_edges_kernel(prm, h, c, mat, tl0, tl7, later0, later7):
    tab = Tables(prm)
    side = pl.program_id(0)

    def body(i, t):
        values = Cells(tab, mat[0, t.at, :]).melt(h[0, t.at, :], c[0, t.at, :])

        @pl.when(side == 0)
        def _():
            for f in F2:
                tl0[f, t.at, :] = values[f]
                later0[f, t.at, :] = values[f]

        @pl.when(side == 1)
        def _():
            for f in F2:
                tl7[f, t.at, :] = values[f]
                later7[f, t.at, :] = values[f]

    tiles(1, h.shape[1], body)


def first_step_kernel(prm, h, c, mat, ph, sm, sn, part, ids, ide, pad):
    tab = Tables(prm)
    rows, ny = h.shape[0], h.shape[1]
    outs = {"m": sm, "n": sn, "x": part}
    clear_rims(pad)
    clear_ends(pad)

    def melt(r, t):
        cell = mat[r, t.at, :] + 4 * ph[r, t.at, :]
        ids[r, t.at, :] = cell
        put_melt(tab, pad, r + 1, t, cell, h[r, t.at, :], c[r, t.at, :])

    def update(part_name, i, r, t):
        new = fine(tab, pad, r + 1, t, ids[r, t.at, :], (h[r, t.at, :], c[r, t.at, :]))
        for f in F2:
            outs[part_name][f, i, t.at, :] = new[f]

    tiles(rows, ny, melt)
    ide[0] = ids[0]
    ide[1] = ids[rows - 1]
    Parts(rows - 4).each(ny, update)


def step_body(prm, sm, sn, sx, ids, outs, pad):
    tab = Tables(prm)
    ny = sm.shape[2]
    now = {"m": sm, "n": sn, "x": sx}
    block = Parts(sm.shape[1])
    clear_rims(pad)
    clear_ends(pad)

    def at(name, i, t):
        return [now[name][f, i, t.at, :] for f in F2]

    def melt(name, i, r, t):
        put_melt(tab, pad, r + 1, t, ids[r, t.at, :], *at(name, i, t))

    def update(name, i, r, t):
        new = fine(tab, pad, r + 1, t, ids[r, t.at, :], at(name, i, t))
        for f in F2:
            outs[name][f, i, t.at, :] = new[f]

    block.each(ny, melt)
    block.each(ny, update, outs)


def step_kernel(prm, sm, sn, sx, ids, nm, nn, part, pad):
    step_body(prm, sm, sn, sx, ids, {"x": part, "n": nn, "m": nm}, pad)


def step_apart_kernel(prm, sm, sn, sx, ids, mh, mc, nn, part, pad):
    step_body(prm, sm, sn, sx, ids, {"x": part, "n": nn, "m": Fields(mh, mc)}, pad)


def step_joined_kernel(prm, mh, mc, sn, sx, ids, nm, nn, part, pad):
    step_body(prm, Fields(mh, mc), sn, sx, ids, {"x": part, "n": nn, "m": nm}, pad)


def replay_kernel(own, prm, mh, mc, sn, sx, ids, km, om, am, an, nm, pad):
    @pl.when(own[0] != 0)
    def _():
        step_body(prm, Fields(mh, mc), sn, sx, ids, {"n": an, "m": am}, pad)
        coarse_body(
            prm, {"n": an, "m": am}, {"m": km}, {"m": om}, ids, into({"m": nm}), "m", pad, False
        )

    @pl.when(own[0] == 0)
    def _():
        nm[...] = om[...]


def edges_body(prm, gains, part, low, high, ide, edge, tl0, tl7):
    tab = Tables(prm)
    for e, (halo, tl) in enumerate(((low, tl0), (high, tl7))):

        def body(i, t, e=e, halo=halo, tl=tl):
            cells = Cells(tab, ide[e, t.at, :])
            rate = getattr(cells, gains)()
            new = [part[f, e, t.at, :] + rate[f] * halo[f, t.at, :] for f in F2]
            values = cells.melt(*new)
            for f in F2:
                edge[f, e, t.at, :] = new[f]
                tl[f, t.at, :] = values[f]

        tiles(1, part.shape[2], body)


class Sum:
    def __init__(self, one, other):
        self.one, self.other = one, other

    def __getitem__(self, key):
        return self.one[key] + self.other[key]


def nothing_kernel():
    pass


def edges_kernel(prm, part, low, high, ide, edge, tl0, tl7):
    edges_body(prm, "fine", part, low, high, ide, edge, tl0, tl7)


def edges_apart_kernel(prm, part, low, high, ide, edge, tl0, tl7, eh, ec):
    edges_body(prm, "fine", part, low, high, ide, edge, tl0, tl7)
    eh[...] = edge[0]
    ec[...] = edge[1]


def edges_kernel_of_two(prm, part, low, high, low2, high2, ide, edge, tl0, tl7):
    edges_body(prm, "fine", part, Sum(low, low2), Sum(high, high2), ide, edge, tl0, tl7)


def coarse_edges_kernel(own, prm, part, low, high, ide, old, *refs):
    edge, tl0, tl7 = refs

    @pl.when(own[0] != 0)
    def _():
        edges_body(prm, "coarse", part, low, high, ide, edge, tl0, tl7)

    @pl.when(own[0] == 0)
    def _():
        edge[...] = old[...]


def base_kernel(prm, h, c, sm, sn, sx, ids, km, kn, kx):
    tab = Tables(prm)
    first = {"m": sm, "n": sn, "x": sx}
    outs = {"m": km, "n": kn, "x": kx}

    def body(name, i, r, t):
        ratio = Cells(tab, ids[r, t.at, :]).ratio()
        for f, u in enumerate((h[r, t.at, :], c[r, t.at, :])):
            outs[name][f, i, t.at, :] = u + ratio[f] * (first[name][f, i, t.at, :] - u)

    Parts(sm.shape[1]).each(h.shape[1], body)


def coarse_body(prm, arrived, base, old, ids, put, which, pad, edge_less):
    tab = Tables(prm)
    mid, ny = arrived["m"].shape[1], arrived["m"].shape[2]
    block = Parts(mid)
    clear_rims(pad)
    if edge_less:
        clear_ends(pad)

    def at(ref, i, t):
        return [ref[f, i, t.at, :] for f in F2]

    def melt(name, i, r, t):
        put_melt(tab, pad, r + 1, t, ids[r, t.at, :], *at(arrived[name], i, t))

    def update(name, i, r, t):
        new = coarse(tab, pad, r + 1, t, ids[r, t.at, :], at(arrived[name], i, t))
        end, start = at(old[name], i, t), at(base[name], i, t)
        for f in F2:
            put(name, f, i, r, t, new[f] + (end[f] - start[f]))

    if "m" in which:
        block.each(ny, melt, arrived)
    else:
        block.each(ny, melt, "nx")
        tiles(2, ny, lambda i, t: melt("m", i * (mid - 1), 2 + i * (mid - 1), t))
    block.each(ny, update, which)


def into(outs):
    def put(name, f, i, r, t, value):
        outs[name][f, i, t.at, :] = value

    return put


def coarse_mid_kernel(own, prm, am, an, km, ids, om, nm, pad):
    @pl.when(own[0] != 0)
    def _():
        coarse_body(
            prm, {"n": an, "m": am}, {"m": km}, {"m": om}, ids, into({"m": nm}), "m", pad, False
        )

    @pl.when(own[0] == 0)
    def _():
        nm[...] = om[...]


def coarse_rim_kernel(own, prm, am, an, xh, xc, kn, kx, ids, on, ox, nn, part, pad):
    ax = Fields(xh, xc)

    @pl.when(own[0] != 0)
    def _():
        coarse_body(
            prm,
            {"x": ax, "n": an, "m": am},
            {"n": kn, "x": kx},
            {"n": on, "x": ox},
            ids,
            into({"n": nn, "x": part}),
            "xn",
            pad,
            True,
        )

    @pl.when(own[0] == 0)
    def _():
        nn[...] = on[...]


def coarse_outer_kernel(own, prm, am, an, ax, low, high, kn, kx, on, ox, idm, idn, idx, *refs):
    rim, tl0, tl7, pad = refs[-4:]
    e = pl.program_id(0)
    ny = ax.shape[2]

    @pl.when(own[0] != 0)
    def _():
        tab = Tables(prm)
        clear_rims(pad)

        def zero(i, t):
            for f in F2:
                pad[f, 0, t.pad(), :] = jnp.zeros((t.n, 128), jnp.float32)

        tiles(1, ny, zero)
        for k, (now, ids) in enumerate(((ax, idx), (an, idn), (am, idm))):

            def melt(i, t, k=k, now=now, ids=ids):
                values = [now[f, 0, t.at, :] for f in F2]
                put_melt(tab, pad, k + 1, t, ids[0, t.at, :], *values)

            tiles(1, ny, melt)
        for k, (now, ids, end, start) in enumerate(((ax, idx, ox, kx), (an, idn, on, kn))):

            def update(i, t, k=k, now=now, ids=ids, end=end, start=start):
                cells = Cells(tab, ids[0, t.at, :])
                rate = cells.coarse()
                new = []
                for f in F2:
                    total = lap(pad, f, k + 1, t)
                    if k == 0:
                        total = total + jnp.where(e == 0, low[f, t.at, :], high[f, t.at, :])
                    value = now[f, 0, t.at, :] + rate[f] * total
                    new.append(value + (end[f, 0, t.at, :] - start[f, 0, t.at, :]))
                    rim[f, k, t.at, :] = new[f]
                if k == 0:
                    values = cells.melt(*new)

                    @pl.when(e == 0)
                    def _():
                        for f in F2:
                            tl0[f, t.at, :] = values[f]

                    @pl.when(e == 1)
                    def _():
                        for f in F2:
                            tl7[f, t.at, :] = values[f]

            tiles(1, ny, update)

    @pl.when(own[0] == 0)
    def _():
        for f in F2:
            rim[f, 0] = ox[f, 0]
            rim[f, 1] = on[f, 0]


def last_rows_kernel(own, prm, am, aq, ar, km, kn, kx, ids, idq, om, rim, oh, oc, pad):
    out = (oh, oc)
    e = pl.program_id(0)
    half, ny = am.shape[1], am.shape[2]
    count = half + 2

    def place(k):
        return jnp.where(e == 0, k, count - 1 - k)

    def inner(j):
        return jnp.where(e == 0, j, half - 1 - j)

    def each(body):
        tiles(1, ny, lambda i, t: body(0, t, 0, "x"))
        tiles(1, ny, lambda i, t: body(1, t, 0, "n"))
        tiles(half, ny, lambda j, t: body(j + 2, t, inner(j), "m"))

    def at(ref, i, t):
        return [ref[f, i, t.at, :] for f in F2]

    arrived = {"x": Rows(ar, 0), "n": Rows(ar, 1), "m": am}
    old = {"x": Rows(rim, 0), "n": Rows(rim, 1), "m": om}
    base = {"x": kx, "n": kn, "m": km}

    @pl.when(own[0] != 0)
    def _():
        tab = Tables(prm)
        clear_rims(pad)

        def zero(i, t):
            for f in F2:
                pad[f, 0, t.pad(), :] = jnp.zeros((t.n, 128), jnp.float32)

        def melt(k, t, i, name):
            put_melt(tab, pad, k + 1, t, ids[place(k), t.at, :], *at(arrived[name], i, t))

        def beyond(i, t):
            put_melt(tab, pad, count + 1, t, idq[0, t.at, :], *at(aq, 0, t))

        def update(k, t, i, name):
            new = coarse(tab, pad, k + 1, t, ids[place(k), t.at, :], at(arrived[name], i, t))
            end, start = at(old[name], i, t), at(base[name], i, t)
            for f in F2:
                out[f][0, place(k), t.at, :] = new[f] + (end[f] - start[f])

        tiles(1, ny, zero)
        each(melt)
        tiles(1, ny, beyond)
        each(update)

    @pl.when(own[0] == 0)
    def _():
        def keep(k, t, i, name):
            for f in F2:
                out[f][0, place(k), t.at, :] = old[name][f, i, t.at, :]

        each(keep)


def last_edges_kernel(own, prm, low, high, ide, oh, oc, nh, nc):
    first = pl.program_id(0) == 0

    @pl.when(own[0] != 0)
    def _():
        tab = Tables(prm)

        def body(i, t):
            rate = Cells(tab, ide[0, t.at, :]).coarse()
            for f, (old, new) in enumerate(((oh, nh), (oc, nc))):
                halo = jnp.where(first, low[f, t.at, :], high[f, t.at, :])
                new[0, 0, t.at, :] = old[0, 0, t.at, :] + rate[f] * halo

        tiles(1, ide.shape[1], body)

    @pl.when(own[0] == 0)
    def _():
        nh[...] = oh[...]
        nc[...] = oc[...]


def f32(*shape):
    return jax.ShapeDtypeStruct(shape, jnp.float32)


def i32(*shape):
    return jax.ShapeDtypeStruct(shape, jnp.int32)


TINY = pl.CostEstimate(flops=1000, bytes_accessed=1000, transcendentals=0)


def tiled(kernel, tile):
    def run(*refs):
        TILE.append(tile)
        kernel(*refs)
        TILE.pop()

    return run


def call(kernel, outs, args, smem, name, scratch=(), limit=8, after=(), through=(), flops=1000, tile=256):
    after = (*after, *through)
    first = len(args) + len(after) - len(through)
    count = len(args)

    def run(*refs):
        TILE.append(tile)
        kernel(*refs[:count], *refs[count + len(after) + len(through) :])
        TILE.pop()

    return pl.pallas_call(
        run,
        out_shape=[f32(*x.shape) for x in through] + list(outs),
        in_specs=[SMEM] * smem + [VMEM] * (len(args) - smem) + [ANY] * len(after),
        out_specs=[ANY] * len(through) + [VMEM] * len(outs),
        input_output_aliases={first + i: i for i in range(len(through))},
        scratch_shapes=scratch,
        compiler_params=pltpu.CompilerParams(vmem_limit_bytes=limit * MIB),
        cost_estimate=pl.CostEstimate(flops=flops, bytes_accessed=1000, transcendentals=0),
        name=name,
    )(*args, *after)


def per_device(slices, parts, enthalpy, solute, material, phase_flag, *params):
    rows, ny, nz = material.shape
    mid = rows - 4
    h0 = enthalpy.reshape(rows, ny, nz)
    c0 = solute.reshape(rows, ny, nz)
    prm = jnp.concatenate(params)
    slot = lax.axis_index("tm")
    pair, tall = f32(2, 2, ny, nz), f32(2, mid, ny, nz)
    halo = f32(2, ny, nz)
    pad = [pltpu.VMEM((2, rows + 2, ny + 16, nz), jnp.float32)]

    def move(x, tms, up, by):
        pairs = [
            (t * parts + s, (t + up) * parts + s + by)
            for t in tms
            for s in range(parts)
            if 0 <= s + by < parts
        ]
        return lax.ppermute(x, ("tm", "space"), pairs)

    def halos(tl0, tl7, tms, up):
        return move(tl7, tms, up, 1), move(tl0, tms, up, -1)

    def hbm(x):
        return pltpu.with_memory_space_constraint(x, pltpu.HBM)

    def send(x, n):
        return move(x, (n - 1,), 1, 0)

    def own(n):
        return (slot == n).astype(jnp.int32).reshape(1)

    def gridded(kernel, steps, outs, out_specs, in_specs, args, name, aliases={}):
        return pl.pallas_call(
            kernel,
            grid=(steps,),
            out_shape=outs,
            in_specs=in_specs,
            out_specs=out_specs,
            input_output_aliases=aliases,
            compiler_params=pltpu.CompilerParams(vmem_limit_bytes=8 * MIB),
            cost_estimate=TINY,
            name=name,
        )(*args)

    edge_row = pl.BlockSpec((1, ny, nz), lambda i: ((rows - 1) * i, 0, 0))
    whole = pl.BlockSpec((2, ny, nz), lambda i: (0, 0, 0))
    far = [pltpu.with_memory_space_constraint(x, pltpu.HBM) for x in (h0, c0, material)]
    tl0, tl7, later0, later7 = gridded(
        first_edges_kernel,
        2,
        [halo] * 4,
        [whole] * 4,
        [SMEM] + [edge_row] * 3,
        (prm, *far),
        "first_edges",
    )
    every = range(slices)
    even = halos(tl0, tl7, every[::2], 0)
    later0, later7, sm, sn, part, ids, ide = call(
        first_step_kernel,
        [tall, pair, pair, i32(rows, ny, nz), i32(2, ny, nz)],
        (prm, h0, c0, material, phase_flag),
        1,
        "first_step",
        pad,
        26,
        tile=128,
        through=(later0, later7),
    )
    odd = halos(later0, later7, every[1::2], 0)
    even = call(nothing_kernel, [], (), 0, "even_arrived", through=even, flops=10**11)

    def fine_edges(part, sides, after=()):
        return call(
            edges_kernel if len(sides) == 2 else edges_kernel_of_two,
            [pair, halo, halo],
            (prm, part, *sides, ide),
            1,
            "edges",
            after=after,
            tile=512,
        )

    base = ()
    sides = (*even, *odd)
    for k in range(STEPS - 1):
        sx, tl0, tl7 = fine_edges(part, sides, base)
        sides = halos(tl0, tl7, every, 0)
        if k == 0:
            base = call(
                base_kernel,
                [tall, pair, pair],
                (prm, h0, c0, sm, sn, sx, ids),
                1,
                "base",
                limit=16,
                tile=128,
            )
        if k == STEPS - 3:
            *sm, sn, part = call(
                step_apart_kernel,
                [pltpu.HBM((mid, ny, nz), jnp.float32)] * 2 + [pair, pair],
                (prm, sm, sn, sx, ids),
                1,
                "step_apart",
                pad,
                18,
                tile=128,
            )
        elif k == STEPS - 2:
            sm = [hbm(x) for x in sm]
            last = (*sm, sn, sx)
            sm, sn, part = call(
                step_joined_kernel,
                [tall, pair, pair],
                (prm, *sm, sn, sx, ids),
                1,
                "step_joined",
                pad,
                18,
                tile=512,
            )
        else:
            sm, sn, part = call(
                step_kernel, [tall, pair, pair], (prm, sm, sn, sx, ids), 1, "step", pad, 18, tile=128
            )
    km, kn, kx = base

    am, an, vm = call(
        replay_kernel,
        [tall, pair, tall],
        (own(1), prm, *(hbm(send(x, 1)) for x in last), ids, hbm(km), sm),
        2,
        "replay",
        pad,
        24,
        tile=512,
    )
    vn = sn
    vx, tl0, tl7, *apart = call(
        edges_apart_kernel,
        [pair, halo, halo, halo, halo],
        (prm, part, *sides, ide),
        1,
        "edges_apart",
        after=(vm,),
    )
    low, high = halos(tl0, tl7, (0,), 1)
    ax = [send(x, 1) for x in apart]
    vn, part = call(
        coarse_rim_kernel,
        [pair, pair],
        (own(1), prm, am, an, *ax, kn, kx, ids, vn, vx),
        2,
        "coarse_rim",
        pad,
        20,
        tile=512,
    )
    vx, tl0, tl7 = call(
        coarse_edges_kernel,
        [pltpu.HBM(pair.shape, pair.dtype), halo, halo],
        (own(1), prm, part, low, high, ide, vx),
        2,
        "coarse_edges",
    )
    side = pl.BlockSpec((2, 1, ny, nz), lambda i: (0, i, 0, 0))
    two = pl.BlockSpec((2, 2, ny, nz), lambda i: (0, i, 0, 0))
    inside = pl.BlockSpec((2, 1, ny, nz), lambda i: (0, (mid - 1) * i, 0, 0))

    def id_row(k):
        return pl.BlockSpec((1, ny, nz), lambda i: (k + (rows - 1 - 2 * k) * i, 0, 0))

    rim = None
    for n in range(2, slices):
        low, high = halos(tl0, tl7, (n - 1,), 1)
        if n == 2:
            am, an, ax = send(vm, n), send(vn, n), send(vx, n)
        else:
            am, ar = am3, send(rim, n)
        if n == slices - 1:
            break
        vm = call(
            coarse_mid_kernel,
            [pltpu.HBM(tall.shape, tall.dtype)],
            (own(n), prm, am, an, km, ids, vm),
            2,
            "coarse_mid",
            pad,
            18,
            tile=128,
        )[0]
        vm = hbm(vm)
        am3 = hbm(send(vm, n + 1))
        low, high = call(
            nothing_kernel, [], (), 0, "arrived", through=(low, high), flops=10**11
        )
        rim, tl0, tl7 = pl.pallas_call(
            tiled(coarse_outer_kernel, 512),
            grid=(2,),
            out_shape=[f32(2, 4, ny, nz), halo, halo],
            in_specs=[SMEM, SMEM, inside, side, side, whole, whole]
            + [side] * 4
            + [id_row(2), id_row(1), id_row(0), ANY],
            out_specs=[two, whole, whole],
            scratch_shapes=[pltpu.VMEM((2, 5, ny + 16, nz), jnp.float32)],
            compiler_params=pltpu.CompilerParams(vmem_limit_bytes=26 * MIB),
            cost_estimate=TINY,
            name="coarse_outer",
        )(own(n), prm, am, an, ax, low, high, hbm(kn), hbm(kx), hbm(vn), hbm(vx), ids, ids, ids, am3)

    out = f32(1, rows, ny, nz)
    last_own = own(slices - 1)
    half = pl.BlockSpec((2, mid // 2, ny, nz), lambda i: (0, i, 0, 0))
    beyond = pl.BlockSpec((2, 1, ny, nz), lambda i: (0, mid // 2 - i, 0, 0))
    id_half = pl.BlockSpec((rows // 2, ny, nz), lambda i: (i, 0, 0))
    id_beyond = pl.BlockSpec((1, ny, nz), lambda i: (rows // 2 - i, 0, 0))
    oh, oc = pl.pallas_call(
        tiled(last_rows_kernel, 512),
        grid=(2,),
        out_shape=[out, out],
        in_specs=[SMEM, SMEM, half, beyond, two, half, side, side, id_half, id_beyond, half, two],
        out_specs=[pl.BlockSpec((1, rows // 2, ny, nz), lambda i: (0, i, 0, 0))] * 2,
        scratch_shapes=[pltpu.VMEM((2, rows // 2 + 2, ny + 16, nz), jnp.float32)],
        compiler_params=pltpu.CompilerParams(vmem_limit_bytes=30 * MIB),
        cost_estimate=TINY,
        name="last_rows",
    )(last_own, prm, am, am, ar, hbm(km), hbm(kn), hbm(kx), ids, ids, hbm(vm), rim)
    out_row = pl.BlockSpec((1, 1, ny, nz), lambda i: (0, (rows - 1) * i, 0, 0))
    one = pl.BlockSpec((1, ny, nz), lambda i: (i, 0, 0))
    return tuple(
        gridded(
            last_edges_kernel,
            2,
            [out, out],
            [out_row] * 2,
            [SMEM, SMEM, whole, whole, one, out_row, out_row],
            (last_own, prm, low, high, ide, oh, oc),
            "last_edges",
            {5: 0, 6: 1},
        )
    )


def solution(mesh):
    body = functools.partial(per_device, mesh.shape["tm"], mesh.shape["space"])
    return jax.shard_map(
        body,
        mesh=mesh,
        in_specs=(
            P("tm", "space", None, None),
            P("tm", "space", None, None),
            P("space", None, None),
            P("space", None, None),
        )
        + (P(),) * 7,
        out_specs=(P("tm", "space", None, None), P("tm", "space", None, None)),
        check_vma=False,
    )
```
